32 devices in a mesh: dp: 8 (over z, x), tensor: 4 (over y, core).
Axes of the slice: x: 2, y: 2, z: 4, core: 2. Of those that a mesh axis runs over, the one named last changes fastest.
Arguments:
- latents: bfloat16 [8, 128, 768], P('dp'), may hold values from -6 to 6
- byte_array: bfloat16 [8, 3196, 768], P('dp'), may hold values from -6 to 6
- caption_lengths: int32 [8], P('dp'), may hold values from 5 to 60
- patch_mask: int32 [8, 3136], P('dp'), may hold values 0 or 1
- cross_keep: int32 [8], P('dp'), may hold values 0 or 1
- cross_norm: float32 [768], replicated, may hold values from 0.5 to 1.5
- byte_norm: float32 [768], replicated, may hold values from 0.5 to 1.5
- cross_query: bfloat16 [768, 768], P(None, 'tensor'), may hold values from -0.21875 to 0.21875
- cross_key: bfloat16 [768, 768], P(None, 'tensor'), may hold values from -0.21875 to 0.21875
- cross_value: bfloat16 [768, 768], P(None, 'tensor'), may hold values from -0.21875 to 0.21875
- cross_output: bfloat16 [768, 768], P('tensor'), may hold values from -6 to 6
- ffn_norm1: float32 [768], replicated, may hold values from 0.5 to 1.5
- ffn_in1: bfloat16 [768, 3072], P(None, 'tensor'), may hold values from -0.21875 to 0.21875
- ffn_out1: bfloat16 [3072, 768], P('tensor'), may hold values from -0.109375 to 0.109375
- self_norm: float32 [768], replicated, may hold values from 0.5 to 1.5
- self_query: bfloat16 [768, 768], P(None, 'tensor'), may hold values from -0.21875 to 0.21875
- self_key: bfloat16 [768, 768], P(None, 'tensor'), may hold values from -0.21875 to 0.21875
- self_value: bfloat16 [768, 768], P(None, 'tensor'), may hold values from -0.21875 to 0.21875
- self_output: bfloat16 [768, 768], P('tensor'), may hold values from -1.25 to 1.25
- ffn_norm2: float32 [768], replicated, may hold values from 0.5 to 1.5
- ffn_in2: bfloat16 [768, 3072], P(None, 'tensor'), may hold values from -0.21875 to 0.21875
- ffn_out2: bfloat16 [3072, 768], P('tensor'), may hold values from -0.109375 to 0.109375
- cotangent: bfloat16 [8, 128, 768], P('dp'), may hold values from -6 to 6
Outputs:
- new_latents: bfloat16 [8, 128, 768], P('dp')
- latent_grads: bfloat16 [8, 128, 768], P('dp')
- byte_grads: bfloat16 [8, 3196, 768], P('dp', 'tensor')
- grad_cross_norm: float32 [768], P('dp')
- grad_byte_norm: float32 [768], replicated
- grad_cross_query: float32 [768, 768], P('dp', 'tensor')
- grad_cross_key: float32 [768, 768], P('dp', 'tensor')
- grad_cross_value: float32 [768, 768], P('dp', 'tensor')
- grad_cross_output: float32 [768, 768], P('tensor', 'dp')
- grad_ffn_norm1: float32 [768], P('dp')
- grad_ffn_in1: float32 [768, 3072], P('dp', 'tensor')
- grad_ffn_out1: float32 [3072, 768], P('tensor', 'dp')
- grad_self_norm: float32 [768], P('dp')
- grad_self_query: float32 [768, 768], P('dp', 'tensor')
- grad_self_key: float32 [768, 768], P('dp', 'tensor')
- grad_self_value: float32 [768, 768], P('dp', 'tensor')
- grad_self_output: float32 [768, 768], P('tensor', 'dp')
- grad_ffn_norm2: float32 [768], P('dp')
- grad_ffn_in2: float32 [768, 3072], P('dp', 'tensor')
- grad_ffn_out2: float32 [3072, 768], P('tensor', 'dp')
- key_counts: float32 [2], replicated
The draws below stay inside these ranges and needn't reach their ends.
Inputs may be any that keep to these rules, and one draw needn't show every extreme that they name: `caption_lengths`: caption tokens of an item; its caption key slots past this number are padding. `patch_mask`: a nonzero entry marks a patch key that takes part. `cross_keep`: 1 where an item's cross-attention runs, 0 where it is skipped.
All inputs are finite; a program needn't handle non-finite values. No bound on the sum of `patch_mask` or of `cross_keep` on one device may be relied on, other than what follows from the above.
Results may differ from the reference program's by a relative error of at most 0.03.
Values may be sent and summed in bfloat16 or wider, within the bound.
A program may use at most 128 MiB of HBM per device.

```python
import jax
import jax.numpy as jnp
from jax import lax

D = 768
HEADS = 12
HEAD_DIM = 64
FF = 3072
LATENTS = 128
PATCHES = 3136
CAPTION = 60
KEYS = 3196
ITEMS = 8


def set_ends(values, stream_key, least, top_value):
    spot = [jax.random.randint(jax.random.fold_in(stream_key, axis), (), 0, length) for axis, length in enumerate(values.shape)]
    widest = values.shape.index(max(values.shape))
    next_to = spot[:widest] + [(spot[widest] + 1) % values.shape[widest]] + spot[widest + 1:]
    return values.at[tuple(spot)].set(least).at[tuple(next_to)].set(top_value)


def block_levels(stream_key, dims, split, least, largest):
    level, own = 1.0, jax.random.fold_in(stream_key, 6)
    for position, parts in split:
        draws = jnp.exp(jax.random.uniform(jax.random.fold_in(own, position), (parts,), jnp.float32, least / len(split), largest / len(split)))
        level = level * jnp.repeat(draws, dims[position] // parts).reshape([-1 if axis == position else 1 for axis in range(len(dims))])
    return level


def scatter_about(rng, shape, scale, bound, pieces=(), held_as=jnp.bfloat16):
    values = jax.random.normal(rng, shape, jnp.float32) * scale
    if len(pieces) > 0:
        values = block_levels(rng, shape, pieces, -0.22, 0.18) * values
    return jnp.clip(values, min=-bound, max=bound).astype(held_as)


def setup_inputs(seed: int = 0) -> dict:
    arg_keys = jax.random.split(jax.random.key(seed), 24)
    return {
        "latents": scatter_about(arg_keys[0], (ITEMS, LATENTS, D), 1.0, 6.0, ((0, 8),)),
        "byte_array": scatter_about(arg_keys[1], (ITEMS, KEYS, D), 1.0, 6.0, ((0, 8),)),
        "caption_lengths": set_ends(jax.random.randint(arg_keys[2], (ITEMS,), max(1, CAPTION // 12), CAPTION + 1), jax.random.fold_in(arg_keys[2], 1), max(1, CAPTION // 12), CAPTION).astype(jnp.int32),
        "patch_mask": set_ends((jax.random.randint(arg_keys[3], (ITEMS, PATCHES), 0, 8) < 7).astype(jnp.int32), jax.random.fold_in(arg_keys[3], 1), 0, 1),
        "cross_keep": set_ends((jax.random.randint(arg_keys[4], (ITEMS,), 0, 4) < 3).astype(jnp.int32), jax.random.fold_in(arg_keys[4], 1), 0, 1),
        "cross_norm": jnp.clip(1.0 + 0.1 * jax.random.normal(arg_keys[5], (D,), jnp.float32), 0.5, 1.5),
        "byte_norm": jnp.clip(1.0 + 0.1 * jax.random.normal(arg_keys[6], (D,), jnp.float32), 0.5, 1.5),
        "cross_query": scatter_about(arg_keys[7], (D, D), D ** -0.5, 0.21875, ((1, 4),)),
        "cross_key": scatter_about(arg_keys[8], (D, D), D ** -0.5, 0.21875, ((1, 4),)),
        "cross_value": scatter_about(arg_keys[9], (D, D), D ** -0.5, 0.21875, ((1, 4),)),
        "cross_output": scatter_about(arg_keys[10], (D, D), (max(1, 4 * D // KEYS)) ** -0.5, 6.0, ((0, 4),)),
        "ffn_norm1": jnp.clip(1.0 + 0.1 * jax.random.normal(arg_keys[11], (D,), jnp.float32), 0.5, 1.5),
        "ffn_in1": scatter_about(arg_keys[12], (D, FF), D ** -0.5, 0.21875, ((1, 4),)),
        "ffn_out1": scatter_about(arg_keys[13], (FF, D), FF ** -0.5, 0.109375, ((0, 4),)),
        "self_norm": jnp.clip(1.0 + 0.1 * jax.random.normal(arg_keys[14], (D,), jnp.float32), 0.5, 1.5),
        "self_query": scatter_about(arg_keys[15], (D, D), D ** -0.5, 0.21875, ((1, 4),)),
        "self_key": scatter_about(arg_keys[16], (D, D), D ** -0.5, 0.21875, ((1, 4),)),
        "self_value": scatter_about(arg_keys[17], (D, D), D ** -0.5, 0.21875, ((1, 4),)),
        "self_output": scatter_about(arg_keys[18], (D, D), (max(1, 4 * D // LATENTS)) ** -0.5, 1.25, ((0, 4),)),
        "ffn_norm2": jnp.clip(1.0 + 0.1 * jax.random.normal(arg_keys[19], (D,), jnp.float32), 0.5, 1.5),
        "ffn_in2": scatter_about(arg_keys[20], (D, FF), D ** -0.5, 0.21875, ((1, 4),)),
        "ffn_out2": scatter_about(arg_keys[21], (FF, D), FF ** -0.5, 0.109375, ((0, 4),)),
        "cotangent": scatter_about(arg_keys[22], (ITEMS, LATENTS, D), 1.0, 6.0, ((0, 8),)),
    }


epsilon = 1e-05
highest = lax.Precision.HIGHEST

@jax.custom_vjp
def low(v):
    return lax.optimization_barrier(v.astype(jnp.bfloat16)).astype(jnp.float32)

@jax.custom_vjp
def low_back(v):
    return v

def low_keep(v):
    return (low(v), None)

def low_pass(kept, grad):
    return (grad,)

def back_keep(v):
    return (v, None)

def back_low(kept, grad):
    return (low(grad),)
low.defvjp(low_keep, low_pass)
low_back.defvjp(back_keep, back_low)

def normalize(values_in, gain_vec):
    centered = values_in - lax.optimization_barrier(jnp.mean(values_in, axis=-1, keepdims=True))
    spread = lax.optimization_barrier(jnp.mean(centered * centered, axis=-1, keepdims=True))
    return centered * lax.rsqrt(spread + epsilon) * gain_vec

def project(left_side, right_side):
    return jnp.dot(left_side, right_side, precision=highest)

def attend(query_in, source, live_keys, weight_q, weight_k, weight_v, weight_o):
    query_vectors = low(low_back(project(query_in, weight_q)))
    key_vectors = low(low_back(project(source, weight_k)))
    value_vectors = low(low_back(project(source, weight_v)))
    factor = HEAD_DIM ** (-0.5)
    shaped_q = query_vectors.reshape(query_vectors.shape[0], HEADS, HEAD_DIM)
    shaped_k = key_vectors.reshape(key_vectors.shape[0], HEADS, HEAD_DIM)
    shaped_v = value_vectors.reshape(value_vectors.shape[0], HEADS, HEAD_DIM)
    scores = low_back(jnp.einsum('qhd,khd->hqk', shaped_q, shaped_k, precision=highest) * factor)
    scores = jnp.where(live_keys[None, None, :], scores, -1000000000.0)
    soft_weights = low(jax.nn.softmax(scores, axis=-1))
    blended = jnp.einsum('hqk,khd->qhd', soft_weights, shaped_v, precision=highest)
    blended = low(low_back(blended.reshape(blended.shape[0], HEADS * HEAD_DIM)))
    return low_back(project(blended, weight_o))

def feed(residual, gain_vec, weight_in, weight_out):
    normed = low(normalize(residual, gain_vec))
    hidden = low_back(project(normed, weight_in))
    active = low(jax.nn.gelu(hidden))
    return residual + low_back(project(active, weight_out))

def forward(params, latent, byte_rows, live_keys, kept_flag):
    query_in = low(normalize(latent, params[0]))
    source = low(normalize(byte_rows, params[1]))
    after_cross = latent + kept_flag * attend(query_in, source, live_keys, params[2], params[3], params[4], params[5])
    after_ffn1 = feed(after_cross, params[6], params[7], params[8])
    inner_in = low(normalize(after_ffn1, params[9]))
    everyone = jnp.ones((inner_in.shape[0],), dtype=bool)
    after_self = after_ffn1 + attend(inner_in, inner_in, everyone, params[10], params[11], params[12], params[13])
    return feed(after_self, params[14], params[15], params[16])

def reference(latents, byte_array, caption_lengths, patch_mask, cross_keep, cross_norm, byte_norm, cross_query, cross_key, cross_value, cross_output, ffn_norm1, ffn_in1, ffn_out1, self_norm, self_query, self_key, self_value, self_output, ffn_norm2, ffn_in2, ffn_out2, cotangent):
    params = tuple((weight.astype(jnp.float32) for weight in (cross_norm, byte_norm, cross_query, cross_key, cross_value, cross_output, ffn_norm1, ffn_in1, ffn_out1, self_norm, self_query, self_key, self_value, self_output, ffn_norm2, ffn_in2, ffn_out2)))
    positions = jnp.arange(CAPTION, dtype=jnp.int32)
    live_keys = jnp.concatenate([patch_mask != 0, positions[None, :] < caption_lengths[:, None]], axis=1)
    kept_flags = cross_keep.astype(jnp.float32)

    def one_item(totals, item_data):
        latent, byte_rows, live_row, kept_flag, grad_out = item_data

        def wrapped(weights, start_rows, source):
            return forward(weights, start_rows, source, live_row, kept_flag)
        result, pullback = jax.vjp(wrapped, params, latent, byte_rows)
        grad_params, grad_latent, grad_bytes = pullback(grad_out)
        totals = jax.tree.map(jnp.add, totals, grad_params)
        return (totals, (result, grad_latent, grad_bytes))
    zero_grads = jax.tree.map(jnp.zeros_like, params)
    totals, (results, grad_latents, grad_bytes) = lax.scan(one_item, zero_grads, (latents.astype(jnp.float32), byte_array.astype(jnp.float32), live_keys, kept_flags, cotangent.astype(jnp.float32)))
    live_counts = lax.optimization_barrier(jnp.sum(live_keys.astype(jnp.float32), axis=1))
    key_counts = jnp.stack([jnp.sum(kept_flags * live_counts), jnp.sum(kept_flags) * LATENTS])
    return (results.astype(jnp.bfloat16), grad_latents.astype(jnp.bfloat16), grad_bytes.astype(jnp.bfloat16), totals[0], totals[1], totals[2], totals[3], totals[4], totals[5], totals[6], totals[7], totals[8], totals[9], totals[10], totals[11], totals[12], totals[13], totals[14], totals[15], totals[16], key_counts)
```

```python
import functools
from types import SimpleNamespace

import jax
import jax.numpy as jnp
from jax import lax
from jax.experimental import pallas as pl
from jax.experimental.pallas import tpu as pltpu
from jax.sharding import PartitionSpec as P

HEAD_DIM = 64
EPSILON = 1e-05
GELU_A = 0.7978845608
GELU_B = 0.044715
KEY_BLOCK = 640
ROW_CHUNK = 64
OWN_CHUNK = 80
MESH = pl.DeviceIdType.MESH
BF = jnp.bfloat16
F32 = jnp.float32

FO2, FI2, SQKV, SO, FO1, FI1, CO, CQ, CKV = range(9)


def nn(left, right):
    return lax.dot_general(left, right, (((1,), (0,)), ((), ())), preferred_element_type=F32)


def nt(left, right):
    return lax.dot_general(left, right, (((1,), (1,)), ((), ())), preferred_element_type=F32)


def tn(left, right):
    return lax.dot_general(left, right, (((0,), (0,)), ((), ())), preferred_element_type=F32)


def mean_of(values):
    return jnp.mean(values, axis=-1, keepdims=True)


def norm_parts(values):
    centered = values - mean_of(values)
    scale = lax.rsqrt(mean_of(centered * centered) + EPSILON)
    return centered * scale, scale


def norm_back(unit, scale, gain, grad):
    inner = grad * gain
    return scale * (inner - mean_of(inner) - unit * mean_of(inner * unit))


def gelu_parts(hidden):
    squared = hidden * hidden
    bent = jnp.tanh(GELU_A * hidden * (1.0 + GELU_B * squared))
    half = 0.5 * (1.0 + bent)
    slope = half + 0.5 * hidden * (1.0 - bent * bent) * (GELU_A * (1.0 + 3.0 * GELU_B * squared))
    return hidden * half, slope


def kernel(cfg, *refs):
    r = SimpleNamespace()
    at = 0
    for tree, count in zip(cfg.trees, cfg.counts):
        vars(r).update(jax.tree.unflatten(tree, refs[at : at + count]))
        at += count
    lat, width, hw, heads = cfg.lat, cfg.width, cfg.hw, cfg.heads
    n_hi, pr, rpd, blocks = cfg.n_hi, cfg.pr, cfg.rpd, cfg.blocks
    half = lat // 2
    dp, t = lax.axis_index("dp"), lax.axis_index("tensor")
    parity, hi, core = lax.rem(dp, 2), lax.div(dp, 2), lax.rem(t, 2)
    sib_t, far_t, diag_t = t + 1 - 2 * core, lax.rem(t + 2, 4), 3 - t
    sibling, far, diagonal = (dp, sib_t), (dp, far_t), (dp, diag_t)
    near = (dp + 1 - 2 * parity, t)
    trio = (sibling, far, diagonal)

    def hi_peer(step):
        index = lax.rem(hi + step, n_hi)
        return index, (index * 2 + parity, t)

    def remote(src, dst, sends, receives, device):
        return pltpu.make_async_remote_copy(
            src_ref=src,
            dst_ref=dst,
            send_sem=sends,
            recv_sem=receives,
            device_id=device,
            device_id_type=MESH,
        )

    byte_copies = [
        pltpu.make_async_copy(
            r.bytes.at[pl.ds(start, size)], r.source.at[pl.ds(start, size)], r.byte_sem.at[i]
        )
        for i, (start, size) in enumerate(cfg.byte_parts)
    ]
    weight_copies = {
        name: pltpu.make_async_copy(ref, r.held[name], r.w_sem.at[i])
        for i, (name, ref) in enumerate(r.weights.items())
    }
    w = SimpleNamespace(**r.held)

    def arrive(*names):
        for name in names:
            weight_copies[name].wait()

    pair_copies = [
        pltpu.make_async_copy(ref, r.wkv.at[t, i], r.pair_sem.at[i])
        for i, ref in enumerate((r.cross_key, r.cross_value))
    ]
    first, *others = weight_copies.values()
    for copy in [first] + pair_copies + byte_copies + others:
        copy.start()

    barrier = pltpu.get_barrier_semaphore()
    for device in trio + (near,):
        pl.semaphore_signal(barrier, inc=1, device_id=device, device_id_type=MESH)

    def greet(step, carry):
        pl.semaphore_signal(barrier, inc=1, device_id=hi_peer(step)[1], device_id_type=MESH)
        return carry

    lax.fori_loop(1, n_hi, greet, 0)
    pl.semaphore_wait(barrier, 4 + n_hi - 1)

    columns = lax.broadcasted_iota(jnp.int32, (lat, hw), 1)
    head_mask = [
        (columns >= h * HEAD_DIM) & (columns < (h + 1) * HEAD_DIM) for h in range(heads)
    ]

    def spread(values):
        wide = values.astype(F32)
        return jnp.concatenate([jnp.where(m, wide, 0.0) for m in head_mask], axis=0)

    def gathered_heads(values):
        total = jnp.where(head_mask[0], values[:lat], 0.0)
        for h in range(1, heads):
            total = total + jnp.where(head_mask[h], values[h * lat : (h + 1) * lat], 0.0)
        return total

    def as_row(column):
        return jnp.broadcast_to(column, (column.shape[0], 128)).T[:8]

    def share(buffer, index):
        copies = [
            remote(
                buffer.at[t], buffer.at[t], r.share_ss.at[index, k], r.share_rs.at[index, k], peer
            )
            for k, peer in enumerate(trio)
        ]
        for copy in copies:
            copy.start()
        return copies

    def wait_all(copies):
        for copy in copies:
            copy.wait()

    hops = {}

    def sum_open(a, part):
        r.ar_s[a] = part.astype(BF).reshape(2, half, width)
        hops[a] = remote(
            r.ar_s.at[a, 1 - core], r.ar_r1.at[a], r.ar_ss.at[a, 0], r.ar_rs.at[a, 0], sibling
        )
        hops[a].start()

    def sum_cross(a):
        hops[a].wait()
        pair = r.ar_s[a, core].astype(F32) + r.ar_r1[a].astype(F32)
        r.ar_t[a, core] = pair.astype(BF)
        hops[a] = remote(
            r.ar_t.at[a, core], r.ar_r2.at[a], r.ar_ss.at[a, 1], r.ar_rs.at[a, 1], far
        )
        hops[a].start()

    def sum_back(a):
        hops[a].wait()
        total = r.ar_t[a, core].astype(F32) + r.ar_r2[a].astype(F32)
        r.ar_t[a, core] = total.astype(BF)
        hops[a] = remote(
            r.ar_t.at[a, core], r.ar_t.at[a, core], r.ar_ss.at[a, 2], r.ar_rs.at[a, 2], sibling
        )
        hops[a].start()

    def sum_close(a):
        hops[a].wait()
        return r.ar_t[a].reshape(lat, width).astype(F32)

    def selection(which):
        shape = (n_hi, pr, width)
        block = lax.broadcasted_iota(jnp.int32, shape, 0)
        row = lax.broadcasted_iota(jnp.int32, shape, 1)
        feature = lax.broadcasted_iota(jnp.int32, shape, 2)
        hit = (feature == (block * 2 + which) * rpd + row) & (row < rpd)
        return jnp.where(hit, 1.0, 0.0).astype(BF).reshape(n_hi * pr, width)

    near_copies = {}

    def near_send(g, left, right):
        own, sent, right_own = r.left_own[g], r.left_sent[g], r.right_own[g]
        sent[...] = nt(r.sel[1], left).astype(BF)
        right_own[...] = right
        copies = [
            remote(sent, r.left_near[g], r.x_ss.at[g, 0], r.x_rs.at[g, 0], near),
            remote(right_own, r.right_near[g], r.x_ss.at[g, 1], r.x_rs.at[g, 1], near),
        ]
        for copy in copies:
            copy.start()
        own[...] = nt(r.sel[0], left).astype(BF)
        near_copies[g] = copies

    def hi_send(g, product):
        sent, received = r.block_sent[g], r.block_got[g]
        sent[...] = product.astype(BF).reshape(n_hi, pr, product.shape[-1])

        def send(step, carry):
            index, device = hi_peer(step)
            remote(
                sent.at[index], received.at[hi], r.z_ss.at[g, index], r.z_rs.at[g, hi], device
            ).start()
            return carry

        lax.fori_loop(1, n_hi, send, 0)
        received[hi] = sent[hi]

    def far_send(g):
        wait_all(near_copies[g])
        hi_send(
            g,
            nn(r.left_own[g][...], r.right_own[g][...])
            + nn(r.left_near[g][...], r.right_near[g][...]),
        )

    def far_close(g):
        sent, received = r.block_sent[g], r.block_got[g]

        def close(step, carry):
            index, device = hi_peer(step)
            remote(
                sent.at[index], received.at[index], r.z_ss.at[g, index], r.z_rs.at[g, index], device
            ).wait()
            return carry

        lax.fori_loop(1, n_hi, close, 0)

        def add(index, total):
            return total + received[index].astype(F32)

        r.grads[g][...] = lax.fori_loop(1, n_hi, add, received[0].astype(F32))

    r.sel[0] = selection(parity)
    r.sel[1] = selection(1 - parity)

    keep = r.keep[0].astype(F32)
    x0 = r.x0[...].astype(F32)
    unit0, _ = norm_parts(x0)
    query_in = (unit0 * r.cross_norm[...]).astype(BF)
    r.query_in[...] = query_in
    arrive("cq")
    query = nn(query_in, w.cq[...]).astype(BF).astype(F32) * HEAD_DIM ** (-0.5)
    r.qf[t] = query.astype(BF)
    q_share = share(r.qf, 0)
    r.q_wide[...] = spread(query).astype(BF)

    wait_all(pair_copies)
    pair_sends = []
    for i in range(2):
        for k, peer in enumerate((sibling, far)):
            copy = remote(
                r.wkv.at[t, i], r.wkv.at[t, i], r.wkv_ss.at[i, k], r.wkv_rs.at[i, k], peer
            )
            copy.start()
            pair_sends.append(copy)

    byte_gain = r.byte_norm[...]

    def normalize_rows(src, src_at, dst, dst_at, size):
        unit, _ = norm_parts(src[pl.ds(src_at, size)].astype(F32))
        dst[pl.ds(dst_at, size)] = (unit * byte_gain).astype(BF)

    for i, (start, size) in enumerate(cfg.byte_parts):
        byte_copies[i].wait()

        def chunk(c, carry, start=start):
            at = pl.multiple_of(start + c * ROW_CHUNK, ROW_CHUNK)
            normalize_rows(r.source, at, r.source, at, ROW_CHUNK)
            return carry

        lax.fori_loop(0, size // ROW_CHUNK, chunk, 0)
    tail_at = cfg.main_rows
    for c in range((cfg.key_rows - tail_at) // ROW_CHUNK):
        normalize_rows(r.tail, c * ROW_CHUNK, r.source, tail_at + c * ROW_CHUNK, ROW_CHUNK)

    q_wide = r.q_wide[...]

    def masked_scores(b):
        rows = pl.ds(pl.multiple_of(b * KEY_BLOCK, KEY_BLOCK), KEY_BLOCK)
        return jnp.where(r.mask[b] > 0.0, nt(q_wide, r.key[rows]), -1000000000.0)

    def lanes(values, combine):
        total = values[:, :128]
        for at in range(128, values.shape[1], 128):
            total = combine(total, values[:, at : at + 128])
        return total

    r.stat[...] = jnp.full(r.stat.shape, -3.0e38, F32)

    def project(b, carry):
        rows = pl.ds(pl.multiple_of(b * KEY_BLOCK, KEY_BLOCK), KEY_BLOCK)
        source = r.source[rows]
        r.key[rows] = nn(source, r.wkv[t, 0]).astype(BF)
        r.value[rows] = nn(source, r.wkv[t, 1]).astype(BF)
        r.stat[...] = jnp.maximum(r.stat[...], lanes(masked_scores(b), jnp.maximum))
        return carry

    lax.fori_loop(0, blocks, project, 0)
    largest = jnp.max(r.stat[...], axis=1, keepdims=True)
    r.stat[...] = jnp.zeros(r.stat.shape, F32)
    r.wide_acc[...] = jnp.zeros(r.wide_acc.shape, F32)

    def weigh(b, carry):
        rows = pl.ds(pl.multiple_of(b * KEY_BLOCK, KEY_BLOCK), KEY_BLOCK)
        powers = jnp.exp(masked_scores(b) - largest)
        r.stat[...] += lanes(powers, jnp.add)
        soft = powers.astype(BF)
        r.power[b] = soft
        r.wide_acc[...] += nn(soft, r.value[rows])
        return carry

    lax.fori_loop(0, blocks, weigh, 0)
    summed = jnp.sum(r.stat[...], axis=1, keepdims=True)
    inverse = 1.0 / summed
    r.inverse[...] = inverse
    cross_mix = gathered_heads(r.wide_acc[...] * inverse).astype(BF)
    r.right_own[CO][...] = cross_mix
    r.lse[t] = as_row(largest + jnp.log(summed))

    arrive("co")
    sum_open(0, nn(cross_mix, w.co[...]))
    lse_share = share(r.lse, 1)
    for copy in pair_sends:
        copy.wait()
    forwards = [
        remote(
            r.wkv.at[far_t, i], r.wkv.at[far_t, i], r.wkv_ss.at[i, 2], r.wkv_rs.at[i, 2], sibling
        )
        for i in range(2)
    ]
    for copy in forwards:
        copy.start()
    sum_cross(0)

    r.deep_acc[...] = jnp.zeros(r.deep_acc.shape, F32)

    def blend(b, carry):
        rows = pl.ds(pl.multiple_of(b * KEY_BLOCK, KEY_BLOCK), KEY_BLOCK)
        r.deep_acc[...] += nn(r.power[b], r.source[rows])
        return carry

    lax.fori_loop(0, blocks, blend, 0)
    r.blended[...] = (r.deep_acc[...] * inverse).astype(BF)
    sum_back(0)
    after_cross = x0 + keep * sum_close(0)

    def ffn_open(a, values, gain, win, wout, out_group, n):
        unit, scale = norm_parts(values)
        r.unit[n][...] = unit
        r.scale[n][...] = scale
        normed = (unit * gain).astype(BF)
        r.normed[n][...] = normed
        arrive(win)
        active, slope = gelu_parts(nn(normed, r.held[win][...]))
        active = active.astype(BF)
        r.slope[n][...] = slope
        r.right_own[out_group][...] = active
        arrive(wout)
        sum_open(a, nn(active, r.held[wout][...]))

    ffn_open(1, after_cross, r.ffn_norm1[...], "fi1", "fo1", FO1, 0)

    def own_norm(c, carry):
        at = pl.multiple_of(c * OWN_CHUNK, OWN_CHUNK)
        normalize_rows(r.own, at, r.own_source, at, OWN_CHUNK)
        return carry

    sum_cross(1)
    lax.fori_loop(0, cfg.own_rows // OWN_CHUNK, own_norm, 0)
    wait_all(forwards)
    own_source = r.own_source[...]

    def own_project(s, carry):
        r.own_key[s] = nn(own_source, r.wkv[s, 0]).astype(BF)
        r.own_value[s] = nn(own_source, r.wkv[s, 1]).astype(BF)
        return carry

    lax.fori_loop(0, 4, own_project, 0)
    sum_back(1)
    after_ffn1 = after_cross + sum_close(1)

    unit_s, scale_s = norm_parts(after_ffn1)
    r.unit[1][...] = unit_s
    r.scale[1][...] = scale_s
    inner_in = (unit_s * r.self_norm[...]).astype(BF)
    r.normed[1][...] = inner_in
    arrive("sq", "sk", "sv", "so")
    factor = HEAD_DIM ** (-0.5)
    self_q = nn(inner_in, w.sq[...]).astype(BF).astype(F32) * factor
    self_k = nn(inner_in, w.sk[...]).astype(BF)
    self_v = nn(inner_in, w.sv[...]).astype(BF)
    self_q_wide = spread(self_q).astype(BF)
    self_scores = nt(self_k, self_q_wide)
    self_powers = jnp.exp(self_scores - jnp.max(self_scores, axis=0, keepdims=True))
    self_soft = self_powers / jnp.sum(self_powers, axis=0, keepdims=True)
    self_mix = gathered_heads(tn(self_soft.astype(BF), self_v)).astype(BF)
    r.self_q_wide[...] = self_q_wide
    r.self_k[...] = self_k
    r.self_v[...] = self_v
    r.self_soft[...] = self_soft
    sum_open(2, nn(self_mix, w.so[...]))
    r.right_own[SO][...] = self_mix
    sum_cross(2)

    wait_all(q_share)
    wait_all(lse_share)
    live = jnp.concatenate([r.own_live[...]] * heads, axis=1)

    def own_powers(s, carry):
        wide = spread(r.qf[s]).astype(BF)
        scores = nt(r.own_key[s], wide)
        r.own_power[s] = (jnp.exp(jnp.minimum(scores - r.lse[s, 0:1], 0.0)) * live).astype(BF)
        return carry

    lax.fori_loop(0, 4, own_powers, 0)
    sum_back(2)
    after_self = after_ffn1 + sum_close(2)

    ffn_open(3, after_self, r.ffn_norm2[...], "fi2", "fo2", FO2, 2)
    cotangent = r.cot[...]

    def ffn_back(a, win, wout, in_group, n, branch):
        grad_hidden = (nt(branch, wout[...]) * r.slope[n][...]).astype(BF)
        r.right_own[in_group][...] = grad_hidden
        sum_open(a, nt(grad_hidden, win[...]))

    ffn_back(4, w.fi2, w.fo2, FI2, 2, cotangent)
    near_send(FO2, cotangent, r.right_own[FO2][...])
    sum_cross(4)
    near_send(FI2, r.normed[2][...], r.right_own[FI2][...])
    sum_cross(3)
    sum_back(4)
    dnormed = sum_close(4)
    r.vec[...] = jnp.zeros(r.vec.shape, F32)
    r.vec[3:4] = jnp.sum(dnormed * r.unit[2][...], axis=0, keepdims=True)
    grad_after_self = cotangent.astype(F32) + norm_back(
        r.unit[2][...], r.scale[2][...], r.ffn_norm2[...], dnormed
    )

    self_branch = grad_after_self.astype(BF)
    self_do = spread(nt(self_branch, w.so[...]).astype(BF)).astype(BF)
    self_soft = r.self_soft[...]
    grad_soft = nt(r.self_v[...], self_do)
    inner_sum = jnp.sum(self_soft * grad_soft, axis=0, keepdims=True)
    self_ds = (self_soft * (grad_soft - inner_sum)).astype(BF)
    self_dk = nn(self_ds, r.self_q_wide[...]).astype(BF)
    self_dv = nn(self_soft.astype(BF), self_do).astype(BF)
    self_dq = (gathered_heads(tn(self_ds, r.self_k[...])) * factor).astype(BF)
    sum_open(
        5, nt(self_dq, w.sq[...]) + nt(self_dk, w.sk[...]) + nt(self_dv, w.sv[...])
    )
    near_send(SO, self_branch, r.right_own[SO][...])
    sum_cross(5)
    near_send(SQKV, r.normed[1][...], jnp.concatenate([self_dq, self_dk, self_dv], axis=1))
    sum_back(3)
    far_send(FO2)
    far_send(FI2)
    sum_back(5)
    dnormed = sum_close(5)
    r.vec[2:3] = jnp.sum(dnormed * r.unit[1][...], axis=0, keepdims=True)
    grad_after_ffn1 = grad_after_self + norm_back(
        r.unit[1][...], r.scale[1][...], r.self_norm[...], dnormed
    )

    branch1 = grad_after_ffn1.astype(BF)
    ffn_back(6, w.fi1, w.fo1, FI1, 0, branch1)
    near_send(FO1, branch1, r.right_own[FO1][...])
    sum_cross(6)
    near_send(FI1, r.normed[0][...], r.right_own[FI1][...])
    r.new_latents[...] = (after_self + sum_close(3)).astype(BF)
    far_send(SO)
    far_send(SQKV)
    sum_back(6)
    dnormed = sum_close(6)
    r.vec[1:2] = jnp.sum(dnormed * r.unit[0][...], axis=0, keepdims=True)
    grad_after_cross = grad_after_ffn1 + norm_back(
        r.unit[0][...], r.scale[0][...], r.ffn_norm1[...], dnormed
    )

    cross_branch = (keep * grad_after_cross).astype(BF)
    dmix = nt(cross_branch, w.co[...]).astype(BF)
    r.dof[t] = dmix
    do_share = share(r.dof, 2)
    do_wide_f32 = spread(dmix)
    do_wide = do_wide_f32.astype(BF)
    mix3 = jnp.concatenate([r.right_own[CO][...].astype(F32)] * heads, axis=0)
    delta = jnp.sum(do_wide_f32 * mix3, axis=1, keepdims=True)
    r.delta[t] = as_row(delta)
    delta_share = share(r.delta, 3)
    near_send(CO, cross_branch, r.right_own[CO][...])
    far_send(FO1)
    r.deep_acc[...] = jnp.zeros(r.deep_acc.shape, F32)
    r.wide_acc[...] = jnp.zeros(r.wide_acc.shape, F32)
    inverse = r.inverse[...]

    def back(b, carry):
        rows = pl.ds(pl.multiple_of(b * KEY_BLOCK, KEY_BLOCK), KEY_BLOCK)
        grad_power = nt(do_wide, r.value[rows])
        ds = (r.power[b].astype(F32) * (inverse * (grad_power - delta))).astype(BF)
        r.wide_acc[...] += nn(ds, r.key[rows])
        r.deep_acc[...] += nn(ds, r.source[rows])
        return carry

    lax.fori_loop(0, blocks, back, 0)
    cross_dq = (gathered_heads(r.wide_acc[...]) * factor).astype(BF)
    sum_open(7, nt(cross_dq, w.cq[...]))
    near_send(CQ, r.query_in[...], cross_dq)
    far_send(FI1)
    sum_cross(7)
    q_wide = r.q_wide[...]
    deep = r.deep_acc[...]
    deep_low = deep.astype(BF)
    blended = r.blended[...]
    gain_row = (
        jnp.sum(deep * nt(q_wide, r.wkv[t, 0]), axis=0, keepdims=True)
        + jnp.sum(blended.astype(F32) * nt(do_wide, r.wkv[t, 1]), axis=0, keepdims=True)
    ) / byte_gain
    r.gain[t] = jnp.concatenate([gain_row, jnp.zeros((7, width), F32)], axis=0)
    gain_share = share(r.gain, 4)

    def key_value_product(which):
        left = r.sel[which]
        return jnp.concatenate(
            [
                nn(nt(left, deep_low).astype(BF), q_wide),
                nn(nt(left, blended).astype(BF), do_wide),
            ],
            axis=1,
        )

    r.pair_s[...] = key_value_product(1).astype(BF)
    pair_copy = remote(r.pair_s, r.pair_r, r.pair_ss, r.pair_rs, near)
    pair_copy.start()
    own_pair = key_value_product(0)

    wait_all(do_share)
    wait_all(delta_share)
    r.own_acc[...] = jnp.zeros(r.own_acc.shape, F32)

    def own_back(s, carry):
        do_here = spread(r.dof[s]).astype(BF)
        q_here = spread(r.qf[s]).astype(BF)
        soft = r.own_power[s]
        grad_power = nt(r.own_value[s], do_here)
        ds = (soft.astype(F32) * (grad_power - r.delta[s, 0:1])).astype(BF)
        dk = nn(ds, q_here).astype(BF)
        dv = nn(soft, do_here).astype(BF)
        r.own_acc[...] += nt(dk, r.wkv[s, 0]) + nt(dv, r.wkv[s, 1])
        return carry

    lax.fori_loop(0, 2, own_back, 0)
    sum_back(7)
    pair_copy.wait()
    hi_send(CKV, own_pair + r.pair_r[...].astype(F32))
    far_send(CO)
    far_send(CQ)
    dnormed = sum_close(7)
    unit0, scale0 = norm_parts(r.x0[...].astype(F32))
    r.vec[0:1] = jnp.sum(dnormed * unit0, axis=0, keepdims=True)
    r.latent_grads[...] = (
        grad_after_cross + norm_back(unit0, scale0, r.cross_norm[...], dnormed)
    ).astype(BF)
    wait_all(gain_share)
    r.vec[4:5] = r.gain[0, 0:1] + r.gain[1, 0:1] + r.gain[2, 0:1] + r.gain[3, 0:1]
    live_count = jnp.sum(jnp.sum(r.mask[...], axis=0), axis=1, keepdims=True)
    lane = lax.broadcasted_iota(jnp.int32, (1, width), 1)
    r.vec[5:6] = keep * jnp.where(lane == 0, live_count, jnp.where(lane == 1, float(lat), 0.0))
    vec_copy = remote(r.vec, r.vec_r, r.vec_ss, r.vec_rs, near)
    vec_copy.start()
    lax.fori_loop(2, 4, own_back, 0)
    vec_copy.wait()
    r.vec_all[hi] = r.vec[...] + r.vec_r[...]

    def vec_hi(step, source_index):
        index, device = hi_peer(step)
        return remote(
            r.vec_all.at[hi],
            r.vec_all.at[source_index],
            r.vh_ss.at[index],
            r.vh_rs.at[source_index],
            device,
        )

    def vec_send(step, carry):
        vec_hi(step, hi).start()
        return carry

    lax.fori_loop(1, n_hi, vec_send, 0)

    def own_norm_back(c, carry):
        rows = pl.ds(pl.multiple_of(c * OWN_CHUNK, OWN_CHUNK), OWN_CHUNK)
        unit, scale = norm_parts(r.own[rows].astype(F32))
        r.byte_grads[rows] = norm_back(unit, scale, byte_gain, r.own_acc[rows]).astype(BF)
        return carry

    lax.fori_loop(0, cfg.own_rows // OWN_CHUNK, own_norm_back, 0)

    for g in range(CKV + 1):
        far_close(g)

    def vec_close(step, carry):
        vec_hi(step, hi_peer(step)[0]).wait()
        return carry

    lax.fori_loop(1, n_hi, vec_close, 0)
    r.vec_out[...] = lax.fori_loop(
        1, n_hi, lambda i, total: total + r.vec_all[i], r.vec_all[0]
    )


def ceil_to(value, step):
    return -(-value // step) * step


def on_device(
    n_dp,
    latents,
    byte_array,
    caption_lengths,
    patch_mask,
    cross_keep,
    cross_norm,
    byte_norm,
    cross_query,
    cross_key,
    cross_value,
    cross_output,
    ffn_norm1,
    ffn_in1,
    ffn_out1,
    self_norm,
    self_query,
    self_key,
    self_value,
    self_output,
    ffn_norm2,
    ffn_in2,
    ffn_out2,
    cotangent,
):
    _, lat, width = latents.shape
    keys = byte_array.shape[1]
    patches = patch_mask.shape[1]
    hw = cross_query.shape[1]
    ff = ffn_in1.shape[1]
    heads = hw // HEAD_DIM
    share = keys // 4
    key_rows = ceil_to(keys, KEY_BLOCK)
    main_rows = keys // ROW_CHUNK * ROW_CHUNK
    own_rows = ceil_to(share, OWN_CHUNK)
    blocks = key_rows // KEY_BLOCK
    n_hi = n_dp // 2
    rpd = width // n_dp
    pr = ceil_to(rpd, 16)
    rt = n_hi * pr
    part = 7 * ROW_CHUNK
    byte_parts = [
        (start, min(part, main_rows - start)) for start in range(0, main_rows, part)
    ]

    positions = jnp.arange(keys - patches, dtype=jnp.int32)
    live = jnp.concatenate(
        [patch_mask[0] != 0, positions < caption_lengths[0]], axis=0
    ).astype(F32)
    t = lax.axis_index("tensor")
    mask = jnp.pad(live, (0, key_rows - keys)).reshape(blocks, 1, KEY_BLOCK)
    own_live = jnp.pad(lax.dynamic_slice_in_dim(live, t * share, share, axis=0), (0, own_rows - share))
    own_live = jnp.broadcast_to(own_live[:, None], (own_rows, 128))
    own = jnp.pad(
        lax.dynamic_slice_in_dim(byte_array[0], t * share, share, axis=0),
        ((0, own_rows - share), (0, 0)),
    )
    tail = jnp.pad(byte_array[0, main_rows:], ((0, key_rows - keys), (0, 0)))

    vmem = pl.BlockSpec(memory_space=pltpu.VMEM)
    hbm = pl.BlockSpec(memory_space=pl.ANY)
    smem = pl.BlockSpec(memory_space=pltpu.SMEM)
    values = dict(
        keep=cross_keep,
        x0=latents[0],
        bytes=byte_array[0],
        tail=tail,
        own=own,
        mask=mask,
        own_live=own_live,
        cross_norm=cross_norm[None],
        byte_norm=byte_norm[None],
        ffn_norm1=ffn_norm1[None],
        self_norm=self_norm[None],
        ffn_norm2=ffn_norm2[None],
        cot=cotangent[0],
        cross_key=cross_key,
        cross_value=cross_value,
        weights=dict(
            cq=cross_query,
            co=cross_output,
            fi1=ffn_in1,
            fo1=ffn_out1,
            sq=self_query,
            sk=self_key,
            sv=self_value,
            so=self_output,
            fi2=ffn_in2,
            fo2=ffn_out2,
        ),
    )
    specs = {name: vmem for name in values}
    specs.update(
        keep=smem,
        bytes=hbm,
        cross_key=hbm,
        cross_value=hbm,
        weights={name: hbm for name in values["weights"]},
    )
    widths = (ff, ff, 3 * hw, hw, ff, ff, hw, hw, 2 * hw)

    def out(shape, kind):
        return jax.ShapeDtypeStruct(shape, kind)

    outputs = dict(
        new_latents=out((lat, width), BF),
        latent_grads=out((lat, width), BF),
        byte_grads=out((own_rows, width), BF),
        vec_out=out((8, width), F32),
        grads=[out((pr, size), F32) for size in widths],
    )

    def buf(*shape):
        return pltpu.VMEM(shape, BF)

    def wide(*shape):
        return pltpu.VMEM(shape, F32)

    def sems(*shape):
        return pltpu.SemaphoreType.DMA(shape)

    stack = heads * lat
    scratch = dict(
        held={name: buf(*value.shape) for name, value in values["weights"].items()},
        wkv=buf(4, 2, width, hw),
        source=buf(key_rows, width),
        key=buf(key_rows, hw),
        value=buf(key_rows, hw),
        power=buf(blocks, stack, KEY_BLOCK),
        stat=wide(stack, 128),
        inverse=wide(stack, 1),
        wide_acc=wide(stack, hw),
        deep_acc=wide(stack, width),
        blended=buf(stack, width),
        q_wide=buf(stack, hw),
        query_in=buf(lat, width),
        qf=buf(4, lat, hw),
        dof=buf(4, lat, hw),
        lse=wide(4, 8, stack),
        delta=wide(4, 8, stack),
        gain=wide(4, 8, width),
        own_source=buf(own_rows, width),
        own_key=buf(4, own_rows, hw),
        own_value=buf(4, own_rows, hw),
        own_power=buf(4, own_rows, stack),
        own_acc=wide(own_rows, width),
        unit=[wide(lat, width) for _ in range(3)],
        scale=[wide(lat, 1) for _ in range(3)],
        normed=[buf(lat, width) for _ in range(3)],
        slope=[wide(lat, ff), wide(8, 128), wide(lat, ff)],
        self_q_wide=buf(stack, hw),
        self_k=buf(lat, hw),
        self_v=buf(lat, hw),
        self_soft=wide(lat, stack),
        sel=buf(2, rt, width),
        ar_s=buf(8, 2, lat // 2, width),
        ar_r1=buf(8, lat // 2, width),
        ar_r2=buf(8, lat // 2, width),
        ar_t=buf(8, 2, lat // 2, width),
        pair_s=buf(rt, 2 * hw),
        pair_r=buf(rt, 2 * hw),
        vec=wide(8, width),
        vec_r=wide(8, width),
        vec_all=wide(n_hi, 8, width),
        left_own=[buf(rt, lat) for _ in range(CKV)],
        left_sent=[buf(rt, lat) for _ in range(CKV)],
        left_near=[buf(rt, lat) for _ in range(CKV)],
        right_own=[buf(lat, size) for size in widths[:CKV]],
        right_near=[buf(lat, size) for size in widths[:CKV]],
        block_sent=[buf(n_hi, pr, size) for size in widths],
        block_got=[buf(n_hi, pr, size) for size in widths],
        byte_sem=sems(len(byte_parts)),
        w_sem=sems(len(values["weights"])),
        pair_sem=sems(2),
        share_ss=sems(5, 3),
        share_rs=sems(5, 3),
        wkv_ss=sems(2, 3),
        wkv_rs=sems(2, 3),
        ar_ss=sems(8, 3),
        ar_rs=sems(8, 3),
        x_ss=sems(CKV, 2),
        x_rs=sems(CKV, 2),
        z_ss=sems(CKV + 1, n_hi),
        z_rs=sems(CKV + 1, n_hi),
        pair_ss=sems(),
        pair_rs=sems(),
        vec_ss=sems(),
        vec_rs=sems(),
        vh_ss=sems(n_hi),
        vh_rs=sems(n_hi),
    )
    tables = (values, outputs, scratch)

    def leaf(node):
        return not isinstance(node, (dict, list))

    flat = [jax.tree.flatten(table, is_leaf=leaf) for table in tables]
    trees = [tree for _, tree in flat]
    counts = [len(leaves) for leaves, _ in flat]
    cfg = SimpleNamespace(
        trees=trees,
        counts=counts,
        lat=lat,
        width=width,
        hw=hw,
        heads=heads,
        n_hi=n_hi,
        pr=pr,
        rpd=rpd,
        blocks=blocks,
        key_rows=key_rows,
        main_rows=main_rows,
        own_rows=own_rows,
        byte_parts=byte_parts,
    )
    results = pl.pallas_call(
        functools.partial(kernel, cfg),
        out_shape=flat[1][0],
        in_specs=jax.tree.leaves(specs, is_leaf=leaf),
        out_specs=[vmem] * counts[1],
        scratch_shapes=flat[2][0],
        compiler_params=pltpu.CompilerParams(
            collective_id=0, has_side_effects=True, vmem_limit_bytes=64 * 2**20
        ),
        name="layers",
    )(*flat[0][0])
    out = SimpleNamespace(**jax.tree.unflatten(trees[1], results))
    grads = [grad[:rpd] for grad in out.grads]

    dp = lax.axis_index("dp")
    vec = out.vec_out
    mine = lax.dynamic_slice(vec, (0, dp * rpd), (8, rpd))
    return (
        out.new_latents[None],
        out.latent_grads[None],
        out.byte_grads[None, :share],
        mine[0],
        vec[4],
        grads[CQ],
        grads[CKV][:, :hw],
        grads[CKV][:, hw:],
        grads[CO].T,
        mine[1],
        grads[FI1],
        grads[FO1].T,
        mine[2],
        grads[SQKV][:, :hw],
        grads[SQKV][:, hw : 2 * hw],
        grads[SQKV][:, 2 * hw :],
        grads[SO].T,
        mine[3],
        grads[FI2],
        grads[FO2].T,
        vec[5, :2],
    )


def solution(mesh):
    in_specs = (
        P("dp", None, None),
        P("dp", None, None),
        P("dp"),
        P("dp", None),
        P("dp"),
        P(),
        P(),
        P(None, "tensor"),
        P(None, "tensor"),
        P(None, "tensor"),
        P("tensor", None),
        P(),
        P(None, "tensor"),
        P("tensor", None),
        P(),
        P(None, "tensor"),
        P(None, "tensor"),
        P(None, "tensor"),
        P("tensor", None),
        P(),
        P(None, "tensor"),
        P("tensor", None),
        P("dp", None, None),
    )
    out_specs = (
        P("dp", None, None),
        P("dp", None, None),
        P("dp", "tensor", None),
        P("dp"),
        P(),
        P("dp", "tensor"),
        P("dp", "tensor"),
        P("dp", "tensor"),
        P("tensor", "dp"),
        P("dp"),
        P("dp", "tensor"),
        P("tensor", "dp"),
        P("dp"),
        P("dp", "tensor"),
        P("dp", "tensor"),
        P("dp", "tensor"),
        P("tensor", "dp"),
        P("dp"),
        P("dp", "tensor"),
        P("tensor", "dp"),
        P(),
    )
    return jax.shard_map(
        functools.partial(on_device, mesh.shape["dp"]),
        mesh=mesh,
        in_specs=in_specs,
        out_specs=out_specs,
        check_vma=False,
    )
```

```python
import functools
from types import SimpleNamespace

import jax
import jax.numpy as jnp
from jax import lax
from jax.experimental import pallas as pl
from jax.experimental.pallas import tpu as pltpu
from jax.sharding import PartitionSpec as P

HEAD_DIM = 64
EPSILON = 1e-05
GELU_A = 0.7978845608
GELU_B = 0.044715
KEY_BLOCK = 640
TAIL = 64
OWN_CHUNK = 272
MESH = pl.DeviceIdType.MESH
BF = jnp.bfloat16
F32 = jnp.float32

FO2, FI2, SQKV, SO, FO1, FI1, CO, CQ, CKV = range(9)


def nn(left, right):
    return lax.dot_general(left, right, (((1,), (0,)), ((), ())), preferred_element_type=F32)


def nt(left, right):
    return lax.dot_general(left, right, (((1,), (1,)), ((), ())), preferred_element_type=F32)


def tn(left, right):
    return lax.dot_general(left, right, (((0,), (0,)), ((), ())), preferred_element_type=F32)


def mean_of(values):
    return jnp.mean(values, axis=-1, keepdims=True)


def norm_parts(values):
    centered = values - mean_of(values)
    scale = lax.rsqrt(mean_of(centered * centered) + EPSILON)
    return centered * scale, scale


def norm_back(unit, scale, gain, grad):
    inner = grad * gain
    return scale * (inner - mean_of(inner) - unit * mean_of(inner * unit))


def gelu_parts(hidden):
    squared = hidden * hidden
    bent = jnp.tanh(GELU_A * hidden * (1.0 + GELU_B * squared))
    half = 0.5 * (1.0 + bent)
    slope = half + 0.5 * hidden * (1.0 - bent * bent) * (GELU_A * (1.0 + 3.0 * GELU_B * squared))
    return hidden * half, slope


def kernel(cfg, *refs):
    r = SimpleNamespace()
    at = 0
    for tree, count in zip(cfg.trees, cfg.counts):
        vars(r).update(jax.tree.unflatten(tree, refs[at : at + count]))
        at += count
    lat, width, hw, heads = cfg.lat, cfg.width, cfg.hw, cfg.heads
    n_hi, pr, rpd, blocks = cfg.n_hi, cfg.pr, cfg.rpd, cfg.blocks
    key_rows, own_rows = cfg.key_rows, cfg.own_rows
    half, stack = lat // 2, heads * lat
    dp, t = lax.axis_index("dp"), lax.axis_index("tensor")
    parity, hi, core = lax.rem(dp, 2), lax.div(dp, 2), lax.rem(t, 2)
    sib_t, far_t, diag_t = t + 1 - 2 * core, lax.rem(t + 2, 4), 3 - t
    sibling, far, diagonal = (dp, sib_t), (dp, far_t), (dp, diag_t)
    near = (dp + 1 - 2 * parity, t)
    side, top = lax.rem(hi, 2), lax.div(hi, 2)
    mid = (dp + 2 - 4 * side, t)
    trio = (sibling, far, diagonal)
    n_top = n_hi // 2

    def top_peer(step):
        index = lax.rem(top + step, n_top)
        return index, (index * 4 + side * 2 + parity, t)

    def remote(src, dst, sends, receives, device):
        return pltpu.make_async_remote_copy(
            src_ref=src,
            dst_ref=dst,
            send_sem=sends,
            recv_sem=receives,
            device_id=device,
            device_id_type=MESH,
        )

    byte_copies = [
        pltpu.make_async_copy(
            r.bytes.at[pl.ds(start, size)], r.source.at[pl.ds(start, size)], r.byte_sem.at[i]
        )
        for i, (start, size) in enumerate(cfg.byte_parts)
    ]
    weight_copies = {
        name: pltpu.make_async_copy(ref, r.held[name], r.w_sem.at[i])
        for i, (name, ref) in enumerate(r.weights.items())
    }
    w = SimpleNamespace(**r.held)

    def arrive(*names):
        for name in names:
            weight_copies[name].wait()

    pair_copies = [
        pltpu.make_async_copy(ref, r.wkv.at[t, i], r.pair_sem.at[i])
        for i, ref in enumerate((r.cross_key, r.cross_value))
    ]
    first, *others = weight_copies.values()
    for copy in [first] + pair_copies + byte_copies + others:
        copy.start()

    barrier = pltpu.get_barrier_semaphore()
    for device in trio + (near, mid):
        pl.semaphore_signal(barrier, inc=1, device_id=device, device_id_type=MESH)

    def greet(step, carry):
        pl.semaphore_signal(barrier, inc=1, device_id=top_peer(step)[1], device_id_type=MESH)
        return carry

    lax.fori_loop(1, n_top, greet, 0)
    pl.semaphore_wait(barrier, 5 + n_top - 1)

    columns = lax.broadcasted_iota(jnp.int32, (lat, hw), 1)
    head_mask = [
        (columns >= h * HEAD_DIM) & (columns < (h + 1) * HEAD_DIM) for h in range(heads)
    ]

    def spread(values):
        wide = values.astype(F32)
        return jnp.concatenate([jnp.where(m, wide, 0.0) for m in head_mask], axis=0)

    def gathered_heads(values):
        total = jnp.where(head_mask[0], values[:lat], 0.0)
        for h in range(1, heads):
            total = total + jnp.where(head_mask[h], values[h * lat : (h + 1) * lat], 0.0)
        return total

    def as_row(column):
        return jnp.broadcast_to(column, (column.shape[0], 128)).T[:8]

    def share(buffer, index):
        copies = [
            remote(
                buffer.at[t], buffer.at[t], r.share_ss.at[index, k], r.share_rs.at[index, k], peer
            )
            for k, peer in enumerate(trio)
        ]
        for copy in copies:
            copy.start()
        return copies

    def wait_all(copies):
        for copy in copies:
            copy.wait()

    hops = {}

    def sum_open(a, part):
        r.ar_s[a] = part.astype(BF).reshape(2, half, width)
        hops[a] = remote(
            r.ar_s.at[a, 1 - core], r.ar_r1.at[a], r.ar_ss.at[a, 0], r.ar_rs.at[a, 0], sibling
        )
        hops[a].start()

    def sum_cross(a):
        hops[a].wait()
        pair = r.ar_s[a, core].astype(F32) + r.ar_r1[a].astype(F32)
        r.ar_t[a, core] = pair.astype(BF)
        hops[a] = remote(
            r.ar_t.at[a, core], r.ar_r2.at[a], r.ar_ss.at[a, 1], r.ar_rs.at[a, 1], far
        )
        hops[a].start()

    def sum_back(a):
        hops[a].wait()
        total = r.ar_t[a, core].astype(F32) + r.ar_r2[a].astype(F32)
        r.ar_t[a, core] = total.astype(BF)
        hops[a] = remote(
            r.ar_t.at[a, core], r.ar_t.at[a, core], r.ar_ss.at[a, 2], r.ar_rs.at[a, 2], sibling
        )
        hops[a].start()

    def sum_close(a):
        hops[a].wait()
        return r.ar_t[a].reshape(lat, width).astype(F32)

    def selection(which):
        shape = (n_top, pr, width)
        block = lax.broadcasted_iota(jnp.int32, shape, 0)
        row = lax.broadcasted_iota(jnp.int32, shape, 1)
        feature = lax.broadcasted_iota(jnp.int32, shape, 2)
        parts = []
        for flank in (side, 1 - side):
            hit = (feature == (block * 4 + flank * 2 + which) * rpd + row) & (row < rpd)
            parts.append(jnp.where(hit, 1.0, 0.0).astype(BF).reshape(n_top * pr, width))
        return jnp.concatenate(parts, axis=0)

    near_copies = {}

    def near_send(g, left, right):
        own, sent, right_own = r.left_own[g], r.left_sent[g], r.right_own[g]
        sent[...] = nt(r.sel[1], left).astype(BF)
        right_own[...] = right
        copies = [
            remote(sent, r.left_near[g], r.x_ss.at[g, 0], r.x_rs.at[g, 0], near),
            remote(right_own, r.right_near[g], r.x_ss.at[g, 1], r.x_rs.at[g, 1], near),
        ]
        for copy in copies:
            copy.start()
        own[...] = nt(r.sel[0], left).astype(BF)
        near_copies[g] = copies

    rows_half = n_top * pr

    def mid_copy(g):
        return remote(r.mid_sent[g], r.mid_got[g], r.m_ss.at[g], r.m_rs.at[g], mid)

    def product(g, start):
        rows = pl.ds(start, rows_half)
        return nn(r.left_own[g][rows], r.right_own[g][...]) + nn(
            r.left_near[g][rows], r.right_near[g][...]
        )

    def mid_send(g):
        wait_all(near_copies[g])
        r.mid_sent[g][...] = product(g, rows_half).astype(BF)
        mid_copy(g).start()

    def top_send(g):
        mid_copy(g).wait()
        own = r.pair_own[:rows_half] if g == CKV else product(g, 0)
        total = own + r.mid_got[g][...].astype(F32)
        sent, received = r.block_sent[g], r.block_got[g]
        sent[...] = total.astype(BF).reshape(n_top, pr, total.shape[-1])

        def send(step, carry):
            index, device = top_peer(step)
            remote(
                sent.at[index], received.at[top], r.z_ss.at[g, index], r.z_rs.at[g, top], device
            ).start()
            return carry

        lax.fori_loop(1, n_top, send, 0)
        received[top] = sent[top]

    def top_close(g):
        sent, received = r.block_sent[g], r.block_got[g]

        def close(step, carry):
            index, device = top_peer(step)
            remote(
                sent.at[index], received.at[index], r.z_ss.at[g, index], r.z_rs.at[g, index], device
            ).wait()
            return carry

        lax.fori_loop(1, n_top, close, 0)

        def add(index, total):
            return total + received[index].astype(F32)

        total = lax.fori_loop(1, n_top, add, received[0].astype(F32))[:rpd]
        if g == SQKV:
            for i in range(3):
                r.self_grads[i][...] = total[:, i * hw : (i + 1) * hw]
        elif g == CKV:
            for i in range(2):
                r.pair_grads[i][...] = total[:, i * hw : (i + 1) * hw]
        elif g in (SO, CO):
            padded = jnp.concatenate([total, jnp.zeros((ceil_to(rpd, 128) - rpd, hw), F32)], axis=0)
            r.grads[g][...] = padded.T[:, :rpd]
        else:
            r.grads[g][...] = total

    def row_of(ref):
        return ref[...].reshape(1, width)

    r.sel[0] = selection(parity)
    r.sel[1] = selection(1 - parity)

    keep = r.keep[0].astype(F32)
    x0 = r.x0[...].astype(F32)
    unit0, _ = norm_parts(x0)
    query_in = (unit0 * row_of(r.cross_norm)).astype(BF)
    r.query_in[...] = query_in
    arrive("cq")
    query = nt(query_in, w.cq[...]).astype(BF).astype(F32) * HEAD_DIM ** (-0.5)
    r.qf[t] = query.astype(BF)
    q_share = share(r.qf, 0)
    r.q_wide[...] = spread(query).astype(BF)

    wait_all(pair_copies)
    pair_sends = []
    for i in range(2):
        for k, peer in enumerate((sibling, far)):
            copy = remote(
                r.wkv.at[t, i], r.wkv.at[t, i], r.wkv_ss.at[i, k], r.wkv_rs.at[i, k], peer
            )
            copy.start()
            pair_sends.append(copy)

    for b in range(blocks):
        start = b * KEY_BLOCK
        size = min(cfg.patches - start, KEY_BLOCK)
        if size < KEY_BLOCK:
            lane = lax.broadcasted_iota(jnp.int32, (1, KEY_BLOCK), 1) + (start - cfg.patches)
            r.mask[b] = jnp.where((lane >= 0) & (lane < r.captions[0]), 1.0, 0.0)
        if size > 0:
            patch = r.patch_mask[:, start : start + size]
            r.mask[b, :, :size] = jnp.where(patch != 0, 1.0, 0.0)

    share_at = t * cfg.share
    window = pl.multiple_of(lax.div(share_at, 16) * 16, 16)
    tail_row = lax.broadcasted_iota(jnp.int32, (TAIL, width), 0)
    tail = jnp.where(tail_row < cfg.keys - cfg.main_rows, r.tail[...].astype(F32), 0.0)
    r.source[cfg.main_rows :] = tail.astype(BF)
    for copy in byte_copies:
        copy.wait()
    r.own[...] = r.source[pl.ds(window, own_rows)]
    byte_gain = row_of(r.byte_norm)

    def block_rows(b):
        return pl.ds(pl.multiple_of(b * KEY_BLOCK, KEY_BLOCK), KEY_BLOCK)

    def normalize_block(b, carry):
        rows = block_rows(b)
        unit, _ = norm_parts(r.source[rows].astype(F32))
        r.source[rows] = (unit * byte_gain).astype(BF)
        return carry

    lax.fori_loop(0, blocks, normalize_block, 0)

    q_wide = r.q_wide[...]

    def lanes(values, combine):
        total = values[:, :128]
        for at in range(128, values.shape[1], 128):
            total = combine(total, values[:, at : at + 128])
        return total

    largest = jnp.full((stack, 1), -3.0e38, F32)
    r.stat[...] = jnp.zeros(r.stat.shape, F32)
    r.wide_acc[...] = jnp.zeros(r.wide_acc.shape, F32)
    tops = []
    for b in range(blocks):
        rows = pl.ds(b * KEY_BLOCK, KEY_BLOCK)
        source = r.source[rows]
        key = nt(source, r.wkv[t, 0]).astype(BF)
        value = nt(source, r.wkv[t, 1]).astype(BF)
        r.key[rows] = key
        r.value[rows] = value
        scores = jnp.where(r.mask[b] > 0.0, nt(q_wide, key), -1000000000.0)
        top_score = jnp.max(lanes(scores, jnp.maximum), axis=1, keepdims=True)
        before, largest = largest, jnp.maximum(largest, top_score)
        tops.append(largest)
        powers = jnp.exp(scores - largest)
        shrink = jnp.exp(before - largest)
        soft = powers.astype(BF)
        r.power[b] = soft
        r.stat[...] = r.stat[...] * shrink + lanes(powers, jnp.add)
        r.wide_acc[...] = r.wide_acc[...] * shrink + nn(soft, value)
    summed = jnp.sum(r.stat[...], axis=1, keepdims=True)
    inverse = 1.0 / summed
    for b in range(blocks):
        r.weight[b] = inverse * jnp.exp(tops[b] - largest)
    cross_mix = gathered_heads(r.wide_acc[...] * inverse).astype(BF)
    r.right_own[CO][...] = cross_mix
    r.lse[t] = as_row(largest + jnp.log(summed))

    arrive("co")
    sum_open(0, nn(cross_mix, w.co[...]))
    lse_share = share(r.lse, 1)
    for copy in pair_sends:
        copy.wait()
    forwards = [
        remote(
            r.wkv.at[far_t, i], r.wkv.at[far_t, i], r.wkv_ss.at[i, 2], r.wkv_rs.at[i, 2], sibling
        )
        for i in range(2)
    ]
    for copy in forwards:
        copy.start()
    sum_cross(0)

    r.deep_acc[...] = jnp.zeros(r.deep_acc.shape, F32)

    def blend(b, carry):
        r.deep_acc[...] += r.weight[b] * nn(r.power[b], r.source[block_rows(b)])
        return carry

    lax.fori_loop(0, blocks, blend, 0)
    r.blended[...] = r.deep_acc[...].astype(BF)
    sum_back(0)
    after_cross = x0 + keep * sum_close(0)

    def ffn_open(a, values, gain, win, wout, out_group, n):
        unit, scale = norm_parts(values)
        r.unit[n][...] = unit
        r.scale[n][...] = scale
        normed = (unit * gain).astype(BF)
        r.normed[n][...] = normed
        arrive(win)
        active, slope = gelu_parts(nn(normed, r.held[win][...]))
        active = active.astype(BF)
        r.slope[n][...] = slope
        r.right_own[out_group][...] = active
        arrive(wout)
        sum_open(a, nn(active, r.held[wout][...]))

    ffn_open(1, after_cross, row_of(r.ffn_norm1), "fi1", "fo1", FO1, 0)

    sum_cross(1)
    wait_all(forwards)
    own_source = r.source[pl.ds(window, own_rows)]

    def own_project(s, carry):
        r.own_key[s] = nt(own_source, r.wkv[s, 0]).astype(BF)
        r.own_value[s] = nt(own_source, r.wkv[s, 1]).astype(BF)
        return carry

    lax.fori_loop(0, 4, own_project, 0)
    sum_back(1)
    after_ffn1 = after_cross + sum_close(1)

    unit_s, scale_s = norm_parts(after_ffn1)
    r.unit[1][...] = unit_s
    r.scale[1][...] = scale_s
    inner_in = (unit_s * row_of(r.self_norm)).astype(BF)
    r.normed[1][...] = inner_in
    arrive("sq", "sk", "sv", "so")
    factor = HEAD_DIM ** (-0.5)
    self_q = nt(inner_in, w.sq[...]).astype(BF).astype(F32) * factor
    self_k = nt(inner_in, w.sk[...]).astype(BF)
    self_v = nt(inner_in, w.sv[...]).astype(BF)
    self_q_wide = spread(self_q).astype(BF)
    self_scores = nt(self_k, self_q_wide)
    self_powers = jnp.exp(self_scores - jnp.max(self_scores, axis=0, keepdims=True))
    self_soft = self_powers / jnp.sum(self_powers, axis=0, keepdims=True)
    self_mix = gathered_heads(tn(self_soft.astype(BF), self_v)).astype(BF)
    r.self_q_wide[...] = self_q_wide
    r.self_k[...] = self_k
    r.self_v[...] = self_v
    r.self_soft[...] = self_soft
    sum_open(2, nn(self_mix, w.so[...]))
    r.right_own[SO][...] = self_mix
    sum_cross(2)

    wait_all(q_share)
    wait_all(lse_share)
    live_row = jnp.concatenate([r.mask[b] for b in range(blocks)], axis=1)
    live_row = jnp.broadcast_to(live_row, (8, key_rows))
    live_row = pltpu.roll(live_row, lax.rem(key_rows - window, key_rows), 1)
    live_column = live_row[:, : ceil_to(own_rows, 128)].T[:own_rows, :1]
    live = jnp.broadcast_to(live_column, (own_rows, stack))

    def own_powers(s, carry):
        wide = spread(r.qf[s]).astype(BF)
        scores = nt(r.own_key[s], wide)
        r.own_power[s] = (jnp.exp(jnp.minimum(scores - r.lse[s, 0:1], 0.0)) * live).astype(BF)
        return carry

    lax.fori_loop(0, 4, own_powers, 0)
    sum_back(2)
    after_self = after_ffn1 + sum_close(2)

    ffn_open(3, after_self, row_of(r.ffn_norm2), "fi2", "fo2", FO2, 2)
    cotangent = r.cot[...]

    def ffn_back(a, win, wout, in_group, n, branch):
        grad_hidden = (nt(branch, wout[...]) * r.slope[n][...]).astype(BF)
        r.right_own[in_group][...] = grad_hidden
        sum_open(a, nt(grad_hidden, win[...]))

    ffn_back(4, w.fi2, w.fo2, FI2, 2, cotangent)
    near_send(FO2, cotangent, r.right_own[FO2][...])
    sum_cross(4)
    near_send(FI2, r.normed[2][...], r.right_own[FI2][...])
    sum_cross(3)
    sum_back(4)
    dnormed = sum_close(4)
    r.vec[...] = jnp.zeros(r.vec.shape, F32)
    r.vec[3:4] = jnp.sum(dnormed * r.unit[2][...], axis=0, keepdims=True)
    grad_after_self = cotangent.astype(F32) + norm_back(
        r.unit[2][...], r.scale[2][...], row_of(r.ffn_norm2), dnormed
    )

    self_branch = grad_after_self.astype(BF)
    self_do = spread(nt(self_branch, w.so[...]).astype(BF)).astype(BF)
    self_soft = r.self_soft[...]
    grad_soft = nt(r.self_v[...], self_do)
    inner_sum = jnp.sum(self_soft * grad_soft, axis=0, keepdims=True)
    self_ds = (self_soft * (grad_soft - inner_sum)).astype(BF)
    self_dk = nn(self_ds, r.self_q_wide[...]).astype(BF)
    self_dv = nn(self_soft.astype(BF), self_do).astype(BF)
    self_dq = (gathered_heads(tn(self_ds, r.self_k[...])) * factor).astype(BF)
    sum_open(5, nn(self_dq, w.sq[...]) + nn(self_dk, w.sk[...]) + nn(self_dv, w.sv[...]))
    near_send(SO, self_branch, r.right_own[SO][...])
    sum_cross(5)
    near_send(SQKV, r.normed[1][...], jnp.concatenate([self_dq, self_dk, self_dv], axis=1))
    sum_back(3)
    mid_send(FO2)
    sum_back(5)
    dnormed = sum_close(5)
    r.vec[2:3] = jnp.sum(dnormed * r.unit[1][...], axis=0, keepdims=True)
    grad_after_ffn1 = grad_after_self + norm_back(
        r.unit[1][...], r.scale[1][...], row_of(r.self_norm), dnormed
    )

    branch1 = grad_after_ffn1.astype(BF)
    ffn_back(6, w.fi1, w.fo1, FI1, 0, branch1)
    near_send(FO1, branch1, r.right_own[FO1][...])
    sum_cross(6)
    near_send(FI1, r.normed[0][...], r.right_own[FI1][...])
    r.new_latents[...] = (after_self + sum_close(3)).astype(BF)
    mid_send(FI2)
    sum_back(6)
    dnormed = sum_close(6)
    r.vec[1:2] = jnp.sum(dnormed * r.unit[0][...], axis=0, keepdims=True)
    grad_after_cross = grad_after_ffn1 + norm_back(
        r.unit[0][...], r.scale[0][...], row_of(r.ffn_norm1), dnormed
    )

    cross_branch = (keep * grad_after_cross).astype(BF)
    dmix = nt(cross_branch, w.co[...]).astype(BF)
    r.dof[t] = dmix
    do_share = share(r.dof, 2)
    do_wide_f32 = spread(dmix)
    do_wide = do_wide_f32.astype(BF)
    mix3 = jnp.concatenate([r.right_own[CO][...].astype(F32)] * heads, axis=0)
    delta = jnp.sum(do_wide_f32 * mix3, axis=1, keepdims=True)
    r.delta[t] = as_row(delta)
    delta_share = share(r.delta, 3)
    near_send(CO, cross_branch, r.right_own[CO][...])
    mid_send(SO)
    mid_send(SQKV)
    top_send(FO2)
    r.deep_acc[...] = jnp.zeros(r.deep_acc.shape, F32)
    r.wide_acc[...] = jnp.zeros(r.wide_acc.shape, F32)

    def back(b, carry):
        rows = block_rows(b)
        grad_power = nt(do_wide, r.value[rows])
        ds = (r.power[b].astype(F32) * (r.weight[b] * (grad_power - delta))).astype(BF)
        r.wide_acc[...] += nn(ds, r.key[rows])
        r.deep_acc[...] += nn(ds, r.source[rows])
        return carry

    lax.fori_loop(0, blocks, back, 0)
    cross_dq = (gathered_heads(r.wide_acc[...]) * factor).astype(BF)
    sum_open(7, nn(cross_dq, w.cq[...]))
    near_send(CQ, r.query_in[...], cross_dq)
    sum_cross(7)
    q_wide = r.q_wide[...]
    deep = r.deep_acc[...]
    deep_low = deep.astype(BF)
    blended = r.blended[...]
    gain_row = (
        jnp.sum(deep * nn(q_wide, r.wkv[t, 0]), axis=0, keepdims=True)
        + jnp.sum(blended.astype(F32) * nn(do_wide, r.wkv[t, 1]), axis=0, keepdims=True)
    ) / byte_gain
    r.gain[t] = jnp.concatenate([gain_row, jnp.zeros((7, width), F32)], axis=0)
    gain_share = share(r.gain, 4)

    def key_value_product(which):
        left = r.sel[which]
        return jnp.concatenate(
            [
                nn(nt(left, deep_low).astype(BF), q_wide),
                nn(nt(left, blended).astype(BF), do_wide),
            ],
            axis=1,
        )

    r.pair_s[...] = key_value_product(1).astype(BF)
    pair_copy = remote(r.pair_s, r.pair_r, r.pair_ss, r.pair_rs, near)
    pair_copy.start()
    r.pair_own[...] = key_value_product(0)
    mid_send(FO1)
    top_send(FI2)

    wait_all(do_share)
    wait_all(delta_share)
    r.own_acc[...] = jnp.zeros(r.own_acc.shape, F32)

    def own_back(s, carry):
        do_here = spread(r.dof[s]).astype(BF)
        q_here = spread(r.qf[s]).astype(BF)
        soft = r.own_power[s]
        grad_power = nt(r.own_value[s], do_here)
        ds = (soft.astype(F32) * (grad_power - r.delta[s, 0:1])).astype(BF)
        dk = nn(ds, q_here).astype(BF)
        dv = nn(soft, do_here).astype(BF)
        r.own_acc[...] += nn(dk, r.wkv[s, 0]) + nn(dv, r.wkv[s, 1])
        return carry

    lax.fori_loop(0, 2, own_back, 0)
    sum_back(7)
    mid_send(FI1)
    mid_send(CO)
    mid_send(CQ)
    top_send(SO)
    top_send(SQKV)
    lax.fori_loop(2, 3, own_back, 0)
    pair_copy.wait()
    r.pair_own[...] += r.pair_r[...].astype(F32)
    r.mid_sent[CKV][...] = r.pair_own[rows_half:].astype(BF)
    mid_copy(CKV).start()
    dnormed = sum_close(7)
    unit0, scale0 = norm_parts(r.x0[...].astype(F32))
    r.vec[0:1] = jnp.sum(dnormed * unit0, axis=0, keepdims=True)
    r.latent_grads[...] = (
        grad_after_cross + norm_back(unit0, scale0, row_of(r.cross_norm), dnormed)
    ).astype(BF)
    wait_all(gain_share)
    r.vec[4:5] = r.gain[0, 0:1] + r.gain[1, 0:1] + r.gain[2, 0:1] + r.gain[3, 0:1]
    live_count = jnp.sum(jnp.sum(r.mask[...], axis=0), axis=1, keepdims=True)
    lane = lax.broadcasted_iota(jnp.int32, (1, width), 1)
    r.vec[5:6] = keep * jnp.where(lane == 0, live_count, jnp.where(lane == 1, float(lat), 0.0))
    vec_copy = remote(r.vec, r.vec_r, r.vec_ss.at[0], r.vec_rs.at[0], near)
    vec_copy.start()
    top_send(FO1)
    lax.fori_loop(3, 4, own_back, 0)
    vec_copy.wait()
    r.vec[...] += r.vec_r[...]
    vec_copy = remote(r.vec, r.vec_m, r.vec_ss.at[1], r.vec_rs.at[1], mid)
    vec_copy.start()
    for g in (CO, CQ, FI1):
        top_send(g)

    def own_norm_back(c, carry):
        rows = pl.ds(pl.multiple_of(c * OWN_CHUNK, OWN_CHUNK), OWN_CHUNK)
        unit, scale = norm_parts(r.own[rows].astype(F32))
        r.own_acc[rows] = norm_back(unit, scale, byte_gain, r.own_acc[rows])
        return carry

    lax.fori_loop(0, own_rows // OWN_CHUNK, own_norm_back, 0)
    top_send(CKV)
    vec_copy.wait()
    r.vec_all[top] = r.vec[...] + r.vec_m[...]

    def vec_top(step, source_index):
        index, device = top_peer(step)
        return remote(
            r.vec_all.at[top],
            r.vec_all.at[source_index],
            r.vh_ss.at[index],
            r.vh_rs.at[source_index],
            device,
        )

    def vec_send(step, carry):
        vec_top(step, top).start()
        return carry

    lax.fori_loop(1, n_top, vec_send, 0)
    for k in range(4):

        @pl.when(t == k)
        def _(skip=k * cfg.share % 16):
            r.byte_grads[...] = r.own_acc[skip : skip + cfg.share].astype(BF)

    for g in range(CKV + 1):
        top_close(g)

    def vec_close(step, carry):
        vec_top(step, top_peer(step)[0]).wait()
        return carry

    lax.fori_loop(1, n_top, vec_close, 0)
    vec = lax.fori_loop(1, n_top, lambda i, total: total + r.vec_all[i], r.vec_all[0])
    mine = pltpu.roll(vec, lax.rem(width - dp * rpd, width), 1)
    for i in range(4):
        r.gain_grads[i][...] = mine[i : i + 1, :rpd].reshape(rpd)
    r.byte_gain_grad[...] = vec[4:5].reshape(width)
    r.counts[...] = vec[5:6, :2].reshape(2)


def finish(count, *refs):
    sources, targets, held = (refs[i * count : (i + 1) * count] for i in range(3))
    in_sems, out_sems = refs[3 * count :]
    arrivals = [
        pltpu.make_async_copy(src, via, in_sems.at[i])
        for i, (src, via) in enumerate(zip(sources, held))
    ]
    departures = [
        pltpu.make_async_copy(via, dst, out_sems.at[i])
        for i, (via, dst) in enumerate(zip(held, targets))
    ]
    for copy in arrivals:
        copy.start()
    for arrival, departure in zip(arrivals, departures):
        arrival.wait()
        departure.start()
    for copy in departures:
        copy.wait()


def ceil_to(value, step):
    return -(-value // step) * step


def on_device(
    n_dp,
    latents,
    byte_array,
    caption_lengths,
    patch_mask,
    cross_keep,
    cross_norm,
    byte_norm,
    cross_query,
    cross_key,
    cross_value,
    cross_output,
    ffn_norm1,
    ffn_in1,
    ffn_out1,
    self_norm,
    self_query,
    self_key,
    self_value,
    self_output,
    ffn_norm2,
    ffn_in2,
    ffn_out2,
    cotangent,
):
    _, lat, width = latents.shape
    keys = byte_array.shape[1]
    patches = patch_mask.shape[1]
    hw = cross_query.shape[1]
    ff = ffn_in1.shape[1]
    heads = hw // HEAD_DIM
    share = keys // 4
    key_rows = ceil_to(keys, KEY_BLOCK)
    main_rows = keys // TAIL * TAIL
    own_rows = ceil_to(share + 15, OWN_CHUNK)
    blocks = key_rows // KEY_BLOCK
    n_hi = n_dp // 2
    n_top = n_hi // 2
    rpd = width // n_dp
    pr = ceil_to(rpd, 16)
    rt = n_hi * pr
    part = 7 * TAIL
    byte_parts = [
        (start, min(part, main_rows - start)) for start in range(0, main_rows, part)
    ]
    assert main_rows + TAIL == key_rows and 3 * share // 16 * 16 + own_rows <= key_rows

    hbm = pl.BlockSpec(memory_space=pl.ANY)
    smem = pl.BlockSpec(memory_space=pltpu.SMEM)
    values = dict(
        keep=cross_keep,
        captions=caption_lengths,
        x0=latents[0],
        bytes=byte_array[0],
        tail=byte_array[0],
        patch_mask=patch_mask,
        cross_norm=cross_norm,
        byte_norm=byte_norm,
        ffn_norm1=ffn_norm1,
        self_norm=self_norm,
        ffn_norm2=ffn_norm2,
        cot=cotangent[0],
        cross_key=cross_key.T,
        cross_value=cross_value.T,
        weights=dict(
            cq=cross_query.T,
            co=cross_output,
            fi1=ffn_in1,
            fo1=ffn_out1,
            sq=self_query.T,
            sk=self_key.T,
            sv=self_value.T,
            so=self_output,
            fi2=ffn_in2,
            fo2=ffn_out2,
        ),
    )

    def once(array):
        zeros = (0,) * array.ndim
        return pl.BlockSpec(array.shape, lambda i: zeros, pipeline_mode=pl.Buffered(1))

    specs = {name: once(array) for name, array in values.items() if name != "weights"}
    specs.update(
        keep=smem,
        captions=smem,
        bytes=hbm,
        tail=pl.BlockSpec(
            (TAIL, width), lambda i: (main_rows // TAIL, 0), pipeline_mode=pl.Buffered(1)
        ),
        cross_key=hbm,
        cross_value=hbm,
        weights={name: hbm for name in values["weights"]},
    )
    widths = (ff, ff, 3 * hw, hw, ff, ff, hw, hw, 2 * hw)

    def out(shape, kind):
        return jax.ShapeDtypeStruct(shape, kind)

    outputs = dict(
        new_latents=out((lat, width), BF),
        latent_grads=out((lat, width), BF),
        byte_grads=out((share, width), BF),
        gain_grads=[out((rpd,), F32) for _ in range(4)],
        byte_gain_grad=out((width,), F32),
        counts=out((2,), F32),
        self_grads=[out((rpd, hw), F32) for _ in range(3)],
        pair_grads=[out((rpd, hw), F32) for _ in range(2)],
        grads={
            FO2: out((rpd, ff), F32),
            FI2: out((rpd, ff), F32),
            SO: out((hw, rpd), F32),
            FO1: out((rpd, ff), F32),
            FI1: out((rpd, ff), F32),
            CO: out((hw, rpd), F32),
            CQ: out((rpd, hw), F32),
        },
    )

    def buf(*shape):
        return pltpu.VMEM(shape, BF)

    def wide(*shape):
        return pltpu.VMEM(shape, F32)

    def sems(*shape):
        return pltpu.SemaphoreType.DMA(shape)

    stack = heads * lat
    scratch = dict(
        held={name: buf(*value.shape) for name, value in values["weights"].items()},
        wkv=buf(4, 2, hw, width),
        source=buf(key_rows, width),
        key=buf(key_rows, hw),
        value=buf(key_rows, hw),
        power=buf(blocks, stack, KEY_BLOCK),
        stat=wide(stack, 128),
        mask=wide(blocks, 1, KEY_BLOCK),
        weight=wide(blocks, stack, 1),
        wide_acc=wide(stack, hw),
        deep_acc=wide(stack, width),
        blended=buf(stack, width),
        q_wide=buf(stack, hw),
        query_in=buf(lat, width),
        qf=buf(4, lat, hw),
        dof=buf(4, lat, hw),
        lse=wide(4, 8, stack),
        delta=wide(4, 8, stack),
        gain=wide(4, 8, width),
        own=buf(own_rows, width),
        own_key=buf(4, own_rows, hw),
        own_value=buf(4, own_rows, hw),
        own_power=buf(4, own_rows, stack),
        own_acc=wide(own_rows, width),
        unit=[wide(lat, width) for _ in range(3)],
        scale=[wide(lat, 1) for _ in range(3)],
        normed=[buf(lat, width) for _ in range(3)],
        slope=[wide(lat, ff), wide(8, 128), wide(lat, ff)],
        self_q_wide=buf(stack, hw),
        self_k=buf(lat, hw),
        self_v=buf(lat, hw),
        self_soft=wide(lat, stack),
        sel=buf(2, rt, width),
        ar_s=buf(8, 2, lat // 2, width),
        ar_r1=buf(8, lat // 2, width),
        ar_r2=buf(8, lat // 2, width),
        ar_t=buf(8, 2, lat // 2, width),
        pair_own=wide(rt, 2 * hw),
        pair_s=buf(rt, 2 * hw),
        pair_r=buf(rt, 2 * hw),
        vec=wide(8, width),
        vec_r=wide(8, width),
        vec_m=wide(8, width),
        vec_all=wide(n_top, 8, width),
        left_own=[buf(rt, lat) for _ in range(CKV)],
        left_sent=[buf(rt, lat) for _ in range(CKV)],
        left_near=[buf(rt, lat) for _ in range(CKV)],
        right_own=[buf(lat, size) for size in widths[:CKV]],
        right_near=[buf(lat, size) for size in widths[:CKV]],
        mid_sent=[buf(rt // 2, size) for size in widths],
        mid_got=[buf(rt // 2, size) for size in widths],
        block_sent=[buf(n_top, pr, size) for size in widths],
        block_got=[buf(n_top, pr, size) for size in widths],
        byte_sem=sems(len(byte_parts)),
        w_sem=sems(len(values["weights"])),
        pair_sem=sems(2),
        share_ss=sems(5, 3),
        share_rs=sems(5, 3),
        wkv_ss=sems(2, 3),
        wkv_rs=sems(2, 3),
        ar_ss=sems(8, 3),
        ar_rs=sems(8, 3),
        x_ss=sems(CKV, 2),
        x_rs=sems(CKV, 2),
        m_ss=sems(CKV + 1),
        m_rs=sems(CKV + 1),
        z_ss=sems(CKV + 1, n_top),
        z_rs=sems(CKV + 1, n_top),
        pair_ss=sems(),
        pair_rs=sems(),
        vec_ss=sems(2),
        vec_rs=sems(2),
        vh_ss=sems(n_top),
        vh_rs=sems(n_top),
    )
    tables = (values, outputs, scratch)

    def leaf(node):
        return not isinstance(node, (dict, list))

    flat = [jax.tree.flatten(table, is_leaf=leaf) for table in tables]
    trees = [tree for _, tree in flat]
    counts = [len(leaves) for leaves, _ in flat]
    cfg = SimpleNamespace(
        trees=trees,
        counts=counts,
        lat=lat,
        width=width,
        hw=hw,
        heads=heads,
        n_hi=n_hi,
        pr=pr,
        rpd=rpd,
        blocks=blocks,
        key_rows=key_rows,
        main_rows=main_rows,
        own_rows=own_rows,
        byte_parts=byte_parts,
        patches=patches,
        keys=keys,
        share=share,
    )
    results = pl.pallas_call(
        functools.partial(kernel, cfg),
        out_shape=flat[1][0],
        grid=(1,),
        in_specs=jax.tree.leaves(specs, is_leaf=leaf),
        out_specs=[once(array) for array in flat[1][0]],
        scratch_shapes=flat[2][0],
        compiler_params=pltpu.CompilerParams(
            collective_id=0, has_side_effects=True, vmem_limit_bytes=64 * 2**20
        ),
        name="layers",
    )(*flat[0][0])
    results = pl.pallas_call(
        functools.partial(finish, counts[1]),
        out_shape=flat[1][0],
        in_specs=[hbm] * counts[1],
        out_specs=[hbm] * counts[1],
        scratch_shapes=[pltpu.VMEM(array.shape, array.dtype) for array in flat[1][0]]
        + [sems(counts[1])] * 2,
        name="results",
    )(*results)
    out = SimpleNamespace(**jax.tree.unflatten(trees[1], results))
    grads = out.grads
    return (
        out.new_latents[None],
        out.latent_grads[None],
        out.byte_grads[None],
        out.gain_grads[0],
        out.byte_gain_grad,
        grads[CQ],
        out.pair_grads[0],
        out.pair_grads[1],
        grads[CO],
        out.gain_grads[1],
        grads[FI1],
        grads[FO1].T,
        out.gain_grads[2],
        out.self_grads[0],
        out.self_grads[1],
        out.self_grads[2],
        grads[SO],
        out.gain_grads[3],
        grads[FI2],
        grads[FO2].T,
        out.counts,
    )


def solution(mesh):
    in_specs = (
        P("dp", None, None),
        P("dp", None, None),
        P("dp"),
        P("dp", None),
        P("dp"),
        P(),
        P(),
        P(None, "tensor"),
        P(None, "tensor"),
        P(None, "tensor"),
        P("tensor", None),
        P(),
        P(None, "tensor"),
        P("tensor", None),
        P(),
        P(None, "tensor"),
        P(None, "tensor"),
        P(None, "tensor"),
        P("tensor", None),
        P(),
        P(None, "tensor"),
        P("tensor", None),
        P("dp", None, None),
    )
    out_specs = (
        P("dp", None, None),
        P("dp", None, None),
        P("dp", "tensor", None),
        P("dp"),
        P(),
        P("dp", "tensor"),
        P("dp", "tensor"),
        P("dp", "tensor"),
        P("tensor", "dp"),
        P("dp"),
        P("dp", "tensor"),
        P("tensor", "dp"),
        P("dp"),
        P("dp", "tensor"),
        P("dp", "tensor"),
        P("dp", "tensor"),
        P("tensor", "dp"),
        P("dp"),
        P("dp", "tensor"),
        P("tensor", "dp"),
        P(),
    )
    return jax.shard_map(
        functools.partial(on_device, mesh.shape["dp"]),
        mesh=mesh,
        in_specs=in_specs,
        out_specs=out_specs,
        check_vma=False,
    )
```

```python
import functools
from types import SimpleNamespace

import jax
import jax.numpy as jnp
from jax import lax
from jax.experimental import pallas as pl
from jax.experimental.pallas import tpu as pltpu
from jax.sharding import PartitionSpec as P

HEAD_DIM = 64
EPSILON = 1e-05
GELU_A = 0.7978845608
GELU_B = 0.044715
KEY_BLOCK = 640
TAIL = 64
SETS = 4
OWN_CHUNK = 272
MESH = pl.DeviceIdType.MESH
BF = jnp.bfloat16
F32 = jnp.float32

FO2, FI2, SQKV, SO, FO1, FI1, CO, CQ, CV, CK = range(10)
BUNDLES = ((FO2,), (FI2,), (SQKV, SO), (FI1,), (CO, CV), (CQ, CK), (FO1,))
Z_FO2, Z_FI2, Z_SELF, Z_FI1, Z_VALUE, Z_KEY, Z_FO1 = range(7)


def nn(left, right):
    return lax.dot_general(left, right, (((1,), (0,)), ((), ())), preferred_element_type=F32)


def nt(left, right):
    return lax.dot_general(left, right, (((1,), (1,)), ((), ())), preferred_element_type=F32)


def tn(left, right):
    return lax.dot_general(left, right, (((0,), (0,)), ((), ())), preferred_element_type=F32)


def mean_of(values):
    return jnp.mean(values, axis=-1, keepdims=True)


def norm_parts(values):
    centered = values - mean_of(values)
    scale = lax.rsqrt(mean_of(centered * centered) + EPSILON)
    return centered * scale, scale


def norm_back(unit, scale, gain, grad):
    inner = grad * gain
    return scale * (inner - mean_of(inner) - unit * mean_of(inner * unit))


def gelu_parts(hidden):
    squared = hidden * hidden
    bent = jnp.tanh(GELU_A * hidden * (1.0 + GELU_B * squared))
    half = 0.5 * (1.0 + bent)
    slope = half + 0.5 * hidden * (1.0 - bent * bent) * (GELU_A * (1.0 + 3.0 * GELU_B * squared))
    return hidden * half, slope


def kernel(cfg, *refs):
    r = SimpleNamespace()
    at = 0
    for tree, count in zip(cfg.trees, cfg.counts):
        vars(r).update(jax.tree.unflatten(tree, refs[at : at + count]))
        at += count
    lat, width, hw, heads = cfg.lat, cfg.width, cfg.hw, cfg.heads
    n_hi, pr, rpd, blocks = cfg.n_hi, cfg.pr, cfg.rpd, cfg.blocks
    key_rows, own_rows = cfg.key_rows, cfg.own_rows
    half, stack = lat // 2, heads * lat
    dp, t = lax.axis_index("dp"), lax.axis_index("tensor")
    parity, hi, core = lax.rem(dp, 2), lax.div(dp, 2), lax.rem(t, 2)
    sib_t, far_t, diag_t = t + 1 - 2 * core, lax.rem(t + 2, 4), 3 - t
    sibling, far, diagonal = (dp, sib_t), (dp, far_t), (dp, diag_t)
    near = (dp + 1 - 2 * parity, t)
    side, top = lax.rem(hi, 2), lax.div(hi, 2)
    mid = (dp + 2 - 4 * side, t)
    trio = (sibling, far, diagonal)
    n_top = n_hi // 2

    def top_peer(step):
        index = lax.rem(top + step, n_top)
        return index, (index * 4 + side * 2 + parity, t)

    def remote(src, dst, sends, receives, device):
        return pltpu.make_async_remote_copy(
            src_ref=src,
            dst_ref=dst,
            send_sem=sends,
            recv_sem=receives,
            device_id=device,
            device_id_type=MESH,
        )

    byte_copies = [
        pltpu.make_async_copy(
            r.bytes.at[pl.ds(start, size)], r.source.at[pl.ds(start, size)], r.byte_sem.at[i]
        )
        for i, (start, size) in enumerate(cfg.byte_parts)
    ]
    weight_copies = {
        name: pltpu.make_async_copy(ref, r.held[name], r.w_sem.at[i])
        for i, (name, ref) in enumerate(r.weights.items())
    }
    w = SimpleNamespace(**r.held)

    def arrive(*names):
        for name in names:
            weight_copies[name].wait()

    pair_copies = [
        pltpu.make_async_copy(ref, r.wkv.at[t, i], r.pair_sem.at[i])
        for i, ref in enumerate((r.cross_key, r.cross_value))
    ]
    first, *others = weight_copies.values()
    for copy in [first] + pair_copies + byte_copies + others:
        copy.start()

    barrier = pltpu.get_barrier_semaphore()
    for device in trio + (near,):
        pl.semaphore_signal(barrier, inc=1, device_id=device, device_id_type=MESH)

    def greet(step, carry):
        device = (lax.rem(hi + step, n_hi) * 2 + parity, t)
        pl.semaphore_signal(barrier, inc=1, device_id=device, device_id_type=MESH)
        return carry

    lax.fori_loop(1, n_hi, greet, 0)

    columns = lax.broadcasted_iota(jnp.int32, (lat, hw), 1)
    head_mask = [
        (columns >= h * HEAD_DIM) & (columns < (h + 1) * HEAD_DIM) for h in range(heads)
    ]

    def spread(values):
        wide = values.astype(F32)
        return jnp.concatenate([jnp.where(m, wide, 0.0) for m in head_mask], axis=0)

    def gathered_heads(values):
        total = jnp.where(head_mask[0], values[:lat], 0.0)
        for h in range(1, heads):
            total = total + jnp.where(head_mask[h], values[h * lat : (h + 1) * lat], 0.0)
        return total

    def as_row(column):
        return jnp.broadcast_to(column, (column.shape[0], 128)).T[:8]

    def share(buffer, index):
        copies = [
            remote(
                buffer.at[t], buffer.at[t], r.share_ss.at[index, k], r.share_rs.at[index, k], peer
            )
            for k, peer in enumerate(trio)
        ]
        for copy in copies:
            copy.start()
        return copies

    def wait_all(copies):
        for copy in copies:
            copy.wait()

    hops = {}

    def sum_open(a, part):
        r.ar_s[a % SETS] = part.astype(BF).reshape(2, half, width)
        hops[a] = remote(
            r.ar_s.at[a % SETS, 1 - core], r.ar_r1.at[a % SETS], r.ar_ss.at[a, 0], r.ar_rs.at[a, 0], sibling
        )
        hops[a].start()

    def sum_cross(a):
        hops[a].wait()
        pair = r.ar_s[a % SETS, core].astype(F32) + r.ar_r1[a % SETS].astype(F32)
        r.ar_t[a % SETS, core] = pair.astype(BF)
        hops[a] = remote(
            r.ar_t.at[a % SETS, core], r.ar_r2.at[a % SETS], r.ar_ss.at[a, 1], r.ar_rs.at[a, 1], far
        )
        hops[a].start()

    def sum_back(a):
        hops[a].wait()
        total = r.ar_t[a % SETS, core].astype(F32) + r.ar_r2[a % SETS].astype(F32)
        r.ar_t[a % SETS, core] = total.astype(BF)
        hops[a] = remote(
            r.ar_t.at[a % SETS, core], r.ar_t.at[a % SETS, core], r.ar_ss.at[a, 2], r.ar_rs.at[a, 2], sibling
        )
        hops[a].start()

    def sum_close(a):
        hops[a].wait()
        return r.ar_t[a % SETS].reshape(lat, width).astype(F32)

    def selection(which):
        shape = (n_top, pr, width)
        block = lax.broadcasted_iota(jnp.int32, shape, 0)
        row = lax.broadcasted_iota(jnp.int32, shape, 1)
        feature = lax.broadcasted_iota(jnp.int32, shape, 2)
        parts = []
        for flank in (side, 1 - side):
            hit = (feature == (block * 4 + flank * 2 + which) * rpd + row) & (row < rpd)
            parts.append(jnp.where(hit, 1.0, 0.0).astype(BF).reshape(n_top * pr, width))
        return jnp.concatenate(parts, axis=0)

    near_copies = {g: [] for g in range(CK + 1)}

    def near_start(g, i, sent, got):
        copy = remote(sent, got, r.x_ss.at[g, i], r.x_rs.at[g, i], near)
        copy.start()
        near_copies[g].append(copy)

    def near_left(g, left):
        r.left_sent[g][...] = nt(r.sel[1], left).astype(BF)
        near_start(g, 0, r.left_sent[g], r.left_near[g])
        r.left_own[g][...] = nt(r.sel[0], left).astype(BF)

    def near_right(g):
        near_start(g, 1, r.right_own[g], r.right_near[g])

    rows_half = n_top * pr

    def mid_copy(z):
        return remote(r.mid_sent[z], r.mid_got[z], r.m_ss.at[z], r.m_rs.at[z], mid)

    def product(g, start):
        rows = pl.ds(start, rows_half)
        if g >= CV:
            return r.pair_own[g - CV, rows] + r.pair_r[g - CV, rows].astype(F32)
        return nn(r.left_own[g][rows], r.right_own[g][...]) + nn(
            r.left_near[g][rows], r.right_near[g][...]
        )

    def products(z, start):
        parts = [product(g, start) for g in BUNDLES[z]]
        return parts[0] if len(parts) == 1 else jnp.concatenate(parts, axis=1)

    def mid_send(z):
        for g in BUNDLES[z]:
            wait_all(near_copies[g])
        r.mid_sent[z][...] = products(z, rows_half).astype(BF)
        mid_copy(z).start()

    def top_send(z):
        mid_copy(z).wait()
        total = products(z, 0) + r.mid_got[z][...].astype(F32)
        sent, received = r.block_sent[z], r.block_got[z]
        sent[...] = total.astype(BF).reshape(n_top, pr, total.shape[-1])

        def send(step, carry):
            index, device = top_peer(step)
            remote(
                sent.at[index], received.at[top], r.z_ss.at[z, index], r.z_rs.at[z, top], device
            ).start()
            return carry

        lax.fori_loop(1, n_top, send, 0)
        received[top] = sent[top]

    def top_close(z):
        sent, received = r.block_sent[z], r.block_got[z]

        def close(step, carry):
            index, device = top_peer(step)
            remote(
                sent.at[index], received.at[index], r.z_ss.at[z, index], r.z_rs.at[z, index], device
            ).wait()
            return carry

        lax.fori_loop(1, n_top, close, 0)

        def add(index, total):
            return total + received[index].astype(F32)

        total = lax.fori_loop(1, n_top, add, received[0].astype(F32))[:rpd]
        at = 0
        for g in BUNDLES[z]:
            size = cfg.widths[g]
            part, at = total[:, at : at + size], at + size
            if g == SQKV:
                for i in range(3):
                    r.self_grads[i][...] = part[:, i * hw : (i + 1) * hw]
            elif g in (SO, CO):
                pad = jnp.zeros((ceil_to(rpd, 128) - rpd, hw), F32)
                r.grads[g][...] = jnp.concatenate([part, pad], axis=0).T[:, :rpd]
            else:
                r.grads[g][...] = part

    def early_peers(start):
        def step_of(step, carry):
            index = lax.rem(hi + step, n_hi)
            start(index, (index * 2 + parity, t))
            return carry

        lax.fori_loop(1, n_hi, step_of, 0)

    def early_right_copy(index, device, slot):
        return remote(
            r.early_right.at[hi], r.early_right.at[slot], r.er_ss.at[index], r.er_rs.at[slot], device
        )

    def early_left_copy(index, device, slot):
        return remote(
            r.early_sent.at[index], r.early_left.at[slot], r.el_ss.at[index], r.el_rs.at[slot], device
        )

    def early_left_open(left):
        for which in range(2):
            rows = nt(r.sel[which], left).astype(BF).reshape(2, n_top, pr, lat)
            for m in range(n_top):
                r.early_sent[2 * m + side, which] = rows[0, m]
                r.early_sent[2 * m + 1 - side, which] = rows[1, m]
        early_peers(lambda index, device: early_left_copy(index, device, hi).start())
        r.early_left[hi] = r.early_sent[hi]

    def early_copy():
        return remote(r.early_part, r.early_got, r.ep_ss.at[0], r.ep_rs.at[0], near)

    def early_product(which):
        def add(index, total):
            return total + nn(r.early_left[index, which], r.early_right[index])

        return lax.fori_loop(0, n_hi, add, jnp.zeros((pr, width), F32))

    def early_send():
        def wait(index, device):
            early_right_copy(index, device, index).wait()
            early_left_copy(index, device, index).wait()

        early_peers(wait)
        r.early_part[...] = early_product(1).astype(BF)
        early_copy().start()
        r.grads[FO1][...] = early_product(0)[:rpd]

    def early_close():
        early_copy().wait()
        r.grads[FO1][...] += r.early_got[:rpd].astype(F32)

    early = cfg.early

    def row_of(ref):
        return ref[...].reshape(1, width)

    keep = r.keep[0].astype(F32)
    x0 = r.x0[...].astype(F32)
    unit0, _ = norm_parts(x0)
    query_in = (unit0 * row_of(r.cross_norm)).astype(BF)
    r.query_in[...] = query_in
    arrive("cq")
    query = nt(query_in, w.cq[...]).astype(BF).astype(F32) * HEAD_DIM ** (-0.5)
    r.qf[t] = query.astype(BF)
    r.q_wide[...] = spread(query).astype(BF)

    pl.semaphore_wait(barrier, 4 + n_hi - 1)

    wait_all(pair_copies)

    def pair_part(part, owner, k, peer):
        i, start, size = ((0, 0, hw), (1, 0, hw // 2), (1, hw // 2, hw // 2))[part]
        ref = r.wkv.at[owner, i, pl.ds(start, size)]
        return remote(ref, ref, r.wkv_ss.at[part, k], r.wkv_rs.at[part, k], peer)

    def pair_send(part):
        copies = [pair_part(part, t, 0, sibling), pair_part(part, t, 1, far)]
        for copy in copies:
            copy.start()
        return copies

    def pair_forward(part, copies):
        wait_all(copies)
        copy = pair_part(part, far_t, 2, sibling)
        copy.start()
        return copy

    key_sends = pair_send(0)

    for b in range(blocks):
        start = b * KEY_BLOCK
        size = min(cfg.patches - start, KEY_BLOCK)
        if size < KEY_BLOCK:
            lane = lax.broadcasted_iota(jnp.int32, (1, KEY_BLOCK), 1) + (start - cfg.patches)
            r.mask[b] = jnp.where((lane >= 0) & (lane < r.captions[0]), 1.0, 0.0)
        if size > 0:
            patch = r.patch_mask[:, start : start + size]
            r.mask[b, :, :size] = jnp.where(patch != 0, 1.0, 0.0)

    share_at = t * cfg.share
    window = pl.multiple_of(lax.div(share_at, 16) * 16, 16)
    tail_row = lax.broadcasted_iota(jnp.int32, (TAIL, width), 0)
    tail = jnp.where(tail_row < cfg.keys - cfg.main_rows, r.tail[...].astype(F32), 0.0)
    r.source[cfg.main_rows :] = tail.astype(BF)
    for copy in byte_copies:
        copy.wait()
    r.own[...] = r.source[pl.ds(window, own_rows)]
    byte_gain = row_of(r.byte_norm)

    def block_rows(b):
        return pl.ds(pl.multiple_of(b * KEY_BLOCK, KEY_BLOCK), KEY_BLOCK)

    q_wide = r.q_wide[...]

    def lanes(values, combine):
        total = values[:, :128]
        for at in range(128, values.shape[1], 128):
            total = combine(total, values[:, at : at + 128])
        return total

    largest = jnp.full((stack, 1), -3.0e38, F32)
    r.stat[...] = jnp.zeros(r.stat.shape, F32)
    r.wide_acc[...] = jnp.zeros(r.wide_acc.shape, F32)
    tops = []
    for b in range(blocks):
        rows = pl.ds(b * KEY_BLOCK, KEY_BLOCK)
        unit, _ = norm_parts(r.source[rows].astype(F32))
        source = (unit * byte_gain).astype(BF)
        r.source[rows] = source
        key = nt(source, r.wkv[t, 0]).astype(BF)
        value = nt(source, r.wkv[t, 1]).astype(BF)
        r.key[rows] = key
        r.value[rows] = value
        scores = jnp.where(r.mask[b] > 0.0, nt(q_wide, key), -1000000000.0)
        top_score = jnp.max(lanes(scores, jnp.maximum), axis=1, keepdims=True)
        before, largest = largest, jnp.maximum(largest, top_score)
        tops.append(largest)
        powers = jnp.exp(scores - largest)
        shrink = jnp.exp(before - largest)
        soft = powers.astype(BF)
        r.power[b] = soft
        r.stat[...] = r.stat[...] * shrink + lanes(powers, jnp.add)
        r.wide_acc[...] = r.wide_acc[...] * shrink + nn(soft, value)
    summed = jnp.sum(r.stat[...], axis=1, keepdims=True)
    inverse = 1.0 / summed
    lane = lax.broadcasted_iota(jnp.int32, (stack, 128), 1)
    factors = jnp.zeros((stack, 128), F32)
    for b in range(blocks):
        factors = jnp.where(lane == b, inverse * jnp.exp(tops[b] - largest), factors)
    r.weight[...] = factors

    def weight_of(b):
        picked = lax.broadcasted_iota(jnp.int32, (stack, 128), 1) == b
        return jnp.sum(jnp.where(picked, r.weight[...], 0.0), axis=1, keepdims=True)

    cross_mix = gathered_heads(r.wide_acc[...] * inverse).astype(BF)
    r.right_own[CO][...] = cross_mix
    r.lse[t] = as_row(largest + jnp.log(summed))

    arrive("co")
    sum_open(0, nn(cross_mix, w.co[...]))
    r.sel[1] = selection(1 - parity)
    r.sel[0] = selection(parity)
    sum_cross(0)
    near_right(CO)
    near_left(FO2, r.cot[...])

    r.deep_acc[...] = jnp.zeros(r.deep_acc.shape, F32)

    def blend(b, carry):
        r.deep_acc[...] += weight_of(b) * nn(r.power[b], r.source[block_rows(b)])
        return carry

    lax.fori_loop(0, blocks, blend, 0)
    r.blended[...] = r.deep_acc[...].astype(BF)
    sum_back(0)
    q_share = share(r.qf, 0)
    lse_share = share(r.lse, 1)
    after_cross = x0 + keep * sum_close(0)

    def ffn_open(a, values, gain, win, wout, out_group, n):
        unit, scale = norm_parts(values)
        r.unit[n][...] = unit
        r.scale[n][...] = scale
        normed = (unit * gain).astype(BF)
        r.normed[n][...] = normed
        arrive(win)
        active, slope = gelu_parts(nn(normed, r.held[win][...]))
        active = active.astype(BF)
        r.slope[n][...] = slope
        if out_group == FO1 and early:
            r.early_right[hi] = active
            early_peers(lambda index, device: early_right_copy(index, device, hi).start())
        else:
            r.right_own[out_group][...] = active
            near_right(out_group)
        arrive(wout)
        sum_open(a, nn(active, r.held[wout][...]))

    ffn_open(1, after_cross, row_of(r.ffn_norm1), "fi1", "fo1", FO1, 0)

    sum_cross(1)
    key_forward = pair_forward(0, key_sends)
    near_left(FI1, r.normed[0][...])
    key_forward.wait()
    live_row = jnp.concatenate([r.mask[b] for b in range(blocks)], axis=1)
    live_row = jnp.broadcast_to(live_row, (8, key_rows))
    live_row = pltpu.roll(live_row, lax.rem(key_rows - window, key_rows), 1)
    r.own_live[...] = live_row[:, : ceil_to(own_rows, 128)].T[:own_rows]
    wait_all(q_share)
    wait_all(lse_share)

    def own_powers(s, carry):
        key = nt(r.source[pl.ds(window, own_rows)], r.wkv[s, 0]).astype(BF)
        scores = nt(key, spread(r.qf[s]).astype(BF))
        live = jnp.broadcast_to(r.own_live[:, :1], (own_rows, stack))
        r.own_power[s] = (jnp.exp(jnp.minimum(scores - r.lse[s, 0:1], 0.0)) * live).astype(BF)
        return carry

    lax.fori_loop(0, 2, own_powers, 0)
    sum_back(1)
    value_sends = [pair_send(1)]
    after_ffn1 = after_cross + sum_close(1)

    unit_s, scale_s = norm_parts(after_ffn1)
    r.unit[1][...] = unit_s
    r.scale[1][...] = scale_s
    inner_in = (unit_s * row_of(r.self_norm)).astype(BF)
    r.normed[1][...] = inner_in
    arrive("sq", "sk", "sv", "so")
    factor = HEAD_DIM ** (-0.5)
    self_q = nt(inner_in, w.sq[...]).astype(BF).astype(F32) * factor
    self_k = nt(inner_in, w.sk[...]).astype(BF)
    self_v = nt(inner_in, w.sv[...]).astype(BF)
    self_q_wide = spread(self_q).astype(BF)
    self_scores = nt(self_k, self_q_wide)
    self_powers = jnp.exp(self_scores - jnp.max(self_scores, axis=0, keepdims=True))
    self_soft = self_powers / jnp.sum(self_powers, axis=0, keepdims=True)
    self_mix = gathered_heads(tn(self_soft.astype(BF), self_v)).astype(BF)
    r.self_q_wide[...] = self_q_wide
    r.self_k[...] = self_k
    r.self_v[...] = self_v
    r.self_soft[...] = self_soft
    sum_open(2, nn(self_mix, w.so[...]))
    r.right_own[SO][...] = self_mix
    near_right(SO)
    sum_cross(2)
    near_left(SQKV, inner_in)
    near_left(CQ, r.query_in[...])

    lax.fori_loop(2, 4, own_powers, 0)
    sum_back(2)
    value_sends.append(pair_send(2))
    after_self = after_ffn1 + sum_close(2)

    ffn_open(3, after_self, row_of(r.ffn_norm2), "fi2", "fo2", FO2, 2)
    cotangent = r.cot[...]

    def ffn_back(a, win, wout, in_group, n, branch):
        grad_hidden = (nt(branch, wout[...]) * r.slope[n][...]).astype(BF)
        r.right_own[in_group][...] = grad_hidden
        sum_open(a, nt(grad_hidden, win[...]))

    ffn_back(4, w.fi2, w.fo2, FI2, 2, cotangent)
    near_right(FI2)
    near_left(FI2, r.normed[2][...])
    sum_cross(4)
    value_forwards = [pair_forward(1 + i, copies) for i, copies in enumerate(value_sends)]
    wait_all(value_forwards)

    def own_values(s, carry):
        r.own_value[s] = nt(r.source[pl.ds(window, own_rows)], r.wkv[s, 1]).astype(BF)
        return carry

    lax.fori_loop(0, 4, own_values, 0)
    sum_back(4)
    sum_cross(3)
    mid_send(Z_FO2)
    dnormed = sum_close(4)
    r.vec[...] = jnp.zeros(r.vec.shape, F32)
    r.vec[3:4] = jnp.sum(dnormed * r.unit[2][...], axis=0, keepdims=True)
    grad_after_self = cotangent.astype(F32) + norm_back(
        r.unit[2][...], r.scale[2][...], row_of(r.ffn_norm2), dnormed
    )

    self_branch = grad_after_self.astype(BF)
    self_do = spread(nt(self_branch, w.so[...]).astype(BF)).astype(BF)
    self_soft = r.self_soft[...]
    grad_soft = nt(r.self_v[...], self_do)
    inner_sum = jnp.sum(self_soft * grad_soft, axis=0, keepdims=True)
    self_ds = (self_soft * (grad_soft - inner_sum)).astype(BF)
    self_dk = nn(self_ds, r.self_q_wide[...]).astype(BF)
    self_dv = nn(self_soft.astype(BF), self_do).astype(BF)
    self_dq = (gathered_heads(tn(self_ds, r.self_k[...])) * factor).astype(BF)
    sum_open(5, nn(self_dq, w.sq[...]) + nn(self_dk, w.sk[...]) + nn(self_dv, w.sv[...]))
    r.right_own[SQKV][...] = jnp.concatenate([self_dq, self_dk, self_dv], axis=1)
    near_right(SQKV)
    near_left(SO, self_branch)
    sum_cross(5)
    sum_back(3)
    mid_send(Z_FI2)
    sum_back(5)
    top_send(Z_FO2)
    dnormed = sum_close(5)
    r.vec[2:3] = jnp.sum(dnormed * r.unit[1][...], axis=0, keepdims=True)
    grad_after_ffn1 = grad_after_self + norm_back(
        r.unit[1][...], r.scale[1][...], row_of(r.self_norm), dnormed
    )

    branch1 = grad_after_ffn1.astype(BF)
    ffn_back(6, w.fi1, w.fo1, FI1, 0, branch1)
    near_right(FI1)
    early_left_open(branch1) if early else near_left(FO1, branch1)
    sum_cross(6)
    r.new_latents[...] = (after_self + sum_close(3)).astype(BF)
    mid_send(Z_SELF)
    sum_back(6)
    top_send(Z_FI2)
    dnormed = sum_close(6)
    r.vec[1:2] = jnp.sum(dnormed * r.unit[0][...], axis=0, keepdims=True)
    grad_after_cross = grad_after_ffn1 + norm_back(
        r.unit[0][...], r.scale[0][...], row_of(r.ffn_norm1), dnormed
    )

    cross_branch = (keep * grad_after_cross).astype(BF)
    dmix = nt(cross_branch, w.co[...]).astype(BF)
    r.dof[t] = dmix
    do_share = share(r.dof, 2)
    do_wide_f32 = spread(dmix)
    do_wide = do_wide_f32.astype(BF)
    mix3 = jnp.concatenate([r.right_own[CO][...].astype(F32)] * heads, axis=0)
    delta = jnp.sum(do_wide_f32 * mix3, axis=1, keepdims=True)
    r.delta[t] = as_row(delta)
    delta_share = share(r.delta, 3)
    near_left(CO, cross_branch)

    def pair_open(g, left, right):
        i = g - CV
        r.pair_s[i] = nn(nt(r.sel[1], left).astype(BF), right).astype(BF)
        copy = remote(r.pair_s.at[i], r.pair_r.at[i], r.pair_ss.at[i], r.pair_rs.at[i], near)
        copy.start()
        near_copies[g].append(copy)
        r.pair_own[i] = nn(nt(r.sel[0], left).astype(BF), right)

    blended = r.blended[...]
    pair_open(CV, blended, do_wide)
    r.deep_acc[...] = jnp.zeros(r.deep_acc.shape, F32)
    r.wide_acc[...] = jnp.zeros(r.wide_acc.shape, F32)

    def back(b, carry):
        rows = block_rows(b)
        grad_power = nt(do_wide, r.value[rows])
        ds = (r.power[b].astype(F32) * (weight_of(b) * (grad_power - delta))).astype(BF)
        r.wide_acc[...] += nn(ds, r.key[rows])
        r.deep_acc[...] += nn(ds, r.source[rows])
        return carry

    lax.fori_loop(0, blocks // 2, back, 0)
    mid_send(Z_FI1)
    lax.fori_loop(blocks // 2, blocks, back, 0)
    cross_dq = (gathered_heads(r.wide_acc[...]) * factor).astype(BF)
    sum_open(7, nn(cross_dq, w.cq[...]))
    q_wide = r.q_wide[...]
    deep = r.deep_acc[...]
    deep_low = deep.astype(BF)
    pair_open(CK, deep_low, q_wide)
    r.right_own[CQ][...] = cross_dq
    near_right(CQ)
    sum_cross(7)
    top_send(Z_SELF)
    gain_row = (
        jnp.sum(deep * nn(q_wide, r.wkv[t, 0]), axis=0, keepdims=True)
        + jnp.sum(blended.astype(F32) * nn(do_wide, r.wkv[t, 1]), axis=0, keepdims=True)
    ) / byte_gain
    r.gain[t] = jnp.concatenate([gain_row, jnp.zeros((7, width), F32)], axis=0)
    gain_share = share(r.gain, 4)
    mid_send(Z_VALUE)

    wait_all(do_share)
    wait_all(delta_share)
    r.own_acc[...] = jnp.zeros(r.own_acc.shape, F32)

    def own_back(s, carry):
        do_here = spread(r.dof[s]).astype(BF)
        q_here = spread(r.qf[s]).astype(BF)
        soft = r.own_power[s]
        grad_power = nt(r.own_value[s], do_here)
        ds = (soft.astype(F32) * (grad_power - r.delta[s, 0:1])).astype(BF)
        dk = nn(ds, q_here).astype(BF)
        dv = nn(soft, do_here).astype(BF)
        r.own_acc[...] += nn(dk, r.wkv[s, 0]) + nn(dv, r.wkv[s, 1])
        return carry

    lax.fori_loop(0, 2, own_back, 0)
    sum_back(7)
    mid_send(Z_KEY)
    top_send(Z_FI1)
    dnormed = sum_close(7)
    unit0, scale0 = norm_parts(r.x0[...].astype(F32))
    r.vec[0:1] = jnp.sum(dnormed * unit0, axis=0, keepdims=True)
    r.latent_grads[...] = (
        grad_after_cross + norm_back(unit0, scale0, row_of(r.cross_norm), dnormed)
    ).astype(BF)
    wait_all(gain_share)
    r.vec[4:5] = r.gain[0, 0:1] + r.gain[1, 0:1] + r.gain[2, 0:1] + r.gain[3, 0:1]
    live_count = jnp.sum(jnp.sum(r.mask[...], axis=0), axis=1, keepdims=True)
    lane = lax.broadcasted_iota(jnp.int32, (1, width), 1)
    r.vec[5:6] = keep * jnp.where(lane == 0, live_count, jnp.where(lane == 1, float(lat), 0.0))
    vec_copy = remote(r.vec, r.vec_r, r.vec_ss.at[0], r.vec_rs.at[0], near)
    vec_copy.start()
    lax.fori_loop(2, 4, own_back, 0)
    vec_copy.wait()
    r.vec[...] += r.vec_r[...]
    vec_copy = remote(r.vec, r.vec_m, r.vec_ss.at[1], r.vec_rs.at[1], mid)
    vec_copy.start()
    if early:
        early_send()
    else:
        mid_send(Z_FO1)
    top_send(Z_VALUE)
    top_send(Z_KEY)

    def own_norm_back(c, carry):
        rows = pl.ds(pl.multiple_of(c * OWN_CHUNK, OWN_CHUNK), OWN_CHUNK)
        unit, scale = norm_parts(r.own[rows].astype(F32))
        r.own_acc[rows] = norm_back(unit, scale, byte_gain, r.own_acc[rows])
        return carry

    lax.fori_loop(0, own_rows // OWN_CHUNK, own_norm_back, 0)
    vec_copy.wait()
    r.vec_all[top] = r.vec[...] + r.vec_m[...]

    def vec_top(step, source_index):
        index, device = top_peer(step)
        return remote(
            r.vec_all.at[top],
            r.vec_all.at[source_index],
            r.vh_ss.at[index],
            r.vh_rs.at[source_index],
            device,
        )

    def vec_send(step, carry):
        vec_top(step, top).start()
        return carry

    lax.fori_loop(1, n_top, vec_send, 0)
    for k in range(4):

        @pl.when(t == k)
        def _(skip=k * cfg.share % 16):
            r.byte_grads[...] = r.own_acc[skip : skip + cfg.share].astype(BF)

    if early:
        early_close()
    else:
        top_send(Z_FO1)
    for z in range(len(BUNDLES) - early):
        top_close(z)

    def vec_close(step, carry):
        vec_top(step, top_peer(step)[0]).wait()
        return carry

    lax.fori_loop(1, n_top, vec_close, 0)
    vec = lax.fori_loop(1, n_top, lambda i, total: total + r.vec_all[i], r.vec_all[0])
    mine = pltpu.roll(vec, lax.rem(width - dp * rpd, width), 1)
    for i in range(4):
        r.gain_grads[i][...] = mine[i : i + 1, :rpd].reshape(rpd)
    r.byte_gain_grad[...] = vec[4:5].reshape(width)
    r.counts[...] = vec[5:6, :2].reshape(2)


def finish(count, *refs):
    sources, targets, held = (refs[i * count : (i + 1) * count] for i in range(3))
    in_sems, out_sems = refs[3 * count :]
    arrivals = [
        pltpu.make_async_copy(src, via, in_sems.at[i])
        for i, (src, via) in enumerate(zip(sources, held))
    ]
    departures = [
        pltpu.make_async_copy(via, dst, out_sems.at[i])
        for i, (via, dst) in enumerate(zip(held, targets))
    ]
    for copy in arrivals:
        copy.start()
    for arrival, departure in zip(arrivals, departures):
        arrival.wait()
        departure.start()
    for copy in departures:
        copy.wait()


def ceil_to(value, step):
    return -(-value // step) * step


def on_device(
    n_dp,
    latents,
    byte_array,
    caption_lengths,
    patch_mask,
    cross_keep,
    cross_norm,
    byte_norm,
    cross_query,
    cross_key,
    cross_value,
    cross_output,
    ffn_norm1,
    ffn_in1,
    ffn_out1,
    self_norm,
    self_query,
    self_key,
    self_value,
    self_output,
    ffn_norm2,
    ffn_in2,
    ffn_out2,
    cotangent,
):
    _, lat, width = latents.shape
    keys = byte_array.shape[1]
    patches = patch_mask.shape[1]
    hw = cross_query.shape[1]
    ff = ffn_in1.shape[1]
    heads = hw // HEAD_DIM
    share = keys // 4
    key_rows = ceil_to(keys, KEY_BLOCK)
    main_rows = keys // TAIL * TAIL
    own_rows = ceil_to(share + 15, OWN_CHUNK)
    blocks = key_rows // KEY_BLOCK
    n_hi = n_dp // 2
    n_top = n_hi // 2
    rpd = width // n_dp
    pr = ceil_to(rpd, 16)
    rt = n_hi * pr
    part = 7 * TAIL
    byte_parts = [
        (start, min(part, main_rows - start)) for start in range(0, main_rows, part)
    ]
    assert main_rows + TAIL == key_rows and 3 * share // 16 * 16 + own_rows <= key_rows

    hbm = pl.BlockSpec(memory_space=pl.ANY)
    smem = pl.BlockSpec(memory_space=pltpu.SMEM)
    values = dict(
        keep=cross_keep,
        captions=caption_lengths,
        x0=latents[0],
        bytes=byte_array[0],
        tail=byte_array[0],
        patch_mask=patch_mask,
        cross_norm=cross_norm,
        byte_norm=byte_norm,
        ffn_norm1=ffn_norm1,
        self_norm=self_norm,
        ffn_norm2=ffn_norm2,
        cot=cotangent[0],
        cross_key=cross_key.T,
        cross_value=cross_value.T,
        weights=dict(
            cq=cross_query.T,
            co=cross_output,
            fi1=ffn_in1,
            fo1=ffn_out1,
            sq=self_query.T,
            sk=self_key.T,
            sv=self_value.T,
            so=self_output,
            fi2=ffn_in2,
            fo2=ffn_out2,
        ),
    )

    def once(array):
        zeros = (0,) * array.ndim
        return pl.BlockSpec(array.shape, lambda i: zeros, pipeline_mode=pl.Buffered(1))

    specs = {name: once(array) for name, array in values.items() if name != "weights"}
    specs.update(
        keep=smem,
        captions=smem,
        bytes=hbm,
        tail=pl.BlockSpec(
            (TAIL, width), lambda i: (main_rows // TAIL, 0), pipeline_mode=pl.Buffered(1)
        ),
        cross_key=hbm,
        cross_value=hbm,
        weights={name: hbm for name in values["weights"]},
    )
    widths = (ff, ff, 3 * hw, hw, ff, ff, hw, hw, hw, hw)
    early = n_hi <= 4
    bundles = [
        128 if early and bundle == (FO1,) else sum(widths[g] for g in bundle) for bundle in BUNDLES
    ]

    def out(shape, kind):
        return jax.ShapeDtypeStruct(shape, kind)

    outputs = dict(
        new_latents=out((lat, width), BF),
        latent_grads=out((lat, width), BF),
        byte_grads=out((share, width), BF),
        gain_grads=[out((rpd,), F32) for _ in range(4)],
        byte_gain_grad=out((width,), F32),
        counts=out((2,), F32),
        self_grads=[out((rpd, hw), F32) for _ in range(3)],
        grads={
            FO2: out((rpd, ff), F32),
            FI2: out((rpd, ff), F32),
            SO: out((hw, rpd), F32),
            FO1: out((rpd, ff), F32),
            FI1: out((rpd, ff), F32),
            CO: out((hw, rpd), F32),
            CQ: out((rpd, hw), F32),
            CV: out((rpd, hw), F32),
            CK: out((rpd, hw), F32),
        },
    )

    def buf(*shape):
        return pltpu.VMEM(shape, BF)

    def wide(*shape):
        return pltpu.VMEM(shape, F32)

    def sems(*shape):
        return pltpu.SemaphoreType.DMA(shape)

    stack = heads * lat
    left_rows = [16 if early and g == FO1 else rt for g in range(CV)]
    right_columns = [128 if early and g == FO1 else widths[g] for g in range(CV)]
    scratch = dict(
        held={name: buf(*value.shape) for name, value in values["weights"].items()},
        wkv=buf(4, 2, hw, width),
        source=buf(key_rows, width),
        key=buf(key_rows, hw),
        value=buf(key_rows, hw),
        power=buf(blocks, stack, KEY_BLOCK),
        stat=wide(stack, 128),
        mask=wide(blocks, 1, KEY_BLOCK),
        weight=wide(stack, 128),
        wide_acc=wide(stack, hw),
        deep_acc=wide(stack, width),
        blended=buf(stack, width),
        q_wide=buf(stack, hw),
        query_in=buf(lat, width),
        qf=buf(4, lat, hw),
        dof=buf(4, lat, hw),
        lse=wide(4, 8, stack),
        delta=wide(4, 8, stack),
        gain=wide(4, 8, width),
        own=buf(own_rows, width),
        own_value=buf(4, own_rows, hw),
        own_power=buf(4, own_rows, stack),
        own_live=wide(own_rows, 8),
        own_acc=wide(own_rows, width),
        unit=[wide(lat, width) for _ in range(3)],
        scale=[wide(lat, 1) for _ in range(3)],
        normed=[buf(lat, width) for _ in range(3)],
        slope=[wide(lat, ff), wide(8, 128), wide(lat, ff)],
        self_q_wide=buf(stack, hw),
        self_k=buf(lat, hw),
        self_v=buf(lat, hw),
        self_soft=wide(lat, stack),
        sel=buf(2, rt, width),
        ar_s=buf(SETS, 2, lat // 2, width),
        ar_r1=buf(SETS, lat // 2, width),
        ar_r2=buf(SETS, lat // 2, width),
        ar_t=buf(SETS, 2, lat // 2, width),
        pair_own=wide(2, rt, hw),
        pair_s=buf(2, rt, hw),
        pair_r=buf(2, rt, hw),
        vec=wide(8, width),
        vec_r=wide(8, width),
        vec_m=wide(8, width),
        vec_all=wide(n_top, 8, width),
        left_own=[buf(rows, lat) for rows in left_rows],
        left_sent=[buf(rows, lat) for rows in left_rows],
        left_near=[buf(rows, lat) for rows in left_rows],
        right_own=[buf(lat, size) for size in right_columns],
        right_near=[buf(lat, size) for size in right_columns],
        mid_sent=[buf(rt // 2, size) for size in bundles],
        mid_got=[buf(rt // 2, size) for size in bundles],
        block_sent=[buf(n_top, pr, size) for size in bundles],
        block_got=[buf(n_top, pr, size) for size in bundles],
        byte_sem=sems(len(byte_parts)),
        w_sem=sems(len(values["weights"])),
        pair_sem=sems(2),
        share_ss=sems(5, 3),
        share_rs=sems(5, 3),
        wkv_ss=sems(3, 3),
        wkv_rs=sems(3, 3),
        ar_ss=sems(8, 3),
        ar_rs=sems(8, 3),
        x_ss=sems(CV, 2),
        x_rs=sems(CV, 2),
        m_ss=sems(len(BUNDLES)),
        m_rs=sems(len(BUNDLES)),
        z_ss=sems(len(BUNDLES), n_top),
        z_rs=sems(len(BUNDLES), n_top),
        early_right=buf(*((n_hi, lat, ff) if early else (16, 128))),
        early_sent=buf(*((n_hi, 2, pr, lat) if early else (16, 128))),
        early_left=buf(*((n_hi, 2, pr, lat) if early else (16, 128))),
        early_part=buf(pr, ff),
        early_got=buf(pr, ff),
        er_ss=sems(n_hi),
        er_rs=sems(n_hi),
        el_ss=sems(n_hi),
        el_rs=sems(n_hi),
        ep_ss=sems(1),
        ep_rs=sems(1),
        pair_ss=sems(2),
        pair_rs=sems(2),
        vec_ss=sems(2),
        vec_rs=sems(2),
        vh_ss=sems(n_top),
        vh_rs=sems(n_top),
    )
    tables = (values, outputs, scratch)

    def leaf(node):
        return not isinstance(node, (dict, list))

    flat = [jax.tree.flatten(table, is_leaf=leaf) for table in tables]
    trees = [tree for _, tree in flat]
    counts = [len(leaves) for leaves, _ in flat]
    cfg = SimpleNamespace(
        trees=trees,
        counts=counts,
        lat=lat,
        width=width,
        hw=hw,
        heads=heads,
        n_hi=n_hi,
        pr=pr,
        rpd=rpd,
        blocks=blocks,
        key_rows=key_rows,
        main_rows=main_rows,
        own_rows=own_rows,
        byte_parts=byte_parts,
        patches=patches,
        keys=keys,
        share=share,
        widths=widths,
        early=early,
    )
    results = pl.pallas_call(
        functools.partial(kernel, cfg),
        out_shape=flat[1][0],
        grid=(1,),
        in_specs=jax.tree.leaves(specs, is_leaf=leaf),
        out_specs=[once(array) for array in flat[1][0]],
        scratch_shapes=flat[2][0],
        compiler_params=pltpu.CompilerParams(
            collective_id=0, has_side_effects=True, vmem_limit_bytes=64 * 2**20
        ),
        name="layers",
    )(*flat[0][0])
    results = pl.pallas_call(
        functools.partial(finish, counts[1]),
        out_shape=flat[1][0],
        in_specs=[hbm] * counts[1],
        out_specs=[hbm] * counts[1],
        scratch_shapes=[pltpu.VMEM(array.shape, array.dtype) for array in flat[1][0]]
        + [sems(counts[1])] * 2,
        name="results",
    )(*results)
    out = SimpleNamespace(**jax.tree.unflatten(trees[1], results))
    grads = out.grads
    return (
        out.new_latents[None],
        out.latent_grads[None],
        out.byte_grads[None],
        out.gain_grads[0],
        out.byte_gain_grad,
        grads[CQ],
        grads[CK],
        grads[CV],
        grads[CO],
        out.gain_grads[1],
        grads[FI1],
        grads[FO1].T,
        out.gain_grads[2],
        out.self_grads[0],
        out.self_grads[1],
        out.self_grads[2],
        grads[SO],
        out.gain_grads[3],
        grads[FI2],
        grads[FO2].T,
        out.counts,
    )


def solution(mesh):
    in_specs = (
        P("dp", None, None),
        P("dp", None, None),
        P("dp"),
        P("dp", None),
        P("dp"),
        P(),
        P(),
        P(None, "tensor"),
        P(None, "tensor"),
        P(None, "tensor"),
        P("tensor", None),
        P(),
        P(None, "tensor"),
        P("tensor", None),
        P(),
        P(None, "tensor"),
        P(None, "tensor"),
        P(None, "tensor"),
        P("tensor", None),
        P(),
        P(None, "tensor"),
        P("tensor", None),
        P("dp", None, None),
    )
    out_specs = (
        P("dp", None, None),
        P("dp", None, None),
        P("dp", "tensor", None),
        P("dp"),
        P(),
        P("dp", "tensor"),
        P("dp", "tensor"),
        P("dp", "tensor"),
        P("tensor", "dp"),
        P("dp"),
        P("dp", "tensor"),
        P("tensor", "dp"),
        P("dp"),
        P("dp", "tensor"),
        P("dp", "tensor"),
        P("dp", "tensor"),
        P("tensor", "dp"),
        P("dp"),
        P("dp", "tensor"),
        P("tensor", "dp"),
        P(),
    )
    return jax.shard_map(
        functools.partial(on_device, mesh.shape["dp"]),
        mesh=mesh,
        in_specs=in_specs,
        out_specs=out_specs,
        check_vma=False,
    )
```

```python
import functools
from types import SimpleNamespace

import jax
import jax.numpy as jnp
from jax import lax
from jax.experimental import pallas as pl
from jax.experimental.pallas import tpu as pltpu
from jax.sharding import PartitionSpec as P

HEAD_DIM = 64
EPSILON = 1e-05
GELU_A = 0.7978845608
GELU_B = 0.044715
KEY_BLOCK = 640
TAIL = 64
SETS = 4
OWN_CHUNK = 272
MESH = pl.DeviceIdType.MESH
BF = jnp.bfloat16
F32 = jnp.float32

FO2, FI2, SQKV, SO, FO1, FI1, CO, CQ, CV, CK = range(10)
BUNDLES = ((FO2,), (FI2,), (SQKV, SO), (CO, CV), (CQ, CK), (FI1,), (FO1,))
Z_FO2, Z_FI2, Z_SELF, Z_VALUE, Z_KEY, Z_FI1, Z_FO1 = range(7)


def nn(left, right):
    return lax.dot_general(left, right, (((1,), (0,)), ((), ())), preferred_element_type=F32)


def nt(left, right):
    return lax.dot_general(left, right, (((1,), (1,)), ((), ())), preferred_element_type=F32)


def tn(left, right):
    return lax.dot_general(left, right, (((0,), (0,)), ((), ())), preferred_element_type=F32)


def mean_of(values):
    return jnp.mean(values, axis=-1, keepdims=True)


def norm_parts(values):
    centered = values - mean_of(values)
    scale = lax.rsqrt(mean_of(centered * centered) + EPSILON)
    return centered * scale, scale


def norm_back(unit, scale, gain, grad):
    inner = grad * gain
    return scale * (inner - mean_of(inner) - unit * mean_of(inner * unit))


def gelu_parts(hidden):
    squared = hidden * hidden
    bent = jnp.tanh(GELU_A * hidden * (1.0 + GELU_B * squared))
    half = 0.5 * (1.0 + bent)
    slope = half + 0.5 * hidden * (1.0 - bent * bent) * (GELU_A * (1.0 + 3.0 * GELU_B * squared))
    return hidden * half, slope


def kernel(cfg, *refs):
    r = SimpleNamespace()
    at = 0
    for tree, count in zip(cfg.trees, cfg.counts):
        vars(r).update(jax.tree.unflatten(tree, refs[at : at + count]))
        at += count
    lat, width, hw, heads = cfg.lat, cfg.width, cfg.hw, cfg.heads
    n_hi, pr, rpd, blocks = cfg.n_hi, cfg.pr, cfg.rpd, cfg.blocks
    key_rows, own_rows = cfg.key_rows, cfg.own_rows
    half, stack = lat // 2, heads * lat
    dp, t = lax.axis_index("dp"), lax.axis_index("tensor")
    parity, hi, core = lax.rem(dp, 2), lax.div(dp, 2), lax.rem(t, 2)
    sib_t, far_t, diag_t = t + 1 - 2 * core, lax.rem(t + 2, 4), 3 - t
    sibling, far, diagonal = (dp, sib_t), (dp, far_t), (dp, diag_t)
    near = (dp + 1 - 2 * parity, t)
    side, top = lax.rem(hi, 2), lax.div(hi, 2)
    mid = (dp + 2 - 4 * side, t)
    trio = (sibling, far, diagonal)
    n_top = n_hi // 2

    def top_peer(step):
        index = lax.rem(top + step, n_top)
        return index, (index * 4 + side * 2 + parity, t)

    def remote(src, dst, sends, receives, device):
        return pltpu.make_async_remote_copy(
            src_ref=src,
            dst_ref=dst,
            send_sem=sends,
            recv_sem=receives,
            device_id=device,
            device_id_type=MESH,
        )

    byte_copies = [
        pltpu.make_async_copy(
            r.bytes.at[pl.ds(start, size)], r.source.at[pl.ds(start, size)], r.byte_sem.at[i]
        )
        for i, (start, size) in enumerate(cfg.byte_parts)
    ]
    weight_copies = {
        name: pltpu.make_async_copy(ref, r.held[name], r.w_sem.at[i])
        for i, (name, ref) in enumerate(r.weights.items())
    }
    w = SimpleNamespace(**r.held)

    def arrive(*names):
        for name in names:
            weight_copies[name].wait()

    pair_copies = [
        pltpu.make_async_copy(ref, r.wkv.at[t, i], r.pair_sem.at[i])
        for i, ref in enumerate((r.cross_key, r.cross_value))
    ]
    first = weight_copies["cq"]
    others = [
        weight_copies[name]
        for name in ("co", "fi1", "fo1", "sq", "sk", "sv", "so", "fi2", "fo2")
    ]
    quick = [
        pltpu.make_async_copy(ref, r.placed[name], r.quick_sem.at[i])
        for i, (name, ref) in enumerate(r.quick.items())
    ]
    vars(r).update(r.placed)
    share_at = t * cfg.share
    window = pl.multiple_of(lax.div(share_at, 16) * 16, 16)
    own_main = own_rows - TAIL
    own_copies = [
        pltpu.make_async_copy(
            r.bytes.at[pl.ds(pl.multiple_of(window + at, 16), size)],
            r.own.at[pl.ds(at, size)],
            r.own_sem.at[i],
        )
        for i, (at, size) in enumerate(((0, own_main), (own_main, TAIL)))
    ]
    for copy in quick + [first] + pair_copies + byte_copies + own_copies[:1]:
        copy.start()

    @pl.when(t < 3)
    def _():
        own_copies[1].start()

    leaving = SimpleNamespace(
        **jax.tree.map(
            lambda made, out, i: pltpu.make_async_copy(made, out, r.out_sem.at[i]),
            r.made,
            r.outs,
            cfg.out_order,
        )
    )
    left = []

    def leave(copy):
        copy.start()
        left.append(copy)

    vars(r).update(r.made)

    barrier = pltpu.get_barrier_semaphore()
    diag_mid = (dp + 2 - 4 * side + 1 - 2 * parity, t)
    for device in trio + (near, diag_mid):
        pl.semaphore_signal(barrier, inc=1, device_id=device, device_id_type=MESH)

    def greet(step, carry):
        device = (lax.rem(hi + step, n_hi) * 2 + parity, t)
        pl.semaphore_signal(barrier, inc=1, device_id=device, device_id_type=MESH)
        return carry

    lax.fori_loop(1, n_hi, greet, 0)

    columns = lax.broadcasted_iota(jnp.int32, (lat, hw), 1)
    head_mask = [
        (columns >= h * HEAD_DIM) & (columns < (h + 1) * HEAD_DIM) for h in range(heads)
    ]

    def spread(values):
        wide = values.astype(F32)
        return jnp.concatenate([jnp.where(m, wide, 0.0) for m in head_mask], axis=0)

    def gathered_heads(values):
        total = jnp.where(head_mask[0], values[:lat], 0.0)
        for h in range(1, heads):
            total = total + jnp.where(head_mask[h], values[h * lat : (h + 1) * lat], 0.0)
        return total

    def as_row(column):
        return jnp.broadcast_to(column, (column.shape[0], 128)).T[:8]

    def share(buffer, index):
        copies = [
            remote(
                buffer.at[t], buffer.at[t], r.share_ss.at[index, k], r.share_rs.at[index, k], peer
            )
            for k, peer in enumerate(trio)
        ]
        for copy in copies:
            copy.start()
        return copies

    def wait_all(copies):
        for copy in copies:
            copy.wait()

    hops = {}

    def sum_open(a, part):
        r.ar_s[a % SETS] = part.astype(BF).reshape(2, half, width)
        hops[a] = remote(
            r.ar_s.at[a % SETS, 1 - core], r.ar_r1.at[a % SETS], r.ar_ss.at[a, 0], r.ar_rs.at[a, 0], sibling
        )
        hops[a].start()

    def sum_cross(a):
        hops[a].wait()
        pair = r.ar_s[a % SETS, core].astype(F32) + r.ar_r1[a % SETS].astype(F32)
        r.ar_t[a % SETS, core] = pair.astype(BF)
        hops[a] = remote(
            r.ar_t.at[a % SETS, core], r.ar_r2.at[a % SETS], r.ar_ss.at[a, 1], r.ar_rs.at[a, 1], far
        )
        hops[a].start()

    def back_copy(a):
        half_total = r.ar_t.at[a % SETS, core]
        return remote(half_total, half_total, r.ar_ss.at[a, 2], r.ar_rs.at[a, 2], sibling)

    def sum_back(a):
        hops[a].wait()
        total = r.ar_t[a % SETS, core].astype(F32) + r.ar_r2[a % SETS].astype(F32)
        r.ar_t[a % SETS, core] = total.astype(BF)
        back_copy(a).start()

    def sum_close(a):
        back_copy(a).wait()
        return r.ar_t[a % SETS].reshape(lat, width).astype(F32)

    def selection(which):
        shape = (n_top, pr, width)
        block = lax.broadcasted_iota(jnp.int32, shape, 0)
        row = lax.broadcasted_iota(jnp.int32, shape, 1)
        feature = lax.broadcasted_iota(jnp.int32, shape, 2)
        parts = []
        for flank in (side, 1 - side):
            hit = (feature == (block * 4 + flank * 2 + which) * rpd + row) & (row < rpd)
            parts.append(jnp.where(hit, 1.0, 0.0).astype(BF).reshape(n_top * pr, width))
        return jnp.concatenate(parts, axis=0)

    near_copies = {g: [] for g in range(CK + 1)}

    def near_start(g, i, sent, got):
        copy = remote(sent, got, r.x_ss.at[g, i], r.x_rs.at[g, i], near)
        copy.start()
        near_copies[g].append(copy)

    def near_left_start(g, left):
        r.left_sent[g][...] = nt(r.sel[1], left).astype(BF)
        near_start(g, 0, r.left_sent[g], r.left_near[g])

    def near_left(g, left):
        near_left_start(g, left)
        r.left_own[g][...] = nt(r.sel[0], left).astype(BF)

    def near_right(g):
        if g == FO2:
            for i in range(2):
                columns = pl.ds(i * (cfg.widths[g] // 2), cfg.widths[g] // 2)
                near_start(g, 1 + i, r.right_own[g].at[:, columns], r.right_near[g].at[:, columns])
        else:
            near_start(g, 1, r.right_own[g], r.right_near[g])

    rows_half = n_top * pr

    def mid_copy(z):
        return remote(r.mid_sent[z], r.mid_got[z], r.m_ss.at[z], r.m_rs.at[z], mid)

    def product(g, start):
        rows = pl.ds(start, rows_half)
        if g >= CV:
            columns = pl.ds(0 if start == 0 else hw, hw)
            return r.pair_own[g - CV, rows] + r.pair_r[g - CV, :, columns].astype(F32)
        return nn(r.left_own[g][rows], r.right_own[g][...]) + nn(
            r.left_near[g][rows], r.right_near[g][...]
        )

    def products(z, start):
        parts = [product(g, start) for g in BUNDLES[z]]
        return parts[0] if len(parts) == 1 else jnp.concatenate(parts, axis=1)

    def mid_half(i):
        columns = pl.ds(i * (cfg.widths[FO2] // 2), cfg.widths[FO2] // 2)
        sent, got = r.mid_sent[Z_FO2].at[:, columns], r.mid_got[Z_FO2].at[:, columns]
        return remote(sent, got, r.mh_ss.at[i], r.mh_rs.at[i], mid)

    def mid_send_half(i):
        left, right, right_half = near_copies[FO2]
        if i == 0:
            left.wait()
            right.wait()
        else:
            right_half.wait()
        columns = pl.ds(i * (cfg.widths[FO2] // 2), cfg.widths[FO2] // 2)
        rows = pl.ds(rows_half, rows_half)
        part = nn(r.left_own[FO2][rows], r.right_own[FO2][:, columns]) + nn(
            r.left_near[FO2][rows], r.right_near[FO2][:, columns]
        )
        r.mid_sent[Z_FO2][:, columns] = part.astype(BF)
        mid_half(i).start()

    def mid_send(z):
        for g in BUNDLES[z]:
            wait_all(near_copies[g])
        r.mid_sent[z][...] = products(z, rows_half).astype(BF)
        mid_copy(z).start()

    def top_send(z):
        if z == Z_FO2:
            mid_half(0).wait()
            mid_half(1).wait()
        else:
            mid_copy(z).wait()
        total = products(z, 0) + r.mid_got[z][...].astype(F32)
        sent, received = r.block_sent[z], r.block_got[z]
        sent[...] = total.astype(BF).reshape(n_top, pr, total.shape[-1])

        def send(step, carry):
            index, device = top_peer(step)
            remote(
                sent.at[index], received.at[top], r.z_ss.at[z, index], r.z_rs.at[z, top], device
            ).start()
            return carry

        lax.fori_loop(1, n_top, send, 0)
        received[top] = sent[top]

    def top_close(z):
        sent, received = r.block_sent[z], r.block_got[z]

        def close(step, carry):
            index, device = top_peer(step)
            remote(
                sent.at[index], received.at[index], r.z_ss.at[z, index], r.z_rs.at[z, index], device
            ).wait()
            return carry

        lax.fori_loop(1, n_top, close, 0)

        def add(index, total):
            return total + received[index].astype(F32)

        total = lax.fori_loop(1, n_top, add, received[0].astype(F32))[:rpd]
        at = 0
        for g in BUNDLES[z]:
            size = cfg.widths[g]
            part, at = total[:, at : at + size], at + size
            if g == SQKV:
                for i in range(3):
                    r.self_grads[i][...] = part[:, i * hw : (i + 1) * hw]
                    leave(leaving.self_grads[i])
                continue
            if g in (SO, CO):
                pad = jnp.zeros((ceil_to(rpd, 128) - rpd, hw), F32)
                r.grads[g][...] = jnp.concatenate([part, pad], axis=0).T[:, :rpd]
            else:
                r.grads[g][...] = part
            leave(leaving.grads[g])

    def early_peers(start):
        def step_of(step, carry):
            index = lax.rem(hi + step, n_hi)
            start(index, (index * 2 + parity, t))
            return carry

        lax.fori_loop(1, n_hi, step_of, 0)

    def early_right_copy(index, device, slot):
        return remote(
            r.early_right.at[hi], r.early_right.at[slot], r.er_ss.at[index], r.er_rs.at[slot], device
        )

    def early_left_copy(index, device, slot):
        return remote(
            r.early_sent.at[index, core],
            r.early_left.at[slot, core],
            r.el_ss.at[index],
            r.el_rs.at[slot],
            device,
        )

    def early_left_pass(index):
        ref = r.early_left.at[index, core]
        return remote(ref, ref, r.ef_ss.at[index], r.ef_rs.at[index], sibling)

    def early_left_exchange():
        def step_of(index, device):
            early_left_copy(index, device, index).wait()
            early_left_pass(index).start()

        early_peers(step_of)

    def early_left_open(left):
        for which in range(2):
            rows = nt(r.sel[which], left).astype(BF).reshape(2, n_top, pr, lat)
            for m in range(n_top):
                r.early_sent[2 * m + side, which] = rows[0, m]
                r.early_sent[2 * m + 1 - side, which] = rows[1, m]
        early_peers(lambda index, device: early_left_copy(index, device, hi).start())
        r.early_left[hi] = r.early_sent[hi]

    inner = (top + side) == 1
    other_inner = ((1 - top) * 4 + (1 - side) * 2 + parity, t)
    other_end = ((1 - top) * 4 + side * 2 + parity, t)

    def line_copy(i, slot, sent, device):
        return remote(
            sent, r.line_in[i].at[slot], r.li_ss.at[i, slot], r.li_rs.at[i, slot], device
        )

    def line_lefts():
        return [
            line_copy(0, 0, r.left_own[FI1], mid),
            line_copy(0, 1, r.left_sent[FI1], diag_mid),
        ]

    def line_right():
        return line_copy(1, 0, r.right_own[FI1], mid)

    def line_forward():
        return line_copy(1, 1, r.line_in[1].at[0], near)

    def line_open(copies):
        @pl.when(jnp.logical_not(inner))
        def _():
            for copy in copies():
                copy.start()

    def line_pass():
        @pl.when(inner)
        def _():
            line_right().wait_recv()
            line_forward().start()

    def line_out(i):
        device, slot = ((mid, 1), (other_inner, 0), (other_end, 0))[i]
        return remote(r.line_sent.at[i], r.line_got.at[slot], r.lo_ss.at[i], r.lo_rs.at[slot], device)

    def line_send():
        wait_all(near_copies[FI1])

        def block(ref, flank, index):
            return ref[pl.ds(pl.multiple_of((flank * n_top + index) * pr, 16), pr)]

        r.line_sum[...] = nn(r.left_own[FI1][...], r.right_own[FI1][...]) + nn(
            r.left_near[FI1][...], r.right_near[FI1][...]
        )

        @pl.when(inner)
        def _():
            for copy in line_lefts():
                copy.wait_recv()
            line_forward().wait()
            r.line_sent[0] = block(r.line_sum, 1, top).astype(BF)
            line_out(0).start()
            end_sum = nn(r.line_in[0][0], r.line_in[1][0]) + nn(r.line_in[0][1], r.line_in[1][1])
            half_rows = n_top * pr
            r.line_sum[:half_rows] += end_sum[half_rows:]
            r.line_sum[half_rows:] += end_sum[:half_rows]
            for i, flank in ((1, 1), (2, 0)):
                r.line_sent[i] = block(r.line_sum, flank, 1 - top).astype(BF)
                line_out(i).start()

        r.grads[FI1][...] = block(r.line_sum, 0, top)[:rpd]

    def line_close():
        @pl.when(inner)
        def _():
            for i in range(3):
                line_out(i).wait_send()

        @pl.when(jnp.logical_not(inner))
        def _():
            for copy in line_lefts() + [line_right()]:
                copy.wait_send()
            line_out(0).wait_recv()
            r.grads[FI1][...] += r.line_got[1, :rpd].astype(F32)

        line_out(1).wait_recv()
        r.grads[FI1][...] += r.line_got[0, :rpd].astype(F32)
        leave(leaving.grads[FI1])

    def early_copy():
        return remote(r.early_part, r.early_got, r.ep_ss.at[0], r.ep_rs.at[0], near)

    def early_product(which):
        def add(index, total):
            return total + nn(r.early_left[index, which], r.early_right[index])

        return lax.fori_loop(0, n_hi, add, jnp.zeros((pr, width), F32))

    def early_send():
        def wait(index, device):
            early_right_copy(index, device, index).wait()
            early_left_pass(index).wait()

        early_peers(wait)
        r.early_part[...] = early_product(1).astype(BF)
        early_copy().start()
        r.grads[FO1][...] = early_product(0)[:rpd]

    def early_close():
        early_copy().wait()
        r.grads[FO1][...] += r.early_got[:rpd].astype(F32)
        leave(leaving.grads[FO1])

    early = cfg.early

    def row_of(ref):
        return ref[...].reshape(1, width)

    r.sel[1] = selection(1 - parity)
    r.sel[0] = selection(parity)
    wait_all(quick)
    keep = r.keep[0].astype(F32)
    x0 = r.x0[...].astype(F32)
    unit0, _ = norm_parts(x0)
    query_in = (unit0 * row_of(r.cross_norm)).astype(BF)
    r.query_in[...] = query_in
    arrive("cq")
    query = nt(query_in, w.cq[...]).astype(BF).astype(F32) * HEAD_DIM ** (-0.5)
    r.qf[t] = query.astype(BF)
    r.q_wide[...] = spread(query).astype(BF)

    pl.semaphore_wait(barrier, 5 + n_hi - 1)

    wait_all(pair_copies)

    def pair_part(part, owner, k, peer):
        i, start, size = ((0, 0, hw), (1, 0, hw // 2), (1, hw // 2, hw // 2))[part]
        ref = r.wkv.at[owner, i, pl.ds(start, size)]
        return remote(ref, ref, r.wkv_ss.at[part, k], r.wkv_rs.at[part, k], peer)

    def pair_send(part):
        copies = [pair_part(part, t, 0, sibling), pair_part(part, t, 1, far)]
        for copy in copies:
            copy.start()
        return copies

    def pair_forward(part, copies):
        wait_all(copies)
        copy = pair_part(part, far_t, 2, sibling)
        copy.start()
        return copy

    key_sends = pair_send(0)

    for b in range(blocks):
        start = b * KEY_BLOCK
        size = min(cfg.patches - start, KEY_BLOCK)
        if size < KEY_BLOCK:
            lane = lax.broadcasted_iota(jnp.int32, (1, KEY_BLOCK), 1) + (start - cfg.patches)
            r.mask[b] = jnp.where((lane >= 0) & (lane < r.captions[0]), 1.0, 0.0)
        if size > 0:
            patch = r.patch_mask[:, start : start + size]
            r.mask[b, :, :size] = jnp.where(patch != 0, 1.0, 0.0)

    tail_row = lax.broadcasted_iota(jnp.int32, (TAIL, width), 0)
    tail = jnp.where(tail_row < cfg.keys - cfg.main_rows, r.tail[...].astype(F32), 0.0)
    r.source[cfg.main_rows :] = tail.astype(BF)

    @pl.when(t == 3)
    def _():
        r.own[own_main:] = tail.astype(BF)

    byte_gain = row_of(r.byte_norm)

    def block_rows(b):
        return pl.ds(pl.multiple_of(b * KEY_BLOCK, KEY_BLOCK), KEY_BLOCK)

    q_wide = r.q_wide[...]
    wait_all(byte_copies)
    for copy in others:
        copy.start()

    def lanes(values, combine):
        total = values[:, :128]
        for at in range(128, values.shape[1], 128):
            total = combine(total, values[:, at : at + 128])
        return total

    largest = jnp.full((stack, 1), -3.0e38, F32)
    r.stat[...] = jnp.zeros(r.stat.shape, F32)
    r.wide_acc[...] = jnp.zeros(r.wide_acc.shape, F32)
    tops = []
    for b in range(blocks):
        rows = pl.ds(b * KEY_BLOCK, KEY_BLOCK)
        unit, _ = norm_parts(r.source[rows].astype(F32))
        source = (unit * byte_gain).astype(BF)
        r.source[rows] = source
        key = nt(source, r.wkv[t, 0]).astype(BF)
        value = nt(source, r.wkv[t, 1]).astype(BF)
        r.key[rows] = key
        r.value[rows] = value
        scores = jnp.where(r.mask[b] > 0.0, nt(q_wide, key), -1000000000.0)
        top_score = jnp.max(lanes(scores, jnp.maximum), axis=1, keepdims=True)
        before, largest = largest, jnp.maximum(largest, top_score)
        tops.append(largest)
        powers = jnp.exp(scores - largest)
        shrink = jnp.exp(before - largest)
        soft = powers.astype(BF)
        r.power[b] = soft
        r.stat[...] = r.stat[...] * shrink + lanes(powers, jnp.add)
        r.wide_acc[...] = r.wide_acc[...] * shrink + nn(soft, value)
    summed = jnp.sum(r.stat[...], axis=1, keepdims=True)
    inverse = 1.0 / summed
    lane = lax.broadcasted_iota(jnp.int32, (stack, 128), 1)
    factors = jnp.zeros((stack, 128), F32)
    for b in range(blocks):
        factors = jnp.where(lane == b, inverse * jnp.exp(tops[b] - largest), factors)
    r.weight[...] = factors

    def weight_of(b):
        picked = lax.broadcasted_iota(jnp.int32, (stack, 128), 1) == b
        return jnp.sum(jnp.where(picked, r.weight[...], 0.0), axis=1, keepdims=True)

    cross_mix = gathered_heads(r.wide_acc[...] * inverse).astype(BF)
    r.right_own[CO][...] = cross_mix
    r.lse[t] = as_row(largest + jnp.log(summed))

    arrive("co")
    sum_open(0, nn(cross_mix, w.co[...]))
    sum_cross(0)
    near_right(CO)
    near_left(FO2, r.cot[...])

    r.deep_acc[...] = jnp.zeros(r.deep_acc.shape, F32)

    def blend(b, carry):
        r.deep_acc[...] += weight_of(b) * nn(r.power[b], r.source[block_rows(b)])
        return carry

    lax.fori_loop(0, blocks, blend, 0)
    r.blended[...] = r.deep_acc[...].astype(BF)
    sum_back(0)
    q_share = share(r.qf, 0)
    lse_share = share(r.lse, 1)
    after_cross = x0 + keep * sum_close(0)

    def ffn_open(a, values, gain, win, wout, out_group, n):
        unit, scale = norm_parts(values)
        r.unit[n][...] = unit
        r.scale[n][...] = scale
        normed = (unit * gain).astype(BF)
        r.normed[n][...] = normed
        if out_group == FO2:
            near_left_start(FI2, normed)
        arrive(win)
        active, slope = gelu_parts(nn(normed, r.held[win][...]))
        active = active.astype(BF)
        r.slope[n][...] = slope
        if out_group == FO1 and early:
            r.early_right[hi] = active
            early_peers(lambda index, device: early_right_copy(index, device, hi).start())
        else:
            r.right_own[out_group][...] = active
            near_right(out_group)
        arrive(wout)
        sum_open(a, nn(active, r.held[wout][...]))

    ffn_open(1, after_cross, row_of(r.ffn_norm1), "fi1", "fo1", FO1, 0)

    sum_cross(1)
    key_forward = pair_forward(0, key_sends)
    near_left(FI1, r.normed[0][...])
    if early:
        line_open(line_lefts)
    key_forward.wait()
    live_row = jnp.concatenate([r.mask[b] for b in range(blocks)], axis=1)
    live_row = jnp.broadcast_to(live_row, (8, key_rows))
    live_row = pltpu.roll(live_row, lax.rem(key_rows - window, key_rows), 1)
    r.own_live[...] = live_row[:, : ceil_to(own_rows, 128)].T[:own_rows]
    wait_all(q_share)
    wait_all(lse_share)

    def own_powers(s, carry):
        key = nt(r.source[pl.ds(window, own_rows)], r.wkv[s, 0]).astype(BF)
        scores = nt(key, spread(r.qf[s]).astype(BF))
        live = jnp.broadcast_to(r.own_live[:, :1], (own_rows, stack))
        r.own_power[s] = (jnp.exp(jnp.minimum(scores - r.lse[s, 0:1], 0.0)) * live).astype(BF)
        return carry

    lax.fori_loop(0, 2, own_powers, 0)
    sum_back(1)
    value_sends = [pair_send(1)]
    after_ffn1 = after_cross + sum_close(1)

    unit_s, scale_s = norm_parts(after_ffn1)
    r.unit[1][...] = unit_s
    r.scale[1][...] = scale_s
    inner_in = (unit_s * row_of(r.self_norm)).astype(BF)
    r.normed[1][...] = inner_in
    arrive("sq", "sk", "sv", "so")
    factor = HEAD_DIM ** (-0.5)
    self_q = nt(inner_in, w.sq[...]).astype(BF).astype(F32) * factor
    self_k = nt(inner_in, w.sk[...]).astype(BF)
    self_v = nt(inner_in, w.sv[...]).astype(BF)
    self_q_wide = spread(self_q).astype(BF)
    self_scores = nt(self_k, self_q_wide)
    self_powers = jnp.exp(self_scores - jnp.max(self_scores, axis=0, keepdims=True))
    self_soft = self_powers / jnp.sum(self_powers, axis=0, keepdims=True)
    self_mix = gathered_heads(tn(self_soft.astype(BF), self_v)).astype(BF)
    r.self_q_wide[...] = self_q_wide
    r.self_k[...] = self_k
    r.self_v[...] = self_v
    r.self_soft[...] = self_soft
    sum_open(2, nn(self_mix, w.so[...]))
    r.right_own[SO][...] = self_mix
    near_right(SO)
    sum_cross(2)
    near_left(SQKV, inner_in)
    near_left(CQ, r.query_in[...])

    lax.fori_loop(2, 4, own_powers, 0)
    sum_back(2)
    value_sends.append(pair_send(2))
    after_self = after_ffn1 + sum_close(2)

    ffn_open(3, after_self, row_of(r.ffn_norm2), "fi2", "fo2", FO2, 2)
    cotangent = r.cot[...]

    def ffn_back(a, win, wout, in_group, n, branch):
        grad_hidden = (nt(branch, wout[...]) * r.slope[n][...]).astype(BF)
        r.right_own[in_group][...] = grad_hidden
        sum_open(a, nt(grad_hidden, win[...]))

    ffn_back(4, w.fi2, w.fo2, FI2, 2, cotangent)
    near_right(FI2)
    r.left_own[FI2][...] = nt(r.sel[0], r.normed[2][...]).astype(BF)
    sum_cross(4)
    mid_send_half(0)
    mid_send_half(1)
    sum_back(4)
    sum_cross(3)
    dnormed = sum_close(4)
    r.vec[...] = jnp.zeros(r.vec.shape, F32)
    r.vec[3:4] = jnp.sum(dnormed * r.unit[2][...], axis=0, keepdims=True)
    grad_after_self = cotangent.astype(F32) + norm_back(
        r.unit[2][...], r.scale[2][...], row_of(r.ffn_norm2), dnormed
    )

    self_branch = grad_after_self.astype(BF)
    self_do = spread(nt(self_branch, w.so[...]).astype(BF)).astype(BF)
    self_soft = r.self_soft[...]
    grad_soft = nt(r.self_v[...], self_do)
    inner_sum = jnp.sum(self_soft * grad_soft, axis=0, keepdims=True)
    self_ds = (self_soft * (grad_soft - inner_sum)).astype(BF)
    self_dk = nn(self_ds, r.self_q_wide[...]).astype(BF)
    self_dv = nn(self_soft.astype(BF), self_do).astype(BF)
    self_dq = (gathered_heads(tn(self_ds, r.self_k[...])) * factor).astype(BF)
    sum_open(5, nn(self_dq, w.sq[...]) + nn(self_dk, w.sk[...]) + nn(self_dv, w.sv[...]))
    r.right_own[SQKV][...] = jnp.concatenate([self_dq, self_dk, self_dv], axis=1)
    near_right(SQKV)
    near_left(SO, self_branch)
    sum_cross(5)
    sum_back(3)
    mid_send(Z_FI2)
    sum_back(5)
    top_send(Z_FO2)
    dnormed = sum_close(5)
    r.vec[2:3] = jnp.sum(dnormed * r.unit[1][...], axis=0, keepdims=True)
    grad_after_ffn1 = grad_after_self + norm_back(
        r.unit[1][...], r.scale[1][...], row_of(r.self_norm), dnormed
    )

    branch1 = grad_after_ffn1.astype(BF)
    ffn_back(6, w.fi1, w.fo1, FI1, 0, branch1)
    near_right(FI1)
    if early:
        line_open(lambda: [line_right()])
    early_left_open(branch1) if early else near_left(FO1, branch1)
    sum_cross(6)
    r.new_latents[...] = (after_self + sum_close(3)).astype(BF)
    leave(leaving.new_latents)
    mid_send(Z_SELF)
    value_forwards = [pair_forward(1 + i, copies) for i, copies in enumerate(value_sends)]
    wait_all(value_forwards)

    def own_values(s, carry):
        r.own_value[s] = nt(r.source[pl.ds(window, own_rows)], r.wkv[s, 1]).astype(BF)
        return carry

    lax.fori_loop(0, 4, own_values, 0)
    sum_back(6)
    dnormed = sum_close(6)
    r.vec[1:2] = jnp.sum(dnormed * r.unit[0][...], axis=0, keepdims=True)
    grad_after_cross = grad_after_ffn1 + norm_back(
        r.unit[0][...], r.scale[0][...], row_of(r.ffn_norm1), dnormed
    )

    cross_branch = (keep * grad_after_cross).astype(BF)
    dmix = nt(cross_branch, w.co[...]).astype(BF)
    r.dof[t] = dmix
    do_share = share(r.dof, 2)
    do_wide_f32 = spread(dmix)
    do_wide = do_wide_f32.astype(BF)
    mix3 = jnp.concatenate([r.right_own[CO][...].astype(F32)] * heads, axis=0)
    delta = jnp.sum(do_wide_f32 * mix3, axis=1, keepdims=True)
    r.delta[t] = as_row(delta)
    delta_share = share(r.delta, 3)
    near_left(CO, cross_branch)
    if not early:
        mid_send(Z_FI1)

    def pair_open(g, left, right):
        i = g - CV
        sent = nn(nt(r.sel[1], left).astype(BF), right)
        r.pair_s[i] = jnp.concatenate([sent[:rows_half], sent[rows_half:]], axis=1).astype(BF)
        copy = remote(r.pair_s.at[i], r.pair_r.at[i], r.pair_ss.at[i], r.pair_rs.at[i], near)
        copy.start()
        near_copies[g].append(copy)
        r.pair_own[i] = nn(nt(r.sel[0], left).astype(BF), right)

    blended = r.blended[...]
    pair_open(CV, blended, do_wide)
    r.deep_acc[...] = jnp.zeros(r.deep_acc.shape, F32)
    r.wide_acc[...] = jnp.zeros(r.wide_acc.shape, F32)

    def back(b, carry):
        rows = block_rows(b)
        grad_power = nt(do_wide, r.value[rows])
        ds = (r.power[b].astype(F32) * (weight_of(b) * (grad_power - delta))).astype(BF)
        r.wide_acc[...] += nn(ds, r.key[rows])
        r.deep_acc[...] += nn(ds, r.source[rows])
        return carry

    def back_and_send(b, carry):
        back(b, carry)

        @pl.when(b == 0)
        def _():
            if early:
                line_pass()

        @pl.when(b == min(1, blocks - 1))
        def _():
            top_send(Z_FI2)

        @pl.when(b == max(0, blocks - 2))
        def _():
            mid_send(Z_VALUE)

        return carry

    lax.fori_loop(0, blocks, back_and_send, 0)
    if early:
        early_left_exchange()
    cross_dq = (gathered_heads(r.wide_acc[...]) * factor).astype(BF)
    sum_open(7, nn(cross_dq, w.cq[...]))
    q_wide = r.q_wide[...]
    deep = r.deep_acc[...]
    deep_low = deep.astype(BF)
    pair_open(CK, deep_low, q_wide)
    r.right_own[CQ][...] = cross_dq
    near_right(CQ)
    sum_cross(7)
    if early:
        line_send()
    gain_row = (
        jnp.sum(deep * nn(q_wide, r.wkv[t, 0]), axis=0, keepdims=True)
        + jnp.sum(blended.astype(F32) * nn(do_wide, r.wkv[t, 1]), axis=0, keepdims=True)
    ) / byte_gain
    r.gain[t] = jnp.concatenate([gain_row, jnp.zeros((7, width), F32)], axis=0)
    gain_share = share(r.gain, 4)
    wait_all(do_share)
    wait_all(delta_share)
    r.own_acc[...] = jnp.zeros(r.own_acc.shape, F32)

    def own_back(s, carry):
        do_here = spread(r.dof[s]).astype(BF)
        q_here = spread(r.qf[s]).astype(BF)
        soft = r.own_power[s]
        grad_power = nt(r.own_value[s], do_here)
        ds = (soft.astype(F32) * (grad_power - r.delta[s, 0:1])).astype(BF)
        dk = nn(ds, q_here).astype(BF)
        dv = nn(soft, do_here).astype(BF)
        r.own_acc[...] += nn(dk, r.wkv[s, 0]) + nn(dv, r.wkv[s, 1])
        return carry


    def own_back_and_send(s, carry):
        own_back(s, carry)

        @pl.when(s == 0)
        def _():
            top_send(Z_SELF)

        @pl.when(s == 1)
        def _():
            sum_back(7)
            mid_send(Z_KEY)

        @pl.when(s == 2)
        def _():
            if not early:
                top_send(Z_FI1)
            top_send(Z_VALUE)

        return carry

    lax.fori_loop(0, 4, own_back_and_send, 0)
    dnormed = sum_close(7)
    unit0, scale0 = norm_parts(r.x0[...].astype(F32))
    r.vec[0:1] = jnp.sum(dnormed * unit0, axis=0, keepdims=True)
    r.latent_grads[...] = (
        grad_after_cross + norm_back(unit0, scale0, row_of(r.cross_norm), dnormed)
    ).astype(BF)
    leave(leaving.latent_grads)
    wait_all(gain_share)
    r.vec[4:5] = r.gain[0, 0:1] + r.gain[1, 0:1] + r.gain[2, 0:1] + r.gain[3, 0:1]
    live_count = jnp.sum(jnp.sum(r.mask[...], axis=0), axis=1, keepdims=True)
    lane = lax.broadcasted_iota(jnp.int32, (1, width), 1)
    r.vec[5:6] = keep * jnp.where(lane == 0, live_count, jnp.where(lane == 1, float(lat), 0.0))
    vec_copy = remote(r.vec, r.vec_r, r.vec_ss.at[0], r.vec_rs.at[0], near)
    vec_copy.start()
    if early:
        early_send()
    else:
        mid_send(Z_FO1)
    top_send(Z_KEY)
    vec_copy.wait()
    r.vec[...] += r.vec_r[...]
    vec_copy = remote(r.vec, r.vec_m, r.vec_ss.at[1], r.vec_rs.at[1], mid)
    vec_copy.start()
    def own_norm_back(c, carry):
        rows = pl.ds(pl.multiple_of(c * OWN_CHUNK, OWN_CHUNK), OWN_CHUNK)
        unit, scale = norm_parts(r.own[rows].astype(F32))
        r.own_acc[rows] = norm_back(unit, scale, byte_gain, r.own_acc[rows])
        return carry

    own_copies[0].wait()

    @pl.when(t < 3)
    def _():
        own_copies[1].wait()

    lax.fori_loop(0, own_rows // OWN_CHUNK, own_norm_back, 0)
    vec_copy.wait()
    r.vec_all[top] = r.vec[...] + r.vec_m[...]

    def vec_top(step, source_index):
        index, device = top_peer(step)
        return remote(
            r.vec_all.at[top],
            r.vec_all.at[source_index],
            r.vh_ss.at[index],
            r.vh_rs.at[source_index],
            device,
        )

    def vec_send(step, carry):
        vec_top(step, top).start()
        return carry

    lax.fori_loop(1, n_top, vec_send, 0)
    for k in range(4):

        @pl.when(t == k)
        def _(skip=k * cfg.share % 16):
            r.byte_grads[...] = r.own_acc[skip : skip + cfg.share].astype(BF)

    leave(leaving.byte_grads)
    for z in (Z_FO2, Z_FI2, Z_SELF):
        top_close(z)
    if early:
        early_close()
        line_close()
    else:
        top_send(Z_FO1)
        top_close(Z_FI1)
        top_close(Z_FO1)
    for z in (Z_VALUE, Z_KEY):
        top_close(z)

    def vec_close(step, carry):
        vec_top(step, top_peer(step)[0]).wait()
        return carry

    lax.fori_loop(1, n_top, vec_close, 0)
    vec = lax.fori_loop(1, n_top, lambda i, total: total + r.vec_all[i], r.vec_all[0])
    mine = pltpu.roll(vec, lax.rem(width - dp * rpd, width), 1)
    for i in range(4):
        r.gain_grads[i][...] = mine[i : i + 1, :rpd].reshape(rpd)
        leave(leaving.gain_grads[i])
    r.byte_gain_grad[...] = vec[4:5].reshape(width)
    leave(leaving.byte_gain_grad)
    r.counts[...] = vec[5:6, :2].reshape(2)
    leave(leaving.counts)
    wait_all(left)


def finish(count, *refs):
    sources, targets, held = (refs[i * count : (i + 1) * count] for i in range(3))
    in_sems, out_sems = refs[3 * count :]
    arrivals = [
        pltpu.make_async_copy(src, via, in_sems.at[i])
        for i, (src, via) in enumerate(zip(sources, held))
    ]
    departures = [
        pltpu.make_async_copy(via, dst, out_sems.at[i])
        for i, (via, dst) in enumerate(zip(held, targets))
    ]
    for copy in arrivals:
        copy.start()
    for arrival, departure in zip(arrivals, departures):
        arrival.wait()
        departure.start()
    for copy in departures:
        copy.wait()


def ceil_to(value, step):
    return -(-value // step) * step


def on_device(
    n_dp,
    latents,
    byte_array,
    caption_lengths,
    patch_mask,
    cross_keep,
    cross_norm,
    byte_norm,
    cross_query,
    cross_key,
    cross_value,
    cross_output,
    ffn_norm1,
    ffn_in1,
    ffn_out1,
    self_norm,
    self_query,
    self_key,
    self_value,
    self_output,
    ffn_norm2,
    ffn_in2,
    ffn_out2,
    cotangent,
):
    _, lat, width = latents.shape
    keys = byte_array.shape[1]
    patches = patch_mask.shape[1]
    hw = cross_query.shape[1]
    ff = ffn_in1.shape[1]
    heads = hw // HEAD_DIM
    share = keys // 4
    key_rows = ceil_to(keys, KEY_BLOCK)
    main_rows = keys // TAIL * TAIL
    own_rows = ceil_to(share + 15, OWN_CHUNK)
    blocks = key_rows // KEY_BLOCK
    n_hi = n_dp // 2
    n_top = n_hi // 2
    rpd = width // n_dp
    pr = ceil_to(rpd, 16)
    rt = n_hi * pr
    byte_parts = [
        (start, min(KEY_BLOCK, main_rows - start)) for start in range(0, main_rows, KEY_BLOCK)
    ]
    assert main_rows + TAIL == key_rows and len(byte_parts) == blocks
    assert 3 * share // 16 * 16 + own_rows == key_rows

    hbm = pl.BlockSpec(memory_space=pl.ANY)
    smem = pl.BlockSpec(memory_space=pltpu.SMEM)
    values = dict(
        keep=cross_keep,
        captions=caption_lengths,
        bytes=byte_array[0],
        tail=byte_array[0],
        quick=dict(
            x0=latents[0],
            cross_norm=cross_norm,
            patch_mask=patch_mask,
            byte_norm=byte_norm,
            ffn_norm1=ffn_norm1,
            self_norm=self_norm,
            ffn_norm2=ffn_norm2,
            cot=cotangent[0],
        ),
        cross_key=cross_key.T,
        cross_value=cross_value.T,
        weights=dict(
            cq=cross_query.T,
            co=cross_output,
            fi1=ffn_in1,
            fo1=ffn_out1,
            sq=self_query.T,
            sk=self_key.T,
            sv=self_value.T,
            so=self_output,
            fi2=ffn_in2,
            fo2=ffn_out2,
        ),
    )
    specs = {}
    specs.update(
        keep=smem,
        captions=smem,
        bytes=hbm,
        tail=pl.BlockSpec(
            (TAIL, width), lambda i: (main_rows // TAIL, 0), pipeline_mode=pl.Buffered(1)
        ),
        cross_key=hbm,
        cross_value=hbm,
        quick={name: hbm for name in values["quick"]},
        weights={name: hbm for name in values["weights"]},
    )
    widths = (ff, ff, 3 * hw, hw, ff, ff, hw, hw, hw, hw)
    early = n_hi == 4
    bundles = [
        128 if early and bundle in ((FI1,), (FO1,)) else sum(widths[g] for g in bundle)
        for bundle in BUNDLES
    ]

    def out(shape, kind):
        return jax.ShapeDtypeStruct(shape, kind)

    outputs = dict(
        new_latents=out((lat, width), BF),
        latent_grads=out((lat, width), BF),
        byte_grads=out((share, width), BF),
        gain_grads=[out((rpd,), F32) for _ in range(4)],
        byte_gain_grad=out((width,), F32),
        counts=out((2,), F32),
        self_grads=[out((rpd, hw), F32) for _ in range(3)],
        grads={
            FO2: out((rpd, ff), F32),
            FI2: out((rpd, ff), F32),
            SO: out((hw, rpd), F32),
            FO1: out((rpd, ff), F32),
            FI1: out((rpd, ff), F32),
            CO: out((hw, rpd), F32),
            CQ: out((rpd, hw), F32),
            CV: out((rpd, hw), F32),
            CK: out((rpd, hw), F32),
        },
    )

    def buf(*shape):
        return pltpu.VMEM(shape, BF)

    def wide(*shape):
        return pltpu.VMEM(shape, F32)

    def sems(*shape):
        return pltpu.SemaphoreType.DMA(shape)

    stack = heads * lat
    left_rows = [16 if early and g == FO1 else rt for g in range(CV)]
    right_columns = [128 if early and g == FO1 else widths[g] for g in range(CV)]
    scratch = dict(
        placed={name: pltpu.VMEM(a.shape, a.dtype) for name, a in values["quick"].items()},
        quick_sem=sems(len(values["quick"])),
        made=jax.tree.map(lambda a: pltpu.VMEM(a.shape, a.dtype), outputs),
        out_sem=sems(len(jax.tree.leaves(outputs))),
        held={name: buf(*value.shape) for name, value in values["weights"].items()},
        wkv=buf(4, 2, hw, width),
        source=buf(key_rows, width),
        key=buf(key_rows, hw),
        value=buf(key_rows, hw),
        power=buf(blocks, stack, KEY_BLOCK),
        stat=wide(stack, 128),
        mask=wide(blocks, 1, KEY_BLOCK),
        weight=wide(stack, 128),
        wide_acc=wide(stack, hw),
        deep_acc=wide(stack, width),
        blended=buf(stack, width),
        q_wide=buf(stack, hw),
        query_in=buf(lat, width),
        qf=buf(4, lat, hw),
        dof=buf(4, lat, hw),
        lse=wide(4, 8, stack),
        delta=wide(4, 8, stack),
        gain=wide(4, 8, width),
        own=buf(own_rows, width),
        own_value=buf(4, own_rows, hw),
        own_power=buf(4, own_rows, stack),
        own_live=wide(own_rows, 8),
        own_acc=wide(own_rows, width),
        unit=[wide(lat, width) for _ in range(3)],
        scale=[wide(lat, 1) for _ in range(3)],
        normed=[buf(lat, width) for _ in range(3)],
        slope=[wide(lat, ff), wide(8, 128), wide(lat, ff)],
        self_q_wide=buf(stack, hw),
        self_k=buf(lat, hw),
        self_v=buf(lat, hw),
        self_soft=wide(lat, stack),
        sel=buf(2, rt, width),
        ar_s=buf(SETS, 2, lat // 2, width),
        ar_r1=buf(SETS, lat // 2, width),
        ar_r2=buf(SETS, lat // 2, width),
        ar_t=buf(SETS, 2, lat // 2, width),
        pair_own=wide(2, rt, hw),
        pair_s=buf(2, rt // 2, 2 * hw),
        pair_r=buf(2, rt // 2, 2 * hw),
        vec=wide(8, width),
        vec_r=wide(8, width),
        vec_m=wide(8, width),
        vec_all=wide(n_top, 8, width),
        left_own=[buf(rows, lat) for rows in left_rows],
        left_sent=[buf(rows, lat) for rows in left_rows],
        left_near=[buf(rows, lat) for rows in left_rows],
        right_own=[buf(lat, size) for size in right_columns],
        right_near=[buf(lat, size) for size in right_columns],
        mid_sent=[buf(rt // 2, size) for size in bundles],
        mid_got=[buf(rt // 2, size) for size in bundles],
        block_sent=[buf(n_top, pr, size) for size in bundles],
        block_got=[buf(n_top, pr, size) for size in bundles],
        byte_sem=sems(len(byte_parts)),
        own_sem=sems(2),
        w_sem=sems(len(values["weights"])),
        pair_sem=sems(2),
        share_ss=sems(5, 3),
        share_rs=sems(5, 3),
        wkv_ss=sems(3, 3),
        wkv_rs=sems(3, 3),
        ar_ss=sems(8, 3),
        ar_rs=sems(8, 3),
        x_ss=sems(CV, 3),
        x_rs=sems(CV, 3),
        mh_ss=sems(2),
        mh_rs=sems(2),
        m_ss=sems(len(BUNDLES)),
        m_rs=sems(len(BUNDLES)),
        z_ss=sems(len(BUNDLES), n_top),
        z_rs=sems(len(BUNDLES), n_top),
        early_right=buf(*((n_hi, lat, ff) if early else (16, 128))),
        early_sent=buf(*((n_hi, 2, pr, lat) if early else (16, 128))),
        early_left=buf(*((n_hi, 2, pr, lat) if early else (16, 128))),
        early_part=buf(pr, ff),
        early_got=buf(pr, ff),
        er_ss=sems(n_hi),
        er_rs=sems(n_hi),
        el_ss=sems(n_hi),
        el_rs=sems(n_hi),
        line_in=[buf(2, *shape) for shape in ((rt, lat), (lat, ff))] if early else [],
        line_sum=wide(*((rt, ff) if early else (16, 128))),
        line_sent=buf(*((3, pr, ff) if early else (16, 128))),
        line_got=buf(*((2, pr, ff) if early else (16, 128))),
        li_ss=sems(2, 2),
        li_rs=sems(2, 2),
        lo_ss=sems(3),
        lo_rs=sems(2),
        ef_ss=sems(n_hi),
        ef_rs=sems(n_hi),
        ep_ss=sems(1),
        ep_rs=sems(1),
        pair_ss=sems(2),
        pair_rs=sems(2),
        vec_ss=sems(2),
        vec_rs=sems(2),
        vh_ss=sems(n_top),
        vh_rs=sems(n_top),
    )
    tables = (values, dict(outs=outputs), scratch)

    def leaf(node):
        return not isinstance(node, (dict, list))

    flat = [jax.tree.flatten(table, is_leaf=leaf) for table in tables]
    trees = [tree for _, tree in flat]
    counts = [len(leaves) for leaves, _ in flat]
    cfg = SimpleNamespace(
        trees=trees,
        counts=counts,
        lat=lat,
        width=width,
        hw=hw,
        heads=heads,
        n_hi=n_hi,
        pr=pr,
        rpd=rpd,
        blocks=blocks,
        key_rows=key_rows,
        main_rows=main_rows,
        own_rows=own_rows,
        byte_parts=byte_parts,
        patches=patches,
        keys=keys,
        share=share,
        widths=widths,
        early=early,
        out_order=jax.tree.unflatten(jax.tree.structure(outputs), range(counts[1])),
    )
    results = pl.pallas_call(
        functools.partial(kernel, cfg),
        out_shape=flat[1][0],
        grid=(1,),
        in_specs=jax.tree.leaves(specs, is_leaf=leaf),
        out_specs=[hbm] * counts[1],
        scratch_shapes=flat[2][0],
        compiler_params=pltpu.CompilerParams(
            collective_id=0, has_side_effects=True, vmem_limit_bytes=64 * 2**20
        ),
        name="layers",
    )(*flat[0][0])
    results = pl.pallas_call(
        functools.partial(finish, counts[1]),
        out_shape=flat[1][0],
        in_specs=[hbm] * counts[1],
        out_specs=[hbm] * counts[1],
        scratch_shapes=[pltpu.VMEM(array.shape, array.dtype) for array in flat[1][0]]
        + [sems(counts[1])] * 2,
        name="results",
    )(*results)
    out = SimpleNamespace(**jax.tree.unflatten(trees[1], results)["outs"])
    grads = out.grads
    return (
        out.new_latents[None],
        out.latent_grads[None],
        out.byte_grads[None],
        out.gain_grads[0],
        out.byte_gain_grad,
        grads[CQ],
        grads[CK],
        grads[CV],
        grads[CO],
        out.gain_grads[1],
        grads[FI1],
        grads[FO1].T,
        out.gain_grads[2],
        out.self_grads[0],
        out.self_grads[1],
        out.self_grads[2],
        grads[SO],
        out.gain_grads[3],
        grads[FI2],
        grads[FO2].T,
        out.counts,
    )


def solution(mesh):
    in_specs = (
        P("dp", None, None),
        P("dp", None, None),
        P("dp"),
        P("dp", None),
        P("dp"),
        P(),
        P(),
        P(None, "tensor"),
        P(None, "tensor"),
        P(None, "tensor"),
        P("tensor", None),
        P(),
        P(None, "tensor"),
        P("tensor", None),
        P(),
        P(None, "tensor"),
        P(None, "tensor"),
        P(None, "tensor"),
        P("tensor", None),
        P(),
        P(None, "tensor"),
        P("tensor", None),
        P("dp", None, None),
    )
    out_specs = (
        P("dp", None, None),
        P("dp", None, None),
        P("dp", "tensor", None),
        P("dp"),
        P(),
        P("dp", "tensor"),
        P("dp", "tensor"),
        P("dp", "tensor"),
        P("tensor", "dp"),
        P("dp"),
        P("dp", "tensor"),
        P("tensor", "dp"),
        P("dp"),
        P("dp", "tensor"),
        P("dp", "tensor"),
        P("dp", "tensor"),
        P("tensor", "dp"),
        P("dp"),
        P("dp", "tensor"),
        P("tensor", "dp"),
        P(),
    )
    return jax.shard_map(
        functools.partial(on_device, mesh.shape["dp"]),
        mesh=mesh,
        in_specs=in_specs,
        out_specs=out_specs,
        check_vma=False,
    )
```

```python
import functools
import math
from types import SimpleNamespace

import jax
import jax.numpy as jnp
from jax import lax
from jax.experimental import pallas as pl
from jax.experimental.pallas import tpu as pltpu
from jax.sharding import PartitionSpec as P

HEAD_DIM = 64
EPSILON = 1e-05
GELU_A = 0.7978845608
GELU_B = 0.044715
KEY_BLOCK = 640
TAIL = 64
SETS = 4
OWN_CHUNK = 272
MESH = pl.DeviceIdType.MESH
BF = jnp.bfloat16
F32 = jnp.float32

FO2, FI2, SQKV, SO, FO1, FI1, CO, CQ, CV, CK = range(10)
BUNDLES = ((FO2,), (FI2,), (SQKV, SO), (CO, CV), (CQ, CK), (FI1,), (FO1,))
Z_FO2, Z_FI2, Z_SELF, Z_VALUE, Z_KEY, Z_FI1, Z_FO1 = range(7)


def nn(left, right):
    return lax.dot_general(left, right, (((1,), (0,)), ((), ())), preferred_element_type=F32)


def nt(left, right):
    return lax.dot_general(left, right, (((1,), (1,)), ((), ())), preferred_element_type=F32)


def tn(left, right):
    return lax.dot_general(left, right, (((0,), (0,)), ((), ())), preferred_element_type=F32)


def mean_of(values):
    return jnp.mean(values, axis=-1, keepdims=True)


def norm_parts(values):
    centered = values - mean_of(values)
    scale = lax.rsqrt(mean_of(centered * centered) + EPSILON)
    return centered * scale, scale


def norm_back(unit, scale, gain, grad):
    inner = grad * gain
    return scale * (inner - mean_of(inner) - unit * mean_of(inner * unit))


def gelu_parts(hidden):
    squared = hidden * hidden
    bent = jnp.tanh(GELU_A * hidden * (1.0 + GELU_B * squared))
    half = 0.5 * (1.0 + bent)
    slope = half + 0.5 * hidden * (1.0 - bent * bent) * (GELU_A * (1.0 + 3.0 * GELU_B * squared))
    return hidden * half, slope


def kernel(cfg, *refs):
    r = SimpleNamespace()
    at = 0
    for tree, count in zip(cfg.trees, cfg.counts):
        vars(r).update(jax.tree.unflatten(tree, refs[at : at + count]))
        at += count
    lat, width, hw, heads = cfg.lat, cfg.width, cfg.hw, cfg.heads
    n_hi, pr, rpd, blocks = cfg.n_hi, cfg.pr, cfg.rpd, cfg.blocks
    key_rows, own_rows = cfg.key_rows, cfg.own_rows
    half, stack = lat // 2, heads * lat
    dp, t = lax.axis_index("dp"), lax.axis_index("tensor")
    parity, hi, core = lax.rem(dp, 2), lax.div(dp, 2), lax.rem(t, 2)
    sib_t, far_t, diag_t = t + 1 - 2 * core, lax.rem(t + 2, 4), 3 - t
    sibling, far, diagonal = (dp, sib_t), (dp, far_t), (dp, diag_t)
    near = (dp + 1 - 2 * parity, t)
    side, top = lax.rem(hi, 2), lax.div(hi, 2)
    mid = (dp + 2 - 4 * side, t)
    trio = (sibling, far, diagonal)
    n_top = n_hi // 2

    def top_peer(step):
        index = lax.rem(top + step, n_top)
        return index, (index * 4 + side * 2 + parity, t)

    def remote(src, dst, sends, receives, device):
        return pltpu.make_async_remote_copy(
            src_ref=src,
            dst_ref=dst,
            send_sem=sends,
            recv_sem=receives,
            device_id=device,
            device_id_type=MESH,
        )

    byte_copies = [
        pltpu.make_async_copy(
            r.bytes.at[pl.ds(start, size)], r.source.at[pl.ds(start, size)], r.byte_sem.at[i]
        )
        for i, (start, size) in enumerate(cfg.byte_parts)
    ]
    weight_copies = {
        name: pltpu.make_async_copy(ref, r.held[name], r.w_sem.at[i])
        for i, (name, ref) in enumerate(r.weights.items())
    }
    w = SimpleNamespace(**r.held)

    def arrive(*names):
        for name in names:
            weight_copies[name].wait()

    pair_copies = [
        pltpu.make_async_copy(ref, r.wkv.at[t, i], r.pair_sem.at[i])
        for i, ref in enumerate((r.cross_key, r.cross_value))
    ]
    first = weight_copies["cq"]
    others = [
        weight_copies[name]
        for name in ("co", "fi1", "fo1", "sq", "sk", "sv", "so", "fi2", "fo2")
    ]
    quick = [
        pltpu.make_async_copy(ref, r.placed[name], r.quick_sem.at[i])
        for i, (name, ref) in enumerate(r.quick.items())
    ]
    vars(r).update(r.placed)
    share_at = t * cfg.share
    window = pl.multiple_of(lax.div(share_at, 16) * 16, 16)
    own_main = own_rows - TAIL
    own_copies = [
        pltpu.make_async_copy(
            r.bytes.at[pl.ds(pl.multiple_of(window + at, 16), size)],
            r.own.at[pl.ds(at, size)],
            r.own_sem.at[i],
        )
        for i, (at, size) in enumerate(((0, own_main), (own_main, TAIL)))
    ]
    for copy in quick + [first] + pair_copies + byte_copies + own_copies[:1]:
        copy.start()

    @pl.when(t < 3)
    def _():
        own_copies[1].start()

    leaving = SimpleNamespace(
        **jax.tree.map(
            lambda made, out, i: pltpu.make_async_copy(made, out, r.out_sem.at[i]),
            r.made,
            r.outs,
            cfg.out_order,
        )
    )
    left = []

    def leave(copy):
        copy.start()
        left.append(copy)

    vars(r).update(r.made)

    barrier = pltpu.get_barrier_semaphore()
    diag_mid = (dp + 2 - 4 * side + 1 - 2 * parity, t)
    for device in trio + (near, diag_mid):
        pl.semaphore_signal(barrier, inc=1, device_id=device, device_id_type=MESH)

    def greet(step, carry):
        device = (lax.rem(hi + step, n_hi) * 2 + parity, t)
        pl.semaphore_signal(barrier, inc=1, device_id=device, device_id_type=MESH)
        return carry

    lax.fori_loop(1, n_hi, greet, 0)

    columns = lax.broadcasted_iota(jnp.int32, (lat, hw), 1)
    head_mask = [
        (columns >= h * HEAD_DIM) & (columns < (h + 1) * HEAD_DIM) for h in range(heads)
    ]

    def spread(values):
        wide = values.astype(F32)
        return jnp.concatenate([jnp.where(m, wide, 0.0) for m in head_mask], axis=0)

    def gathered_heads(values):
        total = jnp.where(head_mask[0], values[:lat], 0.0)
        for h in range(1, heads):
            total = total + jnp.where(head_mask[h], values[h * lat : (h + 1) * lat], 0.0)
        return total

    def as_row(column):
        return jnp.broadcast_to(column, (column.shape[0], 128)).T[:8]

    def share(buffer, index):
        copies = [
            remote(
                buffer.at[t], buffer.at[t], r.share_ss.at[index, k], r.share_rs.at[index, k], peer
            )
            for k, peer in enumerate(trio)
        ]
        for copy in copies:
            copy.start()
        return copies

    def wait_all(copies):
        for copy in copies:
            copy.wait()

    hops = {}

    def sum_open(a, part):
        r.ar_s[a % SETS] = part.astype(BF).reshape(2, half, width)
        hops[a] = remote(
            r.ar_s.at[a % SETS, 1 - core], r.ar_r1.at[a % SETS], r.ar_ss.at[a, 0], r.ar_rs.at[a, 0], sibling
        )
        hops[a].start()

    def sum_cross(a):
        hops[a].wait()
        pair = r.ar_s[a % SETS, core].astype(F32) + r.ar_r1[a % SETS].astype(F32)
        r.ar_t[a % SETS, core] = pair.astype(BF)
        hops[a] = remote(
            r.ar_t.at[a % SETS, core], r.ar_r2.at[a % SETS], r.ar_ss.at[a, 1], r.ar_rs.at[a, 1], far
        )
        hops[a].start()

    def back_copy(a):
        half_total = r.ar_t.at[a % SETS, core]
        return remote(half_total, half_total, r.ar_ss.at[a, 2], r.ar_rs.at[a, 2], sibling)

    def sum_back(a):
        hops[a].wait()
        total = r.ar_t[a % SETS, core].astype(F32) + r.ar_r2[a % SETS].astype(F32)
        r.ar_t[a % SETS, core] = total.astype(BF)
        back_copy(a).start()

    def sum_close(a):
        back_copy(a).wait()
        return r.ar_t[a % SETS].reshape(lat, width).astype(F32)

    def selection(which):
        shape = (n_top, pr, width)
        block = lax.broadcasted_iota(jnp.int32, shape, 0)
        row = lax.broadcasted_iota(jnp.int32, shape, 1)
        feature = lax.broadcasted_iota(jnp.int32, shape, 2)
        parts = []
        for flank in (side, 1 - side):
            hit = (feature == (block * 4 + flank * 2 + which) * rpd + row) & (row < rpd)
            parts.append(jnp.where(hit, 1.0, 0.0).astype(BF).reshape(n_top * pr, width))
        return jnp.concatenate(parts, axis=0)

    near_copies = {g: [] for g in range(CK + 1)}

    def near_start(g, i, sent, got):
        copy = remote(sent, got, r.x_ss.at[g, i], r.x_rs.at[g, i], near)
        copy.start()
        near_copies[g].append(copy)

    def near_left_make(g, left):
        r.left_sent[g][...] = nt(r.sel[1], left).astype(BF)
        r.left_own[g][...] = nt(r.sel[0], left).astype(BF)

    def near_left_start(g, left):
        r.left_sent[g][...] = nt(r.sel[1], left).astype(BF)
        near_start(g, 0, r.left_sent[g], r.left_near[g])

    def near_left(g, left):
        near_left_start(g, left)
        r.left_own[g][...] = nt(r.sel[0], left).astype(BF)

    def near_right(g):
        if g == FO2:
            for i in range(2):
                columns = pl.ds(i * (cfg.widths[g] // 2), cfg.widths[g] // 2)
                near_start(g, 1 + i, r.right_own[g].at[:, columns], r.right_near[g].at[:, columns])
        else:
            near_start(g, 1, r.right_own[g], r.right_near[g])

    rows_half = n_top * pr

    def mid_copy(z):
        return remote(r.mid_sent[z], r.mid_got[z], r.m_ss.at[z], r.m_rs.at[z], mid)

    def product(g, start):
        rows = pl.ds(start, rows_half)
        if g >= CV:
            columns = pl.ds(0 if start == 0 else hw, hw)
            return r.pair_own[g - CV, rows] + r.pair_r[g - CV, :, columns].astype(F32)
        return nn(r.left_own[g][rows], r.right_own[g][...]) + nn(
            r.left_near[g][rows], r.right_near[g][...]
        )

    def products(z, start):
        parts = [product(g, start) for g in BUNDLES[z]]
        return parts[0] if len(parts) == 1 else jnp.concatenate(parts, axis=1)

    def mid_half(i):
        columns = pl.ds(i * (cfg.widths[FO2] // 2), cfg.widths[FO2] // 2)
        sent, got = r.mid_sent[Z_FO2].at[:, columns], r.mid_got[Z_FO2].at[:, columns]
        return remote(sent, got, r.mh_ss.at[i], r.mh_rs.at[i], mid)

    def mid_send_half(i):
        left, right, right_half = near_copies[FO2]
        if i == 0:
            left.wait()
            right.wait()
        else:
            right_half.wait()
        columns = pl.ds(i * (cfg.widths[FO2] // 2), cfg.widths[FO2] // 2)
        rows = pl.ds(rows_half, rows_half)
        part = nn(r.left_own[FO2][rows], r.right_own[FO2][:, columns]) + nn(
            r.left_near[FO2][rows], r.right_near[FO2][:, columns]
        )
        r.mid_sent[Z_FO2][:, columns] = part.astype(BF)
        mid_half(i).start()

    def mid_send(z):
        for g in BUNDLES[z]:
            wait_all(near_copies[g])
        r.mid_sent[z][...] = products(z, rows_half).astype(BF)
        mid_copy(z).start()

    def top_send(z):
        if z == Z_FO2:
            mid_half(0).wait()
            mid_half(1).wait()
        else:
            mid_copy(z).wait()
        total = products(z, 0) + r.mid_got[z][...].astype(F32)
        sent, received = r.block_sent[z], r.block_got[z]
        sent[...] = total.astype(BF).reshape(n_top, pr, total.shape[-1])

        def send(step, carry):
            index, device = top_peer(step)
            remote(
                sent.at[index], received.at[top], r.z_ss.at[z, index], r.z_rs.at[z, top], device
            ).start()
            return carry

        lax.fori_loop(1, n_top, send, 0)
        received[top] = sent[top]

    def top_close(z):
        sent, received = r.block_sent[z], r.block_got[z]

        def close(step, carry):
            index, device = top_peer(step)
            remote(
                sent.at[index], received.at[index], r.z_ss.at[z, index], r.z_rs.at[z, index], device
            ).wait()
            return carry

        lax.fori_loop(1, n_top, close, 0)

        def add(index, total):
            return total + received[index].astype(F32)

        total = lax.fori_loop(1, n_top, add, received[0].astype(F32))[:rpd]
        at = 0
        for g in BUNDLES[z]:
            size = cfg.widths[g]
            part, at = total[:, at : at + size], at + size
            if g == SQKV:
                for i in range(3):
                    r.self_grads[i][...] = part[:, i * hw : (i + 1) * hw]
                    leave(leaving.self_grads[i])
                continue
            if g in (SO, CO):
                pad = jnp.zeros((ceil_to(rpd, 128) - rpd, hw), F32)
                r.grads[g][...] = jnp.concatenate([part, pad], axis=0).T[:, :rpd]
            else:
                r.grads[g][...] = part
            leave(leaving.grads[g])

    def early_peers(start):
        def step_of(step, carry):
            index = lax.rem(hi + step, n_hi)
            start(index, (index * 2 + parity, t))
            return carry

        lax.fori_loop(1, n_hi, step_of, 0)

    def early_right_copy(index, device, slot):
        return remote(
            r.early_right.at[hi], r.early_right.at[slot], r.er_ss.at[index], r.er_rs.at[slot], device
        )

    def early_left_copy(index, device, slot):
        return remote(
            r.early_sent.at[index, core],
            r.early_left.at[slot, core],
            r.el_ss.at[index],
            r.el_rs.at[slot],
            device,
        )

    def early_left_pass(index):
        ref = r.early_left.at[index, core]
        return remote(ref, ref, r.ef_ss.at[index], r.ef_rs.at[index], sibling)

    def early_left_exchange():
        def step_of(index, device):
            early_left_copy(index, device, index).wait()
            early_left_pass(index).start()

        early_peers(step_of)

    def early_left_open(left):
        for which in range(2):
            rows = nt(r.sel[which], left).astype(BF).reshape(2, n_top, pr, lat)
            for m in range(n_top):
                r.early_sent[2 * m + side, which] = rows[0, m]
                r.early_sent[2 * m + 1 - side, which] = rows[1, m]
        early_peers(lambda index, device: early_left_copy(index, device, hi).start())
        r.early_left[hi] = r.early_sent[hi]

    inner = (top + side) == 1
    other_inner = ((1 - top) * 4 + (1 - side) * 2 + parity, t)
    other_end = ((1 - top) * 4 + side * 2 + parity, t)

    def line_copy(i, slot, sent, device):
        return remote(
            sent, r.line_in[i].at[slot], r.li_ss.at[i, slot], r.li_rs.at[i, slot], device
        )

    def line_lefts():
        return [
            line_copy(0, 0, r.left_own[FI1], mid),
            line_copy(0, 1, r.left_sent[FI1], diag_mid),
        ]

    def line_right():
        return line_copy(1, 0, r.right_own[FI1], mid)

    def line_forward():
        return line_copy(1, 1, r.line_in[1].at[0], near)

    def line_open(copies):
        @pl.when(jnp.logical_not(inner))
        def _():
            for copy in copies():
                copy.start()

    def line_pass():
        @pl.when(inner)
        def _():
            line_right().wait_recv()
            line_forward().start()

    def line_out(i):
        device, slot = ((mid, 1), (other_inner, 0), (other_end, 0))[i]
        return remote(r.line_sent.at[i], r.line_got.at[slot], r.lo_ss.at[i], r.lo_rs.at[slot], device)

    def line_send():
        wait_all(near_copies[FI1])

        def block(ref, flank, index):
            return ref[pl.ds(pl.multiple_of((flank * n_top + index) * pr, 16), pr)]

        r.line_sum[...] = nn(r.left_own[FI1][...], r.right_own[FI1][...]) + nn(
            r.left_near[FI1][...], r.right_near[FI1][...]
        )

        @pl.when(inner)
        def _():
            for copy in line_lefts():
                copy.wait_recv()
            line_forward().wait()
            r.line_sent[0] = block(r.line_sum, 1, top).astype(BF)
            line_out(0).start()
            end_sum = nn(r.line_in[0][0], r.line_in[1][0]) + nn(r.line_in[0][1], r.line_in[1][1])
            half_rows = n_top * pr
            r.line_sum[:half_rows] += end_sum[half_rows:]
            r.line_sum[half_rows:] += end_sum[:half_rows]
            for i, flank in ((1, 1), (2, 0)):
                r.line_sent[i] = block(r.line_sum, flank, 1 - top).astype(BF)
                line_out(i).start()

        r.grads[FI1][...] = block(r.line_sum, 0, top)[:rpd]

    def line_close():
        @pl.when(inner)
        def _():
            for i in range(3):
                line_out(i).wait_send()

        @pl.when(jnp.logical_not(inner))
        def _():
            for copy in line_lefts() + [line_right()]:
                copy.wait_send()
            line_out(0).wait_recv()
            r.grads[FI1][...] += r.line_got[1, :rpd].astype(F32)

        line_out(1).wait_recv()
        r.grads[FI1][...] += r.line_got[0, :rpd].astype(F32)
        leave(leaving.grads[FI1])

    def early_copy():
        return remote(r.early_part, r.early_got, r.ep_ss.at[0], r.ep_rs.at[0], near)

    def early_product(which):
        def add(index, total):
            return total + nn(r.early_left[index, which], r.early_right[index])

        return lax.fori_loop(0, n_hi, add, jnp.zeros((pr, width), F32))

    def early_send():
        def wait(index, device):
            early_right_copy(index, device, index).wait()
            early_left_pass(index).wait()

        early_peers(wait)
        r.early_part[...] = early_product(1).astype(BF)
        early_copy().start()
        r.grads[FO1][...] = early_product(0)[:rpd]

    def early_close():
        early_copy().wait()
        r.grads[FO1][...] += r.early_got[:rpd].astype(F32)
        leave(leaving.grads[FO1])

    early = cfg.early

    def row_of(ref):
        return ref[...].reshape(1, width)

    r.sel[1] = selection(1 - parity)
    r.sel[0] = selection(parity)
    wait_all(quick)
    keep = r.keep[0].astype(F32)
    x0 = r.x0[...].astype(F32)
    unit0, _ = norm_parts(x0)
    query_in = (unit0 * row_of(r.cross_norm)).astype(BF)
    r.query_in[...] = query_in
    arrive("cq")
    query = nt(query_in, w.cq[...]).astype(BF).astype(F32) * HEAD_DIM ** (-0.5)
    r.qf[t] = query.astype(BF)
    r.q_wide[...] = spread(query).astype(BF)

    pl.semaphore_wait(barrier, 5 + n_hi - 1)

    wait_all(pair_copies)

    def pair_part(part, owner, k, peer):
        i, start, size = ((0, 0, hw), (1, 0, hw // 2), (1, hw // 2, hw // 2))[part]
        ref = r.wkv.at[owner, i, pl.ds(start, size)]
        return remote(ref, ref, r.wkv_ss.at[part, k], r.wkv_rs.at[part, k], peer)

    def pair_send(part):
        copies = [pair_part(part, t, 0, sibling), pair_part(part, t, 1, far)]
        for copy in copies:
            copy.start()
        return copies

    def pair_forward(part, copies):
        wait_all(copies)
        copy = pair_part(part, far_t, 2, sibling)
        copy.start()
        return copy

    key_sends = pair_send(0)

    for b in range(blocks):
        start = b * KEY_BLOCK
        size = min(cfg.patches - start, KEY_BLOCK)
        if size < KEY_BLOCK:
            lane = lax.broadcasted_iota(jnp.int32, (1, KEY_BLOCK), 1) + (start - cfg.patches)
            r.mask[b] = jnp.where((lane >= 0) & (lane < r.captions[0]), 1.0, 0.0)
        if size > 0:
            patch = r.patch_mask[:, start : start + size]
            r.mask[b, :, :size] = jnp.where(patch != 0, 1.0, 0.0)

    tail_row = lax.broadcasted_iota(jnp.int32, (TAIL, width), 0)
    tail = jnp.where(tail_row < cfg.keys - cfg.main_rows, r.tail[...].astype(F32), 0.0)
    r.source[cfg.main_rows :] = tail.astype(BF)

    @pl.when(t == 3)
    def _():
        r.own[own_main:] = tail.astype(BF)

    byte_gain = row_of(r.byte_norm)

    def block_rows(b):
        return pl.ds(pl.multiple_of(b * KEY_BLOCK, KEY_BLOCK), KEY_BLOCK)

    q_wide = r.q_wide[...]
    wait_all(byte_copies)
    for copy in others:
        copy.start()

    def lanes(values, combine):
        total = values[:, :128]
        for at in range(128, values.shape[1], 128):
            total = combine(total, values[:, at : at + 128])
        return total

    largest = jnp.full((stack, 1), -3.0e38, F32)
    r.stat[...] = jnp.zeros(r.stat.shape, F32)
    r.wide_acc[...] = jnp.zeros(r.wide_acc.shape, F32)
    tops = []
    for b in range(blocks):
        rows = pl.ds(b * KEY_BLOCK, KEY_BLOCK)
        unit, _ = norm_parts(r.source[rows].astype(F32))
        source = (unit * byte_gain).astype(BF)
        r.source[rows] = source
        key = nt(source, r.wkv[t, 0]).astype(BF)
        value = nt(source, r.wkv[t, 1]).astype(BF)
        r.key[rows] = key
        r.value[rows] = value
        scores = jnp.where(r.mask[b] > 0.0, nt(q_wide, key), -1000000000.0)
        top_score = jnp.max(lanes(scores, jnp.maximum), axis=1, keepdims=True)
        before, largest = largest, jnp.maximum(largest, top_score)
        tops.append(largest)
        powers = jnp.exp(scores - largest)
        shrink = jnp.exp(before - largest)
        soft = powers.astype(BF)
        r.power[b] = soft
        r.stat[...] = r.stat[...] * shrink + lanes(powers, jnp.add)
        r.wide_acc[...] = r.wide_acc[...] * shrink + nn(soft, value)
    summed = jnp.sum(r.stat[...], axis=1, keepdims=True)
    inverse = 1.0 / summed
    lane = lax.broadcasted_iota(jnp.int32, (stack, 128), 1)
    factors = jnp.zeros((stack, 128), F32)
    for b in range(blocks):
        factors = jnp.where(lane == b, inverse * jnp.exp(tops[b] - largest), factors)
    r.weight[...] = factors

    def weight_of(b):
        picked = lax.broadcasted_iota(jnp.int32, (stack, 128), 1) == b
        return jnp.sum(jnp.where(picked, r.weight[...], 0.0), axis=1, keepdims=True)

    cross_mix = gathered_heads(r.wide_acc[...] * inverse).astype(BF)
    r.right_own[CO][...] = cross_mix
    r.lse[t] = as_row(largest + jnp.log(summed))

    arrive("co")
    sum_open(0, nn(cross_mix, w.co[...]))
    sum_cross(0)
    near_right(CO)
    near_left(FO2, r.cot[...])

    r.deep_acc[...] = jnp.zeros(r.deep_acc.shape, F32)

    def blend(b, carry):
        r.deep_acc[...] += weight_of(b) * nn(r.power[b], r.source[block_rows(b)])
        return carry

    lax.fori_loop(0, blocks, blend, 0)
    r.blended[...] = r.deep_acc[...].astype(BF)
    sum_back(0)
    q_share = share(r.qf, 0)
    lse_share = share(r.lse, 1)
    after_cross = x0 + keep * sum_close(0)

    def ffn_open(a, values, gain, win, wout, out_group, n):
        unit, scale = norm_parts(values)
        r.unit[n][...] = unit
        r.scale[n][...] = scale
        normed = (unit * gain).astype(BF)
        r.normed[n][...] = normed
        arrive(win)
        active, slope = gelu_parts(nn(normed, r.held[win][...]))
        active = active.astype(BF)
        r.slope[n][...] = slope
        if out_group == FO1 and early:
            r.early_right[hi] = active
            early_peers(lambda index, device: early_right_copy(index, device, hi).start())
        else:
            r.right_own[out_group][...] = active
            near_right(out_group)
        arrive(wout)
        sum_open(a, nn(active, r.held[wout][...]))

    ffn_open(1, after_cross, row_of(r.ffn_norm1), "fi1", "fo1", FO1, 0)

    sum_cross(1)
    key_forward = pair_forward(0, key_sends)
    near_left(FI1, r.normed[0][...])
    if early:
        line_open(line_lefts)
    key_forward.wait()
    live_row = jnp.concatenate([r.mask[b] for b in range(blocks)], axis=1)
    live_row = jnp.broadcast_to(live_row, (8, key_rows))
    live_row = pltpu.roll(live_row, lax.rem(key_rows - window, key_rows), 1)
    r.own_live[...] = live_row[:, : ceil_to(own_rows, 128)].T[:own_rows]
    wait_all(q_share)
    wait_all(lse_share)

    def own_powers(s, carry):
        key = nt(r.source[pl.ds(window, own_rows)], r.wkv[s, 0]).astype(BF)
        scores = nt(key, spread(r.qf[s]).astype(BF))
        live = jnp.broadcast_to(r.own_live[:, :1], (own_rows, stack))
        r.own_power[s] = (jnp.exp(jnp.minimum(scores - r.lse[s, 0:1], 0.0)) * live).astype(BF)
        return carry

    lax.fori_loop(0, 2, own_powers, 0)
    sum_back(1)
    value_sends = [pair_send(1)]
    after_ffn1 = after_cross + sum_close(1)

    unit_s, scale_s = norm_parts(after_ffn1)
    r.unit[1][...] = unit_s
    r.scale[1][...] = scale_s
    inner_in = (unit_s * row_of(r.self_norm)).astype(BF)
    r.normed[1][...] = inner_in
    arrive("sq", "sk", "sv", "so")
    factor = HEAD_DIM ** (-0.5)
    self_q = nt(inner_in, w.sq[...]).astype(BF).astype(F32) * factor
    self_k = nt(inner_in, w.sk[...]).astype(BF)
    self_v = nt(inner_in, w.sv[...]).astype(BF)
    self_q_wide = spread(self_q).astype(BF)
    self_scores = nt(self_k, self_q_wide)
    self_powers = jnp.exp(self_scores - jnp.max(self_scores, axis=0, keepdims=True))
    self_soft = self_powers / jnp.sum(self_powers, axis=0, keepdims=True)
    self_mix = gathered_heads(tn(self_soft.astype(BF), self_v)).astype(BF)
    r.self_q_wide[...] = self_q_wide
    r.self_k[...] = self_k
    r.self_v[...] = self_v
    r.self_soft[...] = self_soft
    sum_open(2, nn(self_mix, w.so[...]))
    r.right_own[SO][...] = self_mix
    near_right(SO)
    sum_cross(2)
    near_left(SQKV, inner_in)
    near_left_make(CQ, r.query_in[...])

    lax.fori_loop(2, 4, own_powers, 0)
    sum_back(2)
    value_sends.append(pair_send(2))
    after_self = after_ffn1 + sum_close(2)

    ffn_open(3, after_self, row_of(r.ffn_norm2), "fi2", "fo2", FO2, 2)
    cotangent = r.cot[...]

    def ffn_back(a, win, wout, in_group, n, branch):
        grad_hidden = (nt(branch, wout[...]) * r.slope[n][...]).astype(BF)
        r.right_own[in_group][...] = grad_hidden
        sum_open(a, nt(grad_hidden, win[...]))

    ffn_back(4, w.fi2, w.fo2, FI2, 2, cotangent)
    near_right(FI2)
    near_left(FI2, r.normed[2][...])
    sum_cross(4)
    if early:
        for which in range(2):
            r.blended_rows[which] = nt(r.sel[which], r.blended[...]).astype(BF)
    value_forwards = [pair_forward(1 + i, copies) for i, copies in enumerate(value_sends)]
    mid_send_half(0)
    mid_send_half(1)
    sum_back(4)
    sum_cross(3)
    dnormed = sum_close(4)
    r.vec[...] = jnp.zeros(r.vec.shape, F32)
    r.vec[3:4] = jnp.sum(dnormed * r.unit[2][...], axis=0, keepdims=True)
    grad_after_self = cotangent.astype(F32) + norm_back(
        r.unit[2][...], r.scale[2][...], row_of(r.ffn_norm2), dnormed
    )

    self_branch = grad_after_self.astype(BF)
    self_do = spread(nt(self_branch, w.so[...]).astype(BF)).astype(BF)
    self_soft = r.self_soft[...]
    grad_soft = nt(r.self_v[...], self_do)
    inner_sum = jnp.sum(self_soft * grad_soft, axis=0, keepdims=True)
    self_ds = (self_soft * (grad_soft - inner_sum)).astype(BF)
    self_dk = nn(self_ds, r.self_q_wide[...]).astype(BF)
    self_dv = nn(self_soft.astype(BF), self_do).astype(BF)
    self_dq = (gathered_heads(tn(self_ds, r.self_k[...])) * factor).astype(BF)
    sum_open(5, nn(self_dq, w.sq[...]) + nn(self_dk, w.sk[...]) + nn(self_dv, w.sv[...]))
    r.right_own[SQKV][...] = jnp.concatenate([self_dq, self_dk, self_dv], axis=1)
    near_right(SQKV)
    near_left(SO, self_branch)
    sum_cross(5)
    sum_back(3)
    wait_all(value_forwards)

    def own_values(s, carry):
        r.own_value[s] = nt(r.source[pl.ds(window, own_rows)], r.wkv[s, 1]).astype(BF)
        return carry

    lax.fori_loop(0, 4, own_values, 0)
    mid_send(Z_FI2)
    sum_back(5)
    top_send(Z_FO2)
    dnormed = sum_close(5)
    r.vec[2:3] = jnp.sum(dnormed * r.unit[1][...], axis=0, keepdims=True)
    grad_after_ffn1 = grad_after_self + norm_back(
        r.unit[1][...], r.scale[1][...], row_of(r.self_norm), dnormed
    )

    branch1 = grad_after_ffn1.astype(BF)
    ffn_back(6, w.fi1, w.fo1, FI1, 0, branch1)
    near_right(FI1)
    if early:
        line_open(lambda: [line_right()])
    early_left_open(branch1) if early else near_left(FO1, branch1)
    sum_cross(6)
    r.new_latents[...] = (after_self + sum_close(3)).astype(BF)
    leave(leaving.new_latents)
    mid_send(Z_SELF)
    near_start(CQ, 0, r.left_sent[CQ], r.left_near[CQ])
    sum_back(6)
    dnormed = sum_close(6)
    r.vec[1:2] = jnp.sum(dnormed * r.unit[0][...], axis=0, keepdims=True)
    grad_after_cross = grad_after_ffn1 + norm_back(
        r.unit[0][...], r.scale[0][...], row_of(r.ffn_norm1), dnormed
    )

    cross_branch = (keep * grad_after_cross).astype(BF)
    dmix = nt(cross_branch, w.co[...]).astype(BF)
    r.dof[t] = dmix
    do_share = share(r.dof, 2)
    do_wide_f32 = spread(dmix)
    do_wide = do_wide_f32.astype(BF)
    mix3 = jnp.concatenate([r.right_own[CO][...].astype(F32)] * heads, axis=0)
    delta = jnp.sum(do_wide_f32 * mix3, axis=1, keepdims=True)
    r.delta[t] = as_row(delta)
    delta_share = share(r.delta, 3)
    near_left(CO, cross_branch)
    if not early:
        mid_send(Z_FI1)

    def pair_open(g, left, right):
        i = g - CV
        sent = nn(left(1), right)
        r.pair_s[i] = jnp.concatenate([sent[:rows_half], sent[rows_half:]], axis=1).astype(BF)
        copy = remote(r.pair_s.at[i], r.pair_r.at[i], r.pair_ss.at[i], r.pair_rs.at[i], near)
        copy.start()
        near_copies[g].append(copy)
        r.pair_own[i] = nn(left(0), right)

    blended = r.blended[...]

    def value_rows(which):
        return r.blended_rows[which] if early else nt(r.sel[which], blended).astype(BF)

    pair_open(CV, value_rows, do_wide)
    r.deep_acc[...] = jnp.zeros(r.deep_acc.shape, F32)
    r.wide_acc[...] = jnp.zeros(r.wide_acc.shape, F32)

    def back(b, carry):
        rows = block_rows(b)
        grad_power = nt(do_wide, r.value[rows])
        ds = (r.power[b].astype(F32) * (weight_of(b) * (grad_power - delta))).astype(BF)
        r.wide_acc[...] += nn(ds, r.key[rows])
        r.deep_acc[...] += nn(ds, r.source[rows])
        return carry

    def back_and_send(b, carry):
        back(b, carry)

        @pl.when(b == 0)
        def _():
            if early:
                line_pass()

        @pl.when(b == min(1, blocks - 1))
        def _():
            top_send(Z_FI2)

        @pl.when(b == max(0, blocks - 2))
        def _():
            mid_send(Z_VALUE)

        return carry

    lax.fori_loop(0, blocks, back_and_send, 0)
    cross_dq = (gathered_heads(r.wide_acc[...]) * factor).astype(BF)
    sum_open(7, nn(cross_dq, w.cq[...]))
    q_wide = r.q_wide[...]
    deep = r.deep_acc[...]
    deep_low = deep.astype(BF)
    pair_open(CK, lambda which: nt(r.sel[which], deep_low).astype(BF), q_wide)
    r.right_own[CQ][...] = cross_dq
    near_right(CQ)
    sum_cross(7)
    top_send(Z_SELF)
    if early:
        line_send()
    gain_row = (
        jnp.sum(deep * nn(q_wide, r.wkv[t, 0]), axis=0, keepdims=True)
        + jnp.sum(blended.astype(F32) * nn(do_wide, r.wkv[t, 1]), axis=0, keepdims=True)
    ) / byte_gain
    r.gain[t] = jnp.concatenate([gain_row, jnp.zeros((7, width), F32)], axis=0)
    gain_share = share(r.gain, 4)
    wait_all(do_share)
    wait_all(delta_share)
    r.own_acc[...] = jnp.zeros(r.own_acc.shape, F32)

    def own_back(s, carry):
        do_here = spread(r.dof[s]).astype(BF)
        q_here = spread(r.qf[s]).astype(BF)
        soft = r.own_power[s]
        grad_power = nt(r.own_value[s], do_here)
        ds = (soft.astype(F32) * (grad_power - r.delta[s, 0:1])).astype(BF)
        dk = nn(ds, q_here).astype(BF)
        dv = nn(soft, do_here).astype(BF)
        r.own_acc[...] += nn(dk, r.wkv[s, 0]) + nn(dv, r.wkv[s, 1])
        return carry


    def own_back_and_send(s, carry):
        own_back(s, carry)

        @pl.when(s == 1)
        def _():
            sum_back(7)
            mid_send(Z_KEY)

        @pl.when(s == 2)
        def _():
            if not early:
                top_send(Z_FI1)
            top_send(Z_VALUE)

        return carry

    lax.fori_loop(0, 4, own_back_and_send, 0)
    if early:
        early_left_exchange()
    dnormed = sum_close(7)
    unit0, scale0 = norm_parts(r.x0[...].astype(F32))
    r.vec[0:1] = jnp.sum(dnormed * unit0, axis=0, keepdims=True)
    r.latent_grads[...] = (
        grad_after_cross + norm_back(unit0, scale0, row_of(r.cross_norm), dnormed)
    ).astype(BF)
    leave(leaving.latent_grads)
    wait_all(gain_share)
    r.vec[4:5] = r.gain[0, 0:1] + r.gain[1, 0:1] + r.gain[2, 0:1] + r.gain[3, 0:1]
    live_count = jnp.sum(jnp.sum(r.mask[...], axis=0), axis=1, keepdims=True)
    lane = lax.broadcasted_iota(jnp.int32, (1, width), 1)
    r.vec[5:6] = keep * jnp.where(lane == 0, live_count, jnp.where(lane == 1, float(lat), 0.0))
    vec_copy = remote(r.vec, r.vec_r, r.vec_ss.at[0], r.vec_rs.at[0], near)
    vec_copy.start()
    if early:
        early_send()
    else:
        mid_send(Z_FO1)
    top_send(Z_KEY)
    vec_copy.wait()
    r.vec[...] += r.vec_r[...]
    vec_copy = remote(r.vec, r.vec_m, r.vec_ss.at[1], r.vec_rs.at[1], mid)
    vec_copy.start()
    def own_norm_back(c, carry):
        rows = pl.ds(pl.multiple_of(c * OWN_CHUNK, OWN_CHUNK), OWN_CHUNK)
        unit, scale = norm_parts(r.own[rows].astype(F32))
        r.own_acc[rows] = norm_back(unit, scale, byte_gain, r.own_acc[rows])
        return carry

    own_copies[0].wait()

    @pl.when(t < 3)
    def _():
        own_copies[1].wait()

    lax.fori_loop(0, own_rows // OWN_CHUNK, own_norm_back, 0)
    vec_copy.wait()
    r.vec_all[top] = r.vec[...] + r.vec_m[...]

    def vec_top(step, source_index):
        index, device = top_peer(step)
        return remote(
            r.vec_all.at[top],
            r.vec_all.at[source_index],
            r.vh_ss.at[index],
            r.vh_rs.at[source_index],
            device,
        )

    def vec_send(step, carry):
        vec_top(step, top).start()
        return carry

    lax.fori_loop(1, n_top, vec_send, 0)
    for k in range(4):

        @pl.when(t == k)
        def _(skip=k * cfg.share % 16):
            r.byte_grads[...] = r.own_acc[skip : skip + cfg.share].astype(BF)

    leave(leaving.byte_grads)
    for z in (Z_FO2, Z_FI2, Z_SELF):
        top_close(z)
    if early:
        early_close()
        line_close()
    else:
        top_send(Z_FO1)
        top_close(Z_FI1)
        top_close(Z_FO1)
    for z in (Z_VALUE, Z_KEY):
        top_close(z)

    def vec_close(step, carry):
        vec_top(step, top_peer(step)[0]).wait()
        return carry

    lax.fori_loop(1, n_top, vec_close, 0)
    vec = lax.fori_loop(1, n_top, lambda i, total: total + r.vec_all[i], r.vec_all[0])
    mine = pltpu.roll(vec, lax.rem(width - dp * rpd, width), 1)
    for i in range(4):
        r.gain_grads[i][...] = mine[i : i + 1, :rpd].reshape(rpd)
        leave(leaving.gain_grads[i])
    r.byte_gain_grad[...] = vec[4:5].reshape(width)
    leave(leaving.byte_gain_grad)
    r.counts[...] = vec[5:6, :2].reshape(2)
    leave(leaving.counts)
    wait_all(left)


def finish(count, *refs):
    sources, targets, held = (refs[i * count : (i + 1) * count] for i in range(3))
    in_sems, out_sems = refs[3 * count :]
    arrivals = [
        pltpu.make_async_copy(src, via, in_sems.at[i])
        for i, (src, via) in enumerate(zip(sources, held))
    ]
    departures = [
        pltpu.make_async_copy(via, dst, out_sems.at[i])
        for i, (via, dst) in enumerate(zip(held, targets))
    ]
    order = sorted(range(count), key=lambda i: -math.prod(held[i].shape) * held[i].dtype.itemsize)
    for i in order:
        arrivals[i].start()
    for i in order:
        arrivals[i].wait()
        departures[i].start()
    for copy in departures:
        copy.wait()


def ceil_to(value, step):
    return -(-value // step) * step


def on_device(
    n_dp,
    latents,
    byte_array,
    caption_lengths,
    patch_mask,
    cross_keep,
    cross_norm,
    byte_norm,
    cross_query,
    cross_key,
    cross_value,
    cross_output,
    ffn_norm1,
    ffn_in1,
    ffn_out1,
    self_norm,
    self_query,
    self_key,
    self_value,
    self_output,
    ffn_norm2,
    ffn_in2,
    ffn_out2,
    cotangent,
):
    _, lat, width = latents.shape
    keys = byte_array.shape[1]
    patches = patch_mask.shape[1]
    hw = cross_query.shape[1]
    ff = ffn_in1.shape[1]
    heads = hw // HEAD_DIM
    share = keys // 4
    key_rows = ceil_to(keys, KEY_BLOCK)
    main_rows = keys // TAIL * TAIL
    own_rows = ceil_to(share + 15, OWN_CHUNK)
    blocks = key_rows // KEY_BLOCK
    n_hi = n_dp // 2
    n_top = n_hi // 2
    rpd = width // n_dp
    pr = ceil_to(rpd, 16)
    rt = n_hi * pr
    byte_parts = [
        (start, min(KEY_BLOCK, main_rows - start)) for start in range(0, main_rows, KEY_BLOCK)
    ]
    assert main_rows + TAIL == key_rows and len(byte_parts) == blocks
    assert 3 * share // 16 * 16 + own_rows == key_rows

    hbm = pl.BlockSpec(memory_space=pl.ANY)
    smem = pl.BlockSpec(memory_space=pltpu.SMEM)
    values = dict(
        keep=cross_keep,
        captions=caption_lengths,
        bytes=byte_array[0],
        tail=byte_array[0],
        quick=dict(
            x0=latents[0],
            cross_norm=cross_norm,
            patch_mask=patch_mask,
            byte_norm=byte_norm,
            ffn_norm1=ffn_norm1,
            self_norm=self_norm,
            ffn_norm2=ffn_norm2,
            cot=cotangent[0],
        ),
        cross_key=cross_key.T,
        cross_value=cross_value.T,
        weights=dict(
            cq=cross_query.T,
            co=cross_output,
            fi1=ffn_in1,
            fo1=ffn_out1,
            sq=self_query.T,
            sk=self_key.T,
            sv=self_value.T,
            so=self_output,
            fi2=ffn_in2,
            fo2=ffn_out2,
        ),
    )
    specs = {}
    specs.update(
        keep=smem,
        captions=smem,
        bytes=hbm,
        tail=pl.BlockSpec(
            (TAIL, width), lambda i: (main_rows // TAIL, 0), pipeline_mode=pl.Buffered(1)
        ),
        cross_key=hbm,
        cross_value=hbm,
        quick={name: hbm for name in values["quick"]},
        weights={name: hbm for name in values["weights"]},
    )
    widths = (ff, ff, 3 * hw, hw, ff, ff, hw, hw, hw, hw)
    early = n_hi == 4
    bundles = [
        128 if early and bundle in ((FI1,), (FO1,)) else sum(widths[g] for g in bundle)
        for bundle in BUNDLES
    ]

    def out(shape, kind):
        return jax.ShapeDtypeStruct(shape, kind)

    outputs = dict(
        new_latents=out((lat, width), BF),
        latent_grads=out((lat, width), BF),
        byte_grads=out((share, width), BF),
        gain_grads=[out((rpd,), F32) for _ in range(4)],
        byte_gain_grad=out((width,), F32),
        counts=out((2,), F32),
        self_grads=[out((rpd, hw), F32) for _ in range(3)],
        grads={
            FO2: out((rpd, ff), F32),
            FI2: out((rpd, ff), F32),
            SO: out((hw, rpd), F32),
            FO1: out((rpd, ff), F32),
            FI1: out((rpd, ff), F32),
            CO: out((hw, rpd), F32),
            CQ: out((rpd, hw), F32),
            CV: out((rpd, hw), F32),
            CK: out((rpd, hw), F32),
        },
    )

    def buf(*shape):
        return pltpu.VMEM(shape, BF)

    def wide(*shape):
        return pltpu.VMEM(shape, F32)

    def sems(*shape):
        return pltpu.SemaphoreType.DMA(shape)

    stack = heads * lat
    left_rows = [16 if early and g == FO1 else rt for g in range(CV)]
    right_columns = [128 if early and g == FO1 else widths[g] for g in range(CV)]
    scratch = dict(
        placed={name: pltpu.VMEM(a.shape, a.dtype) for name, a in values["quick"].items()},
        quick_sem=sems(len(values["quick"])),
        made=jax.tree.map(lambda a: pltpu.VMEM(a.shape, a.dtype), outputs),
        out_sem=sems(len(jax.tree.leaves(outputs))),
        held={name: buf(*value.shape) for name, value in values["weights"].items()},
        wkv=buf(4, 2, hw, width),
        source=buf(key_rows, width),
        key=buf(key_rows, hw),
        value=buf(key_rows, hw),
        power=buf(blocks, stack, KEY_BLOCK),
        stat=wide(stack, 128),
        mask=wide(blocks, 1, KEY_BLOCK),
        weight=wide(stack, 128),
        wide_acc=wide(stack, hw),
        deep_acc=wide(stack, width),
        blended=buf(stack, width),
        blended_rows=buf(*((2, rt, stack) if early else (16, 128))),
        q_wide=buf(stack, hw),
        query_in=buf(lat, width),
        qf=buf(4, lat, hw),
        dof=buf(4, lat, hw),
        lse=wide(4, 8, stack),
        delta=wide(4, 8, stack),
        gain=wide(4, 8, width),
        own=buf(own_rows, width),
        own_value=buf(4, own_rows, hw),
        own_power=buf(4, own_rows, stack),
        own_live=wide(own_rows, 8),
        own_acc=wide(own_rows, width),
        unit=[wide(lat, width) for _ in range(3)],
        scale=[wide(lat, 1) for _ in range(3)],
        normed=[buf(lat, width) for _ in range(3)],
        slope=[wide(lat, ff), wide(8, 128), wide(lat, ff)],
        self_q_wide=buf(stack, hw),
        self_k=buf(lat, hw),
        self_v=buf(lat, hw),
        self_soft=wide(lat, stack),
        sel=buf(2, rt, width),
        ar_s=buf(SETS, 2, lat // 2, width),
        ar_r1=buf(SETS, lat // 2, width),
        ar_r2=buf(SETS, lat // 2, width),
        ar_t=buf(SETS, 2, lat // 2, width),
        pair_own=wide(2, rt, hw),
        pair_s=buf(2, rt // 2, 2 * hw),
        pair_r=buf(2, rt // 2, 2 * hw),
        vec=wide(8, width),
        vec_r=wide(8, width),
        vec_m=wide(8, width),
        vec_all=wide(n_top, 8, width),
        left_own=[buf(rows, lat) for rows in left_rows],
        left_sent=[buf(rows, lat) for rows in left_rows],
        left_near=[buf(rows, lat) for rows in left_rows],
        right_own=[buf(lat, size) for size in right_columns],
        right_near=[buf(lat, size) for size in right_columns],
        mid_sent=[buf(rt // 2, size) for size in bundles],
        mid_got=[buf(rt // 2, size) for size in bundles],
        block_sent=[buf(n_top, pr, size) for size in bundles],
        block_got=[buf(n_top, pr, size) for size in bundles],
        byte_sem=sems(len(byte_parts)),
        own_sem=sems(2),
        w_sem=sems(len(values["weights"])),
        pair_sem=sems(2),
        share_ss=sems(5, 3),
        share_rs=sems(5, 3),
        wkv_ss=sems(3, 3),
        wkv_rs=sems(3, 3),
        ar_ss=sems(8, 3),
        ar_rs=sems(8, 3),
        x_ss=sems(CV, 3),
        x_rs=sems(CV, 3),
        mh_ss=sems(2),
        mh_rs=sems(2),
        m_ss=sems(len(BUNDLES)),
        m_rs=sems(len(BUNDLES)),
        z_ss=sems(len(BUNDLES), n_top),
        z_rs=sems(len(BUNDLES), n_top),
        early_right=buf(*((n_hi, lat, ff) if early else (16, 128))),
        early_sent=buf(*((n_hi, 2, pr, lat) if early else (16, 128))),
        early_left=buf(*((n_hi, 2, pr, lat) if early else (16, 128))),
        early_part=buf(pr, ff),
        early_got=buf(pr, ff),
        er_ss=sems(n_hi),
        er_rs=sems(n_hi),
        el_ss=sems(n_hi),
        el_rs=sems(n_hi),
        line_in=[buf(2, *shape) for shape in ((rt, lat), (lat, ff))] if early else [],
        line_sum=wide(*((rt, ff) if early else (16, 128))),
        line_sent=buf(*((3, pr, ff) if early else (16, 128))),
        line_got=buf(*((2, pr, ff) if early else (16, 128))),
        li_ss=sems(2, 2),
        li_rs=sems(2, 2),
        lo_ss=sems(3),
        lo_rs=sems(2),
        ef_ss=sems(n_hi),
        ef_rs=sems(n_hi),
        ep_ss=sems(1),
        ep_rs=sems(1),
        pair_ss=sems(2),
        pair_rs=sems(2),
        vec_ss=sems(2),
        vec_rs=sems(2),
        vh_ss=sems(n_top),
        vh_rs=sems(n_top),
    )
    tables = (values, dict(outs=outputs), scratch)

    def leaf(node):
        return not isinstance(node, (dict, list))

    flat = [jax.tree.flatten(table, is_leaf=leaf) for table in tables]
    trees = [tree for _, tree in flat]
    counts = [len(leaves) for leaves, _ in flat]
    cfg = SimpleNamespace(
        trees=trees,
        counts=counts,
        lat=lat,
        width=width,
        hw=hw,
        heads=heads,
        n_hi=n_hi,
        pr=pr,
        rpd=rpd,
        blocks=blocks,
        key_rows=key_rows,
        main_rows=main_rows,
        own_rows=own_rows,
        byte_parts=byte_parts,
        patches=patches,
        keys=keys,
        share=share,
        widths=widths,
        early=early,
        out_order=jax.tree.unflatten(jax.tree.structure(outputs), range(counts[1])),
    )
    results = pl.pallas_call(
        functools.partial(kernel, cfg),
        out_shape=flat[1][0],
        grid=(1,),
        in_specs=jax.tree.leaves(specs, is_leaf=leaf),
        out_specs=[hbm] * counts[1],
        scratch_shapes=flat[2][0],
        compiler_params=pltpu.CompilerParams(
            collective_id=0, has_side_effects=True, vmem_limit_bytes=64 * 2**20
        ),
        name="layers",
    )(*flat[0][0])
    results = pl.pallas_call(
        functools.partial(finish, counts[1]),
        out_shape=flat[1][0],
        in_specs=[hbm] * counts[1],
        out_specs=[hbm] * counts[1],
        scratch_shapes=[pltpu.VMEM(array.shape, array.dtype) for array in flat[1][0]]
        + [sems(counts[1])] * 2,
        name="results",
    )(*results)
    out = SimpleNamespace(**jax.tree.unflatten(trees[1], results)["outs"])
    grads = out.grads
    return (
        out.new_latents[None],
        out.latent_grads[None],
        out.byte_grads[None],
        out.gain_grads[0],
        out.byte_gain_grad,
        grads[CQ],
        grads[CK],
        grads[CV],
        grads[CO],
        out.gain_grads[1],
        grads[FI1],
        grads[FO1].T,
        out.gain_grads[2],
        out.self_grads[0],
        out.self_grads[1],
        out.self_grads[2],
        grads[SO],
        out.gain_grads[3],
        grads[FI2],
        grads[FO2].T,
        out.counts,
    )


def solution(mesh):
    in_specs = (
        P("dp", None, None),
        P("dp", None, None),
        P("dp"),
        P("dp", None),
        P("dp"),
        P(),
        P(),
        P(None, "tensor"),
        P(None, "tensor"),
        P(None, "tensor"),
        P("tensor", None),
        P(),
        P(None, "tensor"),
        P("tensor", None),
        P(),
        P(None, "tensor"),
        P(None, "tensor"),
        P(None, "tensor"),
        P("tensor", None),
        P(),
        P(None, "tensor"),
        P("tensor", None),
        P("dp", None, None),
    )
    out_specs = (
        P("dp", None, None),
        P("dp", None, None),
        P("dp", "tensor", None),
        P("dp"),
        P(),
        P("dp", "tensor"),
        P("dp", "tensor"),
        P("dp", "tensor"),
        P("tensor", "dp"),
        P("dp"),
        P("dp", "tensor"),
        P("tensor", "dp"),
        P("dp"),
        P("dp", "tensor"),
        P("dp", "tensor"),
        P("dp", "tensor"),
        P("tensor", "dp"),
        P("dp"),
        P("dp", "tensor"),
        P("tensor", "dp"),
        P(),
    )
    return jax.shard_map(
        functools.partial(on_device, mesh.shape["dp"]),
        mesh=mesh,
        in_specs=in_specs,
        out_specs=out_specs,
        check_vma=False,
    )
```

```python
import functools
import math
from types import SimpleNamespace

import jax
import jax.numpy as jnp
from jax import lax
from jax.experimental import pallas as pl
from jax.experimental.pallas import tpu as pltpu
from jax.sharding import PartitionSpec as P

HEAD_DIM = 64
EPSILON = 1e-05
GELU_A = 0.7978845608
GELU_B = 0.044715
KEY_BLOCK = 640
TAIL = 64
SETS = 4
OWN_CHUNK = 272
MESH = pl.DeviceIdType.MESH
BF = jnp.bfloat16
F32 = jnp.float32

FO2, FI2, SQKV, SO, FO1, FI1, CO, CQ, CV, CK = range(10)
BUNDLES = ((FO2,), (FI2,), (SQKV, SO), (CO, CV), (CQ, CK), (FI1,), (FO1,))
Z_FO2, Z_FI2, Z_SELF, Z_VALUE, Z_KEY, Z_FI1, Z_FO1 = range(7)


def nn(left, right):
    return lax.dot_general(left, right, (((1,), (0,)), ((), ())), preferred_element_type=F32)


def nt(left, right):
    return lax.dot_general(left, right, (((1,), (1,)), ((), ())), preferred_element_type=F32)


def tn(left, right):
    return lax.dot_general(left, right, (((0,), (0,)), ((), ())), preferred_element_type=F32)


def mean_of(values):
    return jnp.mean(values, axis=-1, keepdims=True)


def norm_parts(values):
    centered = values - mean_of(values)
    scale = lax.rsqrt(mean_of(centered * centered) + EPSILON)
    return centered * scale, scale


def norm_back(unit, scale, gain, grad):
    inner = grad * gain
    return scale * (inner - mean_of(inner) - unit * mean_of(inner * unit))


def gelu_parts(hidden):
    squared = hidden * hidden
    bent = jnp.tanh(GELU_A * hidden * (1.0 + GELU_B * squared))
    half = 0.5 * (1.0 + bent)
    slope = half + 0.5 * hidden * (1.0 - bent * bent) * (GELU_A * (1.0 + 3.0 * GELU_B * squared))
    return hidden * half, slope


def kernel(cfg, *refs):
    r = SimpleNamespace()
    at = 0
    for tree, count in zip(cfg.trees, cfg.counts):
        vars(r).update(jax.tree.unflatten(tree, refs[at : at + count]))
        at += count
    lat, width, hw, heads = cfg.lat, cfg.width, cfg.hw, cfg.heads
    n_hi, pr, rpd, blocks = cfg.n_hi, cfg.pr, cfg.rpd, cfg.blocks
    key_rows, own_rows = cfg.key_rows, cfg.own_rows
    half, stack = lat // 2, heads * lat
    dp, t = lax.axis_index("dp"), lax.axis_index("tensor")
    parity, hi, core = lax.rem(dp, 2), lax.div(dp, 2), lax.rem(t, 2)
    sib_t, far_t, diag_t = t + 1 - 2 * core, lax.rem(t + 2, 4), 3 - t
    sibling, far, diagonal = (dp, sib_t), (dp, far_t), (dp, diag_t)
    near = (dp + 1 - 2 * parity, t)
    side, top = lax.rem(hi, 2), lax.div(hi, 2)
    mid = (dp + 2 - 4 * side, t)
    trio = (sibling, far, diagonal)
    n_top = n_hi // 2

    def top_peer(step):
        index = lax.rem(top + step, n_top)
        return index, (index * 4 + side * 2 + parity, t)

    def remote(src, dst, sends, receives, device):
        return pltpu.make_async_remote_copy(
            src_ref=src,
            dst_ref=dst,
            send_sem=sends,
            recv_sem=receives,
            device_id=device,
            device_id_type=MESH,
        )

    byte_copies = [
        pltpu.make_async_copy(
            r.bytes.at[pl.ds(start, size)], r.source.at[pl.ds(start, size)], r.byte_sem.at[i]
        )
        for i, (start, size) in enumerate(cfg.byte_parts)
    ]
    weight_copies = {
        name: pltpu.make_async_copy(ref, r.held[name], r.w_sem.at[i])
        for i, (name, ref) in enumerate(r.weights.items())
    }
    w = SimpleNamespace(**r.held)

    def arrive(*names):
        for name in names:
            weight_copies[name].wait()

    pair_copies = [
        pltpu.make_async_copy(ref, r.wkv.at[t, i], r.pair_sem.at[i])
        for i, ref in enumerate((r.cross_key, r.cross_value))
    ]
    first = weight_copies["cq"]
    others = [
        weight_copies[name]
        for name in ("co", "fi1", "fo1", "sq", "sk", "sv", "so", "fi2", "fo2")
    ]
    quick = [
        pltpu.make_async_copy(ref, r.placed[name], r.quick_sem.at[i])
        for i, (name, ref) in enumerate(r.quick.items())
    ]
    vars(r).update(r.placed)
    share_at = t * cfg.share
    window = pl.multiple_of(lax.div(share_at, 16) * 16, 16)
    own_main = own_rows - TAIL
    own_copies = [
        pltpu.make_async_copy(
            r.bytes.at[pl.ds(pl.multiple_of(window + at, 16), size)],
            r.own.at[pl.ds(at, size)],
            r.own_sem.at[i],
        )
        for i, (at, size) in enumerate(((0, own_main), (own_main, TAIL)))
    ]
    for copy in quick + [first] + pair_copies + byte_copies + own_copies[:1]:
        copy.start()

    @pl.when(t < 3)
    def _():
        own_copies[1].start()

    leaving = SimpleNamespace(
        **jax.tree.map(
            lambda made, out, i: pltpu.make_async_copy(made, out, r.out_sem.at[i]),
            r.made,
            r.outs,
            cfg.out_order,
        )
    )
    left = []

    def leave(copy):
        copy.start()
        left.append(copy)

    vars(r).update(r.made)

    barrier = pltpu.get_barrier_semaphore()
    diag_mid = (dp + 2 - 4 * side + 1 - 2 * parity, t)
    for device in trio + (near, diag_mid):
        pl.semaphore_signal(barrier, inc=1, device_id=device, device_id_type=MESH)

    def greet(step, carry):
        device = (lax.rem(hi + step, n_hi) * 2 + parity, t)
        pl.semaphore_signal(barrier, inc=1, device_id=device, device_id_type=MESH)
        return carry

    lax.fori_loop(1, n_hi, greet, 0)

    columns = lax.broadcasted_iota(jnp.int32, (lat, hw), 1)
    head_mask = [
        (columns >= h * HEAD_DIM) & (columns < (h + 1) * HEAD_DIM) for h in range(heads)
    ]

    def spread(values):
        wide = values.astype(F32)
        return jnp.concatenate([jnp.where(m, wide, 0.0) for m in head_mask], axis=0)

    def gathered_heads(values):
        total = jnp.where(head_mask[0], values[:lat], 0.0)
        for h in range(1, heads):
            total = total + jnp.where(head_mask[h], values[h * lat : (h + 1) * lat], 0.0)
        return total

    def as_row(column):
        return jnp.broadcast_to(column, (column.shape[0], 128)).T[:8]

    def share(buffer, index):
        copies = [
            remote(
                buffer.at[t], buffer.at[t], r.share_ss.at[index, k], r.share_rs.at[index, k], peer
            )
            for k, peer in enumerate(trio)
        ]
        for copy in copies:
            copy.start()
        return copies

    def wait_all(copies):
        for copy in copies:
            copy.wait()

    hops = {}

    def sum_open(a, part):
        r.ar_s[a % SETS] = part.astype(BF).reshape(2, half, width)
        hops[a] = remote(
            r.ar_s.at[a % SETS, 1 - core], r.ar_r1.at[a % SETS], r.ar_ss.at[a, 0], r.ar_rs.at[a, 0], sibling
        )
        hops[a].start()

    def sum_cross(a):
        hops[a].wait()
        pair = r.ar_s[a % SETS, core].astype(F32) + r.ar_r1[a % SETS].astype(F32)
        r.ar_t[a % SETS, core] = pair.astype(BF)
        hops[a] = remote(
            r.ar_t.at[a % SETS, core], r.ar_r2.at[a % SETS], r.ar_ss.at[a, 1], r.ar_rs.at[a, 1], far
        )
        hops[a].start()

    def back_copy(a):
        half_total = r.ar_t.at[a % SETS, core]
        return remote(half_total, half_total, r.ar_ss.at[a, 2], r.ar_rs.at[a, 2], sibling)

    def sum_back(a):
        hops[a].wait()
        total = r.ar_t[a % SETS, core].astype(F32) + r.ar_r2[a % SETS].astype(F32)
        r.ar_t[a % SETS, core] = total.astype(BF)
        back_copy(a).start()

    def sum_close(a):
        back_copy(a).wait()
        return r.ar_t[a % SETS].reshape(lat, width).astype(F32)

    def selection(which):
        shape = (n_top, pr, width)
        block = lax.broadcasted_iota(jnp.int32, shape, 0)
        row = lax.broadcasted_iota(jnp.int32, shape, 1)
        feature = lax.broadcasted_iota(jnp.int32, shape, 2)
        parts = []
        for flank in (side, 1 - side):
            hit = (feature == (block * 4 + flank * 2 + which) * rpd + row) & (row < rpd)
            parts.append(jnp.where(hit, 1.0, 0.0).astype(BF).reshape(n_top * pr, width))
        return jnp.concatenate(parts, axis=0)

    near_copies = {g: [] for g in range(CK + 1)}

    def near_start(g, i, sent, got):
        copy = remote(sent, got, r.x_ss.at[g, i], r.x_rs.at[g, i], near)
        copy.start()
        near_copies[g].append(copy)

    def near_left_make(g, left):
        r.left_sent[g][...] = nt(r.sel[1], left).astype(BF)
        r.left_own[g][...] = nt(r.sel[0], left).astype(BF)

    def near_left_start(g, left):
        r.left_sent[g][...] = nt(r.sel[1], left).astype(BF)
        near_start(g, 0, r.left_sent[g], r.left_near[g])

    def near_left(g, left):
        near_left_start(g, left)
        r.left_own[g][...] = nt(r.sel[0], left).astype(BF)

    def near_right(g):
        if g == FO2:
            for i in range(2):
                columns = pl.ds(i * (cfg.widths[g] // 2), cfg.widths[g] // 2)
                near_start(g, 1 + i, r.right_own[g].at[:, columns], r.right_near[g].at[:, columns])
        else:
            near_start(g, 1, r.right_own[g], r.right_near[g])

    rows_half = n_top * pr

    def mid_copy(z):
        return remote(r.mid_sent[z], r.mid_got[z], r.m_ss.at[z], r.m_rs.at[z], mid)

    def product(g, start):
        rows = pl.ds(start, rows_half)
        if g >= CV:
            columns = pl.ds(0 if start == 0 else hw, hw)
            return r.pair_own[g - CV, rows] + r.pair_r[g - CV, :, columns].astype(F32)
        return nn(r.left_own[g][rows], r.right_own[g][...]) + nn(
            r.left_near[g][rows], r.right_near[g][...]
        )

    def products(z, start):
        parts = [product(g, start) for g in BUNDLES[z]]
        return parts[0] if len(parts) == 1 else jnp.concatenate(parts, axis=1)

    def mid_half(i):
        columns = pl.ds(i * (cfg.widths[FO2] // 2), cfg.widths[FO2] // 2)
        sent, got = r.mid_sent[Z_FO2].at[:, columns], r.mid_got[Z_FO2].at[:, columns]
        return remote(sent, got, r.mh_ss.at[i], r.mh_rs.at[i], mid)

    def mid_send_half(i):
        left, right, right_half = near_copies[FO2]
        if i == 0:
            left.wait()
            right.wait()
        else:
            right_half.wait()
        columns = pl.ds(i * (cfg.widths[FO2] // 2), cfg.widths[FO2] // 2)
        rows = pl.ds(rows_half, rows_half)
        part = nn(r.left_own[FO2][rows], r.right_own[FO2][:, columns]) + nn(
            r.left_near[FO2][rows], r.right_near[FO2][:, columns]
        )
        r.mid_sent[Z_FO2][:, columns] = part.astype(BF)
        mid_half(i).start()

    def mid_send(z):
        for g in BUNDLES[z]:
            wait_all(near_copies[g])
        r.mid_sent[z][...] = products(z, rows_half).astype(BF)
        mid_copy(z).start()

    def top_send(z):
        if z == Z_FO2:
            mid_half(0).wait()
            mid_half(1).wait()
        else:
            mid_copy(z).wait()
        total = products(z, 0) + r.mid_got[z][...].astype(F32)
        sent, received = r.block_sent[z], r.block_got[z]
        sent[...] = total.astype(BF).reshape(n_top, pr, total.shape[-1])

        def send(step, carry):
            index, device = top_peer(step)
            remote(
                sent.at[index], received.at[top], r.z_ss.at[z, index], r.z_rs.at[z, top], device
            ).start()
            return carry

        lax.fori_loop(1, n_top, send, 0)
        received[top] = sent[top]

    def top_close(z):
        sent, received = r.block_sent[z], r.block_got[z]

        def close(step, carry):
            index, device = top_peer(step)
            remote(
                sent.at[index], received.at[index], r.z_ss.at[z, index], r.z_rs.at[z, index], device
            ).wait()
            return carry

        lax.fori_loop(1, n_top, close, 0)

        def add(index, total):
            return total + received[index].astype(F32)

        total = lax.fori_loop(1, n_top, add, received[0].astype(F32))[:rpd]
        at = 0
        for g in BUNDLES[z]:
            size = cfg.widths[g]
            part, at = total[:, at : at + size], at + size
            if g == SQKV:
                for i in range(3):
                    r.self_grads[i][...] = part[:, i * hw : (i + 1) * hw]
                    leave(leaving.self_grads[i])
                continue
            if g in (SO, CO):
                pad = jnp.zeros((ceil_to(rpd, 128) - rpd, hw), F32)
                r.grads[g][...] = jnp.concatenate([part, pad], axis=0).T[:, :rpd]
            else:
                r.grads[g][...] = part
            leave(leaving.grads[g])

    def early_peers(start):
        def step_of(step, carry):
            index = lax.rem(hi + step, n_hi)
            start(index, (index * 2 + parity, t))
            return carry

        lax.fori_loop(1, n_hi, step_of, 0)

    def early_right_copy(index, device, slot):
        return remote(
            r.early_right.at[hi], r.early_right.at[slot], r.er_ss.at[index], r.er_rs.at[slot], device
        )

    def early_left_copy(index, device, slot):
        return remote(
            r.early_sent.at[index, core],
            r.early_left.at[slot, core],
            r.el_ss.at[index],
            r.el_rs.at[slot],
            device,
        )

    def early_left_pass(index):
        ref = r.early_left.at[index, core]
        return remote(ref, ref, r.ef_ss.at[index], r.ef_rs.at[index], sibling)

    def early_left_exchange():
        def step_of(index, device):
            early_left_copy(index, device, index).wait()
            early_left_pass(index).start()

        early_peers(step_of)

    def early_left_open(left):
        for which in range(2):
            rows = nt(r.sel[which], left).astype(BF).reshape(2, n_top, pr, lat)
            for m in range(n_top):
                r.early_sent[2 * m + side, which] = rows[0, m]
                r.early_sent[2 * m + 1 - side, which] = rows[1, m]
        early_peers(lambda index, device: early_left_copy(index, device, hi).start())
        r.early_left[hi] = r.early_sent[hi]

    inner = (top + side) == 1
    other_inner = ((1 - top) * 4 + (1 - side) * 2 + parity, t)
    other_end = ((1 - top) * 4 + side * 2 + parity, t)

    def line_copy(i, slot, sent, device):
        return remote(
            sent, r.line_in[i].at[slot], r.li_ss.at[i, slot], r.li_rs.at[i, slot], device
        )

    def line_lefts():
        return [
            line_copy(0, 0, r.left_own[FI1], mid),
            line_copy(0, 1, r.left_sent[FI1], diag_mid),
        ]

    def line_right():
        return line_copy(1, 0, r.right_own[FI1], mid)

    def line_forward():
        return line_copy(1, 1, r.line_in[1].at[0], near)

    def line_open(copies):
        @pl.when(jnp.logical_not(inner))
        def _():
            for copy in copies():
                copy.start()

    def line_pass():
        @pl.when(inner)
        def _():
            line_right().wait_recv()
            line_forward().start()

    def line_out(i):
        device, slot = ((mid, 1), (other_inner, 0), (other_end, 0))[i]
        return remote(r.line_sent.at[i], r.line_got.at[slot], r.lo_ss.at[i], r.lo_rs.at[slot], device)

    def line_send():
        wait_all(near_copies[FI1])

        def block(ref, flank, index):
            return ref[pl.ds(pl.multiple_of((flank * n_top + index) * pr, 16), pr)]

        r.line_sum[...] = nn(r.left_own[FI1][...], r.right_own[FI1][...]) + nn(
            r.left_near[FI1][...], r.right_near[FI1][...]
        )

        @pl.when(inner)
        def _():
            for copy in line_lefts():
                copy.wait_recv()
            line_forward().wait()
            r.line_sent[0] = block(r.line_sum, 1, top).astype(BF)
            line_out(0).start()
            end_sum = nn(r.line_in[0][0], r.line_in[1][0]) + nn(r.line_in[0][1], r.line_in[1][1])
            half_rows = n_top * pr
            r.line_sum[:half_rows] += end_sum[half_rows:]
            r.line_sum[half_rows:] += end_sum[:half_rows]
            for i, flank in ((2, 0), (1, 1)):
                r.line_sent[i] = block(r.line_sum, flank, 1 - top).astype(BF)
                line_out(i).start()

        r.grads[FI1][...] = block(r.line_sum, 0, top)[:rpd]

    def line_close():
        @pl.when(inner)
        def _():
            for i in range(3):
                line_out(i).wait_send()

        @pl.when(jnp.logical_not(inner))
        def _():
            for copy in line_lefts() + [line_right()]:
                copy.wait_send()
            line_out(0).wait_recv()
            r.grads[FI1][...] += r.line_got[1, :rpd].astype(F32)

        line_out(1).wait_recv()
        r.grads[FI1][...] += r.line_got[0, :rpd].astype(F32)
        leave(leaving.grads[FI1])

    def early_copy():
        return remote(r.early_part, r.early_got, r.ep_ss.at[0], r.ep_rs.at[0], near)

    def early_product(which):
        def add(index, total):
            return total + nn(r.early_left[index, which], r.early_right[index])

        return lax.fori_loop(0, n_hi, add, jnp.zeros((pr, width), F32))

    def early_send():
        def wait(index, device):
            early_right_copy(index, device, index).wait()
            early_left_pass(index).wait()

        early_peers(wait)
        r.early_part[...] = early_product(1).astype(BF)
        early_copy().start()
        r.grads[FO1][...] = early_product(0)[:rpd]

    def early_close():
        early_copy().wait()
        r.grads[FO1][...] += r.early_got[:rpd].astype(F32)
        leave(leaving.grads[FO1])

    early = cfg.early

    def row_of(ref):
        return ref[...].reshape(1, width)

    r.sel[1] = selection(1 - parity)
    r.sel[0] = selection(parity)
    wait_all(quick)
    keep = r.keep[0].astype(F32)
    x0 = r.x0[...].astype(F32)
    unit0, _ = norm_parts(x0)
    query_in = (unit0 * row_of(r.cross_norm)).astype(BF)
    r.query_in[...] = query_in
    arrive("cq")
    query = nt(query_in, w.cq[...]).astype(BF).astype(F32) * HEAD_DIM ** (-0.5)
    r.qf[t] = query.astype(BF)
    r.q_wide[...] = spread(query).astype(BF)

    pl.semaphore_wait(barrier, 5 + n_hi - 1)

    wait_all(pair_copies)

    def pair_part(part, owner, k, peer):
        i, start, size = ((0, 0, hw), (1, 0, hw // 2), (1, hw // 2, hw // 2))[part]
        ref = r.wkv.at[owner, i, pl.ds(start, size)]
        return remote(ref, ref, r.wkv_ss.at[part, k], r.wkv_rs.at[part, k], peer)

    def pair_send(part):
        copies = [pair_part(part, t, 0, sibling), pair_part(part, t, 1, far)]
        for copy in copies:
            copy.start()
        return copies

    def pair_forward(part, copies):
        wait_all(copies)
        copy = pair_part(part, far_t, 2, sibling)
        copy.start()
        return copy

    key_sends = pair_send(0)

    for b in range(blocks):
        start = b * KEY_BLOCK
        size = min(cfg.patches - start, KEY_BLOCK)
        if size < KEY_BLOCK:
            lane = lax.broadcasted_iota(jnp.int32, (1, KEY_BLOCK), 1) + (start - cfg.patches)
            r.mask[b] = jnp.where((lane >= 0) & (lane < r.captions[0]), 1.0, 0.0)
        if size > 0:
            patch = r.patch_mask[:, start : start + size]
            r.mask[b, :, :size] = jnp.where(patch != 0, 1.0, 0.0)

    tail_row = lax.broadcasted_iota(jnp.int32, (TAIL, width), 0)
    tail = jnp.where(tail_row < cfg.keys - cfg.main_rows, r.tail[...].astype(F32), 0.0)
    r.source[cfg.main_rows :] = tail.astype(BF)

    @pl.when(t == 3)
    def _():
        r.own[own_main:] = tail.astype(BF)

    byte_gain = row_of(r.byte_norm)

    def block_rows(b):
        return pl.ds(pl.multiple_of(b * KEY_BLOCK, KEY_BLOCK), KEY_BLOCK)

    q_wide = r.q_wide[...]
    wait_all(byte_copies)
    for copy in others:
        copy.start()

    def lanes(values, combine):
        total = values[:, :128]
        for at in range(128, values.shape[1], 128):
            total = combine(total, values[:, at : at + 128])
        return total

    largest = jnp.full((stack, 1), -3.0e38, F32)
    r.stat[...] = jnp.zeros(r.stat.shape, F32)
    r.wide_acc[...] = jnp.zeros(r.wide_acc.shape, F32)
    tops = []
    for b in range(blocks):
        rows = pl.ds(b * KEY_BLOCK, KEY_BLOCK)
        unit, _ = norm_parts(r.source[rows].astype(F32))
        source = (unit * byte_gain).astype(BF)
        r.source[rows] = source
        key = nt(source, r.wkv[t, 0]).astype(BF)
        value = nt(source, r.wkv[t, 1]).astype(BF)
        r.key[rows] = key
        r.value[rows] = value
        scores = jnp.where(r.mask[b] > 0.0, nt(q_wide, key), -1000000000.0)
        top_score = jnp.max(lanes(scores, jnp.maximum), axis=1, keepdims=True)
        before, largest = largest, jnp.maximum(largest, top_score)
        tops.append(largest)
        powers = jnp.exp(scores - largest)
        shrink = jnp.exp(before - largest)
        soft = powers.astype(BF)
        r.power[b] = soft
        r.stat[...] = r.stat[...] * shrink + lanes(powers, jnp.add)
        r.wide_acc[...] = r.wide_acc[...] * shrink + nn(soft, value)
    summed = jnp.sum(r.stat[...], axis=1, keepdims=True)
    inverse = 1.0 / summed
    lane = lax.broadcasted_iota(jnp.int32, (stack, 128), 1)
    factors = jnp.zeros((stack, 128), F32)
    for b in range(blocks):
        factors = jnp.where(lane == b, inverse * jnp.exp(tops[b] - largest), factors)
    r.weight[...] = factors

    def weight_of(b):
        picked = lax.broadcasted_iota(jnp.int32, (stack, 128), 1) == b
        return jnp.sum(jnp.where(picked, r.weight[...], 0.0), axis=1, keepdims=True)

    cross_mix = gathered_heads(r.wide_acc[...] * inverse).astype(BF)
    r.right_own[CO][...] = cross_mix
    r.lse[t] = as_row(largest + jnp.log(summed))

    arrive("co")
    sum_open(0, nn(cross_mix, w.co[...]))
    sum_cross(0)
    near_right(CO)
    near_left(FO2, r.cot[...])

    r.deep_acc[...] = jnp.zeros(r.deep_acc.shape, F32)

    def blend(b, carry):
        r.deep_acc[...] += weight_of(b) * nn(r.power[b], r.source[block_rows(b)])
        return carry

    lax.fori_loop(0, blocks, blend, 0)
    r.blended[...] = r.deep_acc[...].astype(BF)
    sum_back(0)
    q_share = share(r.qf, 0)
    lse_share = share(r.lse, 1)
    after_cross = x0 + keep * sum_close(0)

    def ffn_open(a, values, gain, win, wout, out_group, n):
        unit, scale = norm_parts(values)
        r.unit[n][...] = unit
        r.scale[n][...] = scale
        normed = (unit * gain).astype(BF)
        r.normed[n][...] = normed
        arrive(win)
        active, slope = gelu_parts(nn(normed, r.held[win][...]))
        active = active.astype(BF)
        r.slope[n][...] = slope
        if out_group == FO1 and early:
            r.early_right[hi] = active
            early_peers(lambda index, device: early_right_copy(index, device, hi).start())
        else:
            r.right_own[out_group][...] = active
            near_right(out_group)
        arrive(wout)
        sum_open(a, nn(active, r.held[wout][...]))

    ffn_open(1, after_cross, row_of(r.ffn_norm1), "fi1", "fo1", FO1, 0)

    sum_cross(1)
    key_forward = pair_forward(0, key_sends)
    near_left(FI1, r.normed[0][...])
    if early:
        line_open(line_lefts)
    key_forward.wait()
    live_row = jnp.concatenate([r.mask[b] for b in range(blocks)], axis=1)
    live_row = jnp.broadcast_to(live_row, (8, key_rows))
    live_row = pltpu.roll(live_row, lax.rem(key_rows - window, key_rows), 1)
    r.own_live[...] = live_row[:, : ceil_to(own_rows, 128)].T[:own_rows]
    wait_all(q_share)
    wait_all(lse_share)

    def own_powers(s, carry):
        key = nt(r.source[pl.ds(window, own_rows)], r.wkv[s, 0]).astype(BF)
        scores = nt(key, spread(r.qf[s]).astype(BF))
        live = jnp.broadcast_to(r.own_live[:, :1], (own_rows, stack))
        r.own_power[s] = (jnp.exp(jnp.minimum(scores - r.lse[s, 0:1], 0.0)) * live).astype(BF)
        return carry

    lax.fori_loop(0, 2, own_powers, 0)
    sum_back(1)
    value_sends = [pair_send(1)]
    after_ffn1 = after_cross + sum_close(1)

    unit_s, scale_s = norm_parts(after_ffn1)
    r.unit[1][...] = unit_s
    r.scale[1][...] = scale_s
    inner_in = (unit_s * row_of(r.self_norm)).astype(BF)
    r.normed[1][...] = inner_in
    arrive("sq", "sk", "sv", "so")
    factor = HEAD_DIM ** (-0.5)
    self_q = nt(inner_in, w.sq[...]).astype(BF).astype(F32) * factor
    self_k = nt(inner_in, w.sk[...]).astype(BF)
    self_v = nt(inner_in, w.sv[...]).astype(BF)
    self_q_wide = spread(self_q).astype(BF)
    self_scores = nt(self_k, self_q_wide)
    self_powers = jnp.exp(self_scores - jnp.max(self_scores, axis=0, keepdims=True))
    self_soft = self_powers / jnp.sum(self_powers, axis=0, keepdims=True)
    self_mix = gathered_heads(tn(self_soft.astype(BF), self_v)).astype(BF)
    r.self_q_wide[...] = self_q_wide
    r.self_k[...] = self_k
    r.self_v[...] = self_v
    r.self_soft[...] = self_soft
    sum_open(2, nn(self_mix, w.so[...]))
    r.right_own[SO][...] = self_mix
    near_right(SO)
    sum_cross(2)
    near_left(SQKV, inner_in)
    near_left_make(CQ, r.query_in[...])

    lax.fori_loop(2, 4, own_powers, 0)
    sum_back(2)
    value_sends.append(pair_send(2))
    after_self = after_ffn1 + sum_close(2)

    ffn_open(3, after_self, row_of(r.ffn_norm2), "fi2", "fo2", FO2, 2)
    cotangent = r.cot[...]

    def ffn_back(a, win, wout, in_group, n, branch):
        grad_hidden = (nt(branch, wout[...]) * r.slope[n][...]).astype(BF)
        r.right_own[in_group][...] = grad_hidden
        sum_open(a, nt(grad_hidden, win[...]))

    ffn_back(4, w.fi2, w.fo2, FI2, 2, cotangent)
    near_right(FI2)
    near_left(FI2, r.normed[2][...])
    sum_cross(4)
    if early:
        for which in range(2):
            r.blended_rows[which] = nt(r.sel[which], r.blended[...]).astype(BF)
    value_forwards = [pair_forward(1 + i, copies) for i, copies in enumerate(value_sends)]
    mid_send_half(0)
    mid_send_half(1)
    sum_back(4)
    sum_cross(3)
    dnormed = sum_close(4)
    r.vec[...] = jnp.zeros(r.vec.shape, F32)
    r.vec[3:4] = jnp.sum(dnormed * r.unit[2][...], axis=0, keepdims=True)
    grad_after_self = cotangent.astype(F32) + norm_back(
        r.unit[2][...], r.scale[2][...], row_of(r.ffn_norm2), dnormed
    )

    self_branch = grad_after_self.astype(BF)
    self_do = spread(nt(self_branch, w.so[...]).astype(BF)).astype(BF)
    self_soft = r.self_soft[...]
    grad_soft = nt(r.self_v[...], self_do)
    inner_sum = jnp.sum(self_soft * grad_soft, axis=0, keepdims=True)
    self_ds = (self_soft * (grad_soft - inner_sum)).astype(BF)
    self_dk = nn(self_ds, r.self_q_wide[...]).astype(BF)
    self_dv = nn(self_soft.astype(BF), self_do).astype(BF)
    self_dq = (gathered_heads(tn(self_ds, r.self_k[...])) * factor).astype(BF)
    sum_open(5, nn(self_dq, w.sq[...]) + nn(self_dk, w.sk[...]) + nn(self_dv, w.sv[...]))
    r.right_own[SQKV][...] = jnp.concatenate([self_dq, self_dk, self_dv], axis=1)
    near_right(SQKV)
    near_left(SO, self_branch)
    sum_cross(5)
    sum_back(3)
    wait_all(value_forwards)

    def own_values(s, carry):
        r.own_value[s] = nt(r.source[pl.ds(window, own_rows)], r.wkv[s, 1]).astype(BF)
        return carry

    lax.fori_loop(0, 4, own_values, 0)
    mid_send(Z_FI2)
    sum_back(5)
    top_send(Z_FO2)
    dnormed = sum_close(5)
    r.vec[2:3] = jnp.sum(dnormed * r.unit[1][...], axis=0, keepdims=True)
    grad_after_ffn1 = grad_after_self + norm_back(
        r.unit[1][...], r.scale[1][...], row_of(r.self_norm), dnormed
    )

    branch1 = grad_after_ffn1.astype(BF)
    ffn_back(6, w.fi1, w.fo1, FI1, 0, branch1)
    near_right(FI1)
    if early:
        line_open(lambda: [line_right()])
    early_left_open(branch1) if early else near_left(FO1, branch1)
    sum_cross(6)
    r.new_latents[...] = (after_self + sum_close(3)).astype(BF)
    leave(leaving.new_latents)
    mid_send(Z_SELF)
    near_start(CQ, 0, r.left_sent[CQ], r.left_near[CQ])
    sum_back(6)
    dnormed = sum_close(6)
    r.vec[1:2] = jnp.sum(dnormed * r.unit[0][...], axis=0, keepdims=True)
    grad_after_cross = grad_after_ffn1 + norm_back(
        r.unit[0][...], r.scale[0][...], row_of(r.ffn_norm1), dnormed
    )

    cross_branch = (keep * grad_after_cross).astype(BF)
    dmix = nt(cross_branch, w.co[...]).astype(BF)
    r.dof[t] = dmix
    do_share = share(r.dof, 2)
    do_wide_f32 = spread(dmix)
    do_wide = do_wide_f32.astype(BF)
    mix3 = jnp.concatenate([r.right_own[CO][...].astype(F32)] * heads, axis=0)
    delta = jnp.sum(do_wide_f32 * mix3, axis=1, keepdims=True)
    r.delta[t] = as_row(delta)
    delta_share = share(r.delta, 3)
    near_left(CO, cross_branch)
    if not early:
        mid_send(Z_FI1)

    def pair_open(g, left, right):
        i = g - CV
        sent = nn(left(1), right)
        r.pair_s[i] = jnp.concatenate([sent[:rows_half], sent[rows_half:]], axis=1).astype(BF)
        copy = remote(r.pair_s.at[i], r.pair_r.at[i], r.pair_ss.at[i], r.pair_rs.at[i], near)
        copy.start()
        near_copies[g].append(copy)
        r.pair_own[i] = nn(left(0), right)

    blended = r.blended[...]

    def value_rows(which):
        return r.blended_rows[which] if early else nt(r.sel[which], blended).astype(BF)

    pair_open(CV, value_rows, do_wide)
    r.deep_acc[...] = jnp.zeros(r.deep_acc.shape, F32)
    r.wide_acc[...] = jnp.zeros(r.wide_acc.shape, F32)

    def back(b, carry):
        rows = block_rows(b)
        grad_power = nt(do_wide, r.value[rows])
        ds = (r.power[b].astype(F32) * (weight_of(b) * (grad_power - delta))).astype(BF)
        r.wide_acc[...] += nn(ds, r.key[rows])
        r.deep_acc[...] += nn(ds, r.source[rows])
        return carry

    def back_and_send(b, carry):
        back(b, carry)

        @pl.when(b == 0)
        def _():
            if early:
                line_pass()

        @pl.when(b == min(1, blocks - 1))
        def _():
            top_send(Z_FI2)

        @pl.when(b == max(0, blocks - 2))
        def _():
            mid_send(Z_VALUE)

        return carry

    lax.fori_loop(0, blocks, back_and_send, 0)
    cross_dq = (gathered_heads(r.wide_acc[...]) * factor).astype(BF)
    sum_open(7, nn(cross_dq, w.cq[...]))
    q_wide = r.q_wide[...]
    deep = r.deep_acc[...]
    deep_low = deep.astype(BF)
    pair_open(CK, lambda which: nt(r.sel[which], deep_low).astype(BF), q_wide)
    r.right_own[CQ][...] = cross_dq
    near_right(CQ)
    sum_cross(7)
    top_send(Z_SELF)
    if early:
        line_send()
    gain_row = (
        jnp.sum(deep * nn(q_wide, r.wkv[t, 0]), axis=0, keepdims=True)
        + jnp.sum(blended.astype(F32) * nn(do_wide, r.wkv[t, 1]), axis=0, keepdims=True)
    ) / byte_gain
    r.gain[t] = jnp.concatenate([gain_row, jnp.zeros((7, width), F32)], axis=0)
    gain_share = share(r.gain, 4)
    wait_all(do_share)
    wait_all(delta_share)
    r.own_acc[...] = jnp.zeros(r.own_acc.shape, F32)

    def own_back(s, carry):
        do_here = spread(r.dof[s]).astype(BF)
        q_here = spread(r.qf[s]).astype(BF)
        soft = r.own_power[s]
        grad_power = nt(r.own_value[s], do_here)
        ds = (soft.astype(F32) * (grad_power - r.delta[s, 0:1])).astype(BF)
        dk = nn(ds, q_here).astype(BF)
        dv = nn(soft, do_here).astype(BF)
        r.own_acc[...] += nn(dk, r.wkv[s, 0]) + nn(dv, r.wkv[s, 1])
        return carry


    def own_back_and_send(s, carry):
        own_back(s, carry)

        @pl.when(s == 1)
        def _():
            sum_back(7)
            mid_send(Z_KEY)

        @pl.when(s == 2)
        def _():
            if not early:
                top_send(Z_FI1)
            top_send(Z_VALUE)

        return carry

    lax.fori_loop(0, 4, own_back_and_send, 0)
    if early:
        early_left_exchange()
    dnormed = sum_close(7)
    unit0, scale0 = norm_parts(r.x0[...].astype(F32))
    r.vec[0:1] = jnp.sum(dnormed * unit0, axis=0, keepdims=True)
    r.latent_grads[...] = (
        grad_after_cross + norm_back(unit0, scale0, row_of(r.cross_norm), dnormed)
    ).astype(BF)
    leave(leaving.latent_grads)
    wait_all(gain_share)
    r.vec[4:5] = r.gain[0, 0:1] + r.gain[1, 0:1] + r.gain[2, 0:1] + r.gain[3, 0:1]
    live_count = jnp.sum(jnp.sum(r.mask[...], axis=0), axis=1, keepdims=True)
    lane = lax.broadcasted_iota(jnp.int32, (1, width), 1)
    r.vec[5:6] = keep * jnp.where(lane == 0, live_count, jnp.where(lane == 1, float(lat), 0.0))
    vec_copy = remote(r.vec, r.vec_r, r.vec_ss.at[0], r.vec_rs.at[0], near)
    vec_copy.start()
    if early:
        early_send()
    else:
        mid_send(Z_FO1)
    top_send(Z_KEY)
    vec_copy.wait()
    r.vec[...] += r.vec_r[...]
    vec_copy = remote(r.vec, r.vec_m, r.vec_ss.at[1], r.vec_rs.at[1], mid)
    vec_copy.start()
    def own_norm_back(c, carry):
        rows = pl.ds(pl.multiple_of(c * OWN_CHUNK, OWN_CHUNK), OWN_CHUNK)
        unit, scale = norm_parts(r.own[rows].astype(F32))
        r.own_acc[rows] = norm_back(unit, scale, byte_gain, r.own_acc[rows])
        return carry

    own_copies[0].wait()

    @pl.when(t < 3)
    def _():
        own_copies[1].wait()

    lax.fori_loop(0, own_rows // OWN_CHUNK, own_norm_back, 0)
    vec_copy.wait()
    r.vec_all[top] = r.vec[...] + r.vec_m[...]

    def vec_top(step, source_index):
        index, device = top_peer(step)
        return remote(
            r.vec_all.at[top],
            r.vec_all.at[source_index],
            r.vh_ss.at[index],
            r.vh_rs.at[source_index],
            device,
        )

    def vec_send(step, carry):
        vec_top(step, top).start()
        return carry

    lax.fori_loop(1, n_top, vec_send, 0)
    for k in range(4):

        @pl.when(t == k)
        def _(skip=k * cfg.share % 16):
            r.byte_grads[...] = r.own_acc[skip : skip + cfg.share].astype(BF)

    leave(leaving.byte_grads)
    for z in (Z_FO2, Z_FI2, Z_SELF):
        top_close(z)
    if early:
        early_close()
        line_close()
    else:
        top_send(Z_FO1)
        top_close(Z_FI1)
        top_close(Z_FO1)
    for z in (Z_VALUE, Z_KEY):
        top_close(z)

    def vec_close(step, carry):
        vec_top(step, top_peer(step)[0]).wait()
        return carry

    lax.fori_loop(1, n_top, vec_close, 0)
    vec = lax.fori_loop(1, n_top, lambda i, total: total + r.vec_all[i], r.vec_all[0])
    mine = pltpu.roll(vec, lax.rem(width - dp * rpd, width), 1)
    for i in range(4):
        r.gain_grads[i][...] = mine[i : i + 1, :rpd].reshape(rpd)
        leave(leaving.gain_grads[i])
    r.byte_gain_grad[...] = vec[4:5].reshape(width)
    leave(leaving.byte_gain_grad)
    r.counts[...] = vec[5:6, :2].reshape(2)
    leave(leaving.counts)
    wait_all(left)


def finish(count, *refs):
    sources, targets, held = (refs[i * count : (i + 1) * count] for i in range(3))
    in_sems, out_sems = refs[3 * count :]
    arrivals = [
        pltpu.make_async_copy(src, via, in_sems.at[i])
        for i, (src, via) in enumerate(zip(sources, held))
    ]
    departures = [
        pltpu.make_async_copy(via, dst, out_sems.at[i])
        for i, (via, dst) in enumerate(zip(held, targets))
    ]
    order = sorted(range(count), key=lambda i: -math.prod(held[i].shape) * held[i].dtype.itemsize)
    for i in order:
        arrivals[i].start()
    for i in order:
        arrivals[i].wait()
        departures[i].start()
    for copy in departures:
        copy.wait()


def ceil_to(value, step):
    return -(-value // step) * step


def on_device(
    n_dp,
    latents,
    byte_array,
    caption_lengths,
    patch_mask,
    cross_keep,
    cross_norm,
    byte_norm,
    cross_query,
    cross_key,
    cross_value,
    cross_output,
    ffn_norm1,
    ffn_in1,
    ffn_out1,
    self_norm,
    self_query,
    self_key,
    self_value,
    self_output,
    ffn_norm2,
    ffn_in2,
    ffn_out2,
    cotangent,
):
    _, lat, width = latents.shape
    keys = byte_array.shape[1]
    patches = patch_mask.shape[1]
    hw = cross_query.shape[1]
    ff = ffn_in1.shape[1]
    heads = hw // HEAD_DIM
    share = keys // 4
    key_rows = ceil_to(keys, KEY_BLOCK)
    main_rows = keys // TAIL * TAIL
    own_rows = ceil_to(share + 15, OWN_CHUNK)
    blocks = key_rows // KEY_BLOCK
    n_hi = n_dp // 2
    n_top = n_hi // 2
    rpd = width // n_dp
    pr = ceil_to(rpd, 16)
    rt = n_hi * pr
    byte_parts = [
        (start, min(KEY_BLOCK, main_rows - start)) for start in range(0, main_rows, KEY_BLOCK)
    ]
    assert main_rows + TAIL == key_rows and len(byte_parts) == blocks
    assert 3 * share // 16 * 16 + own_rows == key_rows

    hbm = pl.BlockSpec(memory_space=pl.ANY)
    smem = pl.BlockSpec(memory_space=pltpu.SMEM)
    values = dict(
        keep=cross_keep,
        captions=caption_lengths,
        bytes=byte_array[0],
        tail=byte_array[0],
        quick=dict(
            x0=latents[0],
            cross_norm=cross_norm,
            patch_mask=patch_mask,
            byte_norm=byte_norm,
            ffn_norm1=ffn_norm1,
            self_norm=self_norm,
            ffn_norm2=ffn_norm2,
            cot=cotangent[0],
        ),
        cross_key=cross_key.T,
        cross_value=cross_value.T,
        weights=dict(
            cq=cross_query.T,
            co=cross_output,
            fi1=ffn_in1,
            fo1=ffn_out1,
            sq=self_query.T,
            sk=self_key.T,
            sv=self_value.T,
            so=self_output,
            fi2=ffn_in2,
            fo2=ffn_out2,
        ),
    )
    specs = {}
    specs.update(
        keep=smem,
        captions=smem,
        bytes=hbm,
        tail=pl.BlockSpec(
            (TAIL, width), lambda i: (main_rows // TAIL, 0), pipeline_mode=pl.Buffered(1)
        ),
        cross_key=hbm,
        cross_value=hbm,
        quick={name: hbm for name in values["quick"]},
        weights={name: hbm for name in values["weights"]},
    )
    widths = (ff, ff, 3 * hw, hw, ff, ff, hw, hw, hw, hw)
    early = n_hi == 4
    bundles = [
        128 if early and bundle in ((FI1,), (FO1,)) else sum(widths[g] for g in bundle)
        for bundle in BUNDLES
    ]

    def out(shape, kind):
        return jax.ShapeDtypeStruct(shape, kind)

    outputs = dict(
        new_latents=out((lat, width), BF),
        latent_grads=out((lat, width), BF),
        byte_grads=out((share, width), BF),
        gain_grads=[out((rpd,), F32) for _ in range(4)],
        byte_gain_grad=out((width,), F32),
        counts=out((2,), F32),
        self_grads=[out((rpd, hw), F32) for _ in range(3)],
        grads={
            FO2: out((rpd, ff), F32),
            FI2: out((rpd, ff), F32),
            SO: out((hw, rpd), F32),
            FO1: out((rpd, ff), F32),
            FI1: out((rpd, ff), F32),
            CO: out((hw, rpd), F32),
            CQ: out((rpd, hw), F32),
            CV: out((rpd, hw), F32),
            CK: out((rpd, hw), F32),
        },
    )

    def buf(*shape):
        return pltpu.VMEM(shape, BF)

    def wide(*shape):
        return pltpu.VMEM(shape, F32)

    def sems(*shape):
        return pltpu.SemaphoreType.DMA(shape)

    stack = heads * lat
    left_rows = [16 if early and g == FO1 else rt for g in range(CV)]
    right_columns = [128 if early and g == FO1 else widths[g] for g in range(CV)]
    scratch = dict(
        placed={name: pltpu.VMEM(a.shape, a.dtype) for name, a in values["quick"].items()},
        quick_sem=sems(len(values["quick"])),
        made=jax.tree.map(lambda a: pltpu.VMEM(a.shape, a.dtype), outputs),
        out_sem=sems(len(jax.tree.leaves(outputs))),
        held={name: buf(*value.shape) for name, value in values["weights"].items()},
        wkv=buf(4, 2, hw, width),
        source=buf(key_rows, width),
        key=buf(key_rows, hw),
        value=buf(key_rows, hw),
        power=buf(blocks, stack, KEY_BLOCK),
        stat=wide(stack, 128),
        mask=wide(blocks, 1, KEY_BLOCK),
        weight=wide(stack, 128),
        wide_acc=wide(stack, hw),
        deep_acc=wide(stack, width),
        blended=buf(stack, width),
        blended_rows=buf(*((2, rt, stack) if early else (16, 128))),
        q_wide=buf(stack, hw),
        query_in=buf(lat, width),
        qf=buf(4, lat, hw),
        dof=buf(4, lat, hw),
        lse=wide(4, 8, stack),
        delta=wide(4, 8, stack),
        gain=wide(4, 8, width),
        own=buf(own_rows, width),
        own_value=buf(4, own_rows, hw),
        own_power=buf(4, own_rows, stack),
        own_live=wide(own_rows, 8),
        own_acc=wide(own_rows, width),
        unit=[wide(lat, width) for _ in range(3)],
        scale=[wide(lat, 1) for _ in range(3)],
        normed=[buf(lat, width) for _ in range(3)],
        slope=[wide(lat, ff), wide(8, 128), wide(lat, ff)],
        self_q_wide=buf(stack, hw),
        self_k=buf(lat, hw),
        self_v=buf(lat, hw),
        self_soft=wide(lat, stack),
        sel=buf(2, rt, width),
        ar_s=buf(SETS, 2, lat // 2, width),
        ar_r1=buf(SETS, lat // 2, width),
        ar_r2=buf(SETS, lat // 2, width),
        ar_t=buf(SETS, 2, lat // 2, width),
        pair_own=wide(2, rt, hw),
        pair_s=buf(2, rt // 2, 2 * hw),
        pair_r=buf(2, rt // 2, 2 * hw),
        vec=wide(8, width),
        vec_r=wide(8, width),
        vec_m=wide(8, width),
        vec_all=wide(n_top, 8, width),
        left_own=[buf(rows, lat) for rows in left_rows],
        left_sent=[buf(rows, lat) for rows in left_rows],
        left_near=[buf(rows, lat) for rows in left_rows],
        right_own=[buf(lat, size) for size in right_columns],
        right_near=[buf(lat, size) for size in right_columns],
        mid_sent=[buf(rt // 2, size) for size in bundles],
        mid_got=[buf(rt // 2, size) for size in bundles],
        block_sent=[buf(n_top, pr, size) for size in bundles],
        block_got=[buf(n_top, pr, size) for size in bundles],
        byte_sem=sems(len(byte_parts)),
        own_sem=sems(2),
        w_sem=sems(len(values["weights"])),
        pair_sem=sems(2),
        share_ss=sems(5, 3),
        share_rs=sems(5, 3),
        wkv_ss=sems(3, 3),
        wkv_rs=sems(3, 3),
        ar_ss=sems(8, 3),
        ar_rs=sems(8, 3),
        x_ss=sems(CV, 3),
        x_rs=sems(CV, 3),
        mh_ss=sems(2),
        mh_rs=sems(2),
        m_ss=sems(len(BUNDLES)),
        m_rs=sems(len(BUNDLES)),
        z_ss=sems(len(BUNDLES), n_top),
        z_rs=sems(len(BUNDLES), n_top),
        early_right=buf(*((n_hi, lat, ff) if early else (16, 128))),
        early_sent=buf(*((n_hi, 2, pr, lat) if early else (16, 128))),
        early_left=buf(*((n_hi, 2, pr, lat) if early else (16, 128))),
        early_part=buf(pr, ff),
        early_got=buf(pr, ff),
        er_ss=sems(n_hi),
        er_rs=sems(n_hi),
        el_ss=sems(n_hi),
        el_rs=sems(n_hi),
        line_in=[buf(2, *shape) for shape in ((rt, lat), (lat, ff))] if early else [],
        line_sum=wide(*((rt, ff) if early else (16, 128))),
        line_sent=buf(*((3, pr, ff) if early else (16, 128))),
        line_got=buf(*((2, pr, ff) if early else (16, 128))),
        li_ss=sems(2, 2),
        li_rs=sems(2, 2),
        lo_ss=sems(3),
        lo_rs=sems(2),
        ef_ss=sems(n_hi),
        ef_rs=sems(n_hi),
        ep_ss=sems(1),
        ep_rs=sems(1),
        pair_ss=sems(2),
        pair_rs=sems(2),
        vec_ss=sems(2),
        vec_rs=sems(2),
        vh_ss=sems(n_top),
        vh_rs=sems(n_top),
    )
    tables = (values, dict(outs=outputs), scratch)

    def leaf(node):
        return not isinstance(node, (dict, list))

    flat = [jax.tree.flatten(table, is_leaf=leaf) for table in tables]
    trees = [tree for _, tree in flat]
    counts = [len(leaves) for leaves, _ in flat]
    cfg = SimpleNamespace(
        trees=trees,
        counts=counts,
        lat=lat,
        width=width,
        hw=hw,
        heads=heads,
        n_hi=n_hi,
        pr=pr,
        rpd=rpd,
        blocks=blocks,
        key_rows=key_rows,
        main_rows=main_rows,
        own_rows=own_rows,
        byte_parts=byte_parts,
        patches=patches,
        keys=keys,
        share=share,
        widths=widths,
        early=early,
        out_order=jax.tree.unflatten(jax.tree.structure(outputs), range(counts[1])),
    )
    results = pl.pallas_call(
        functools.partial(kernel, cfg),
        out_shape=flat[1][0],
        grid=(1,),
        in_specs=jax.tree.leaves(specs, is_leaf=leaf),
        out_specs=[hbm] * counts[1],
        scratch_shapes=flat[2][0],
        compiler_params=pltpu.CompilerParams(
            collective_id=0, has_side_effects=True, vmem_limit_bytes=64 * 2**20
        ),
        name="layers",
    )(*flat[0][0])
    results = pl.pallas_call(
        functools.partial(finish, counts[1]),
        out_shape=flat[1][0],
        in_specs=[hbm] * counts[1],
        out_specs=[hbm] * counts[1],
        scratch_shapes=[pltpu.VMEM(array.shape, array.dtype) for array in flat[1][0]]
        + [sems(counts[1])] * 2,
        name="results",
    )(*results)
    out = SimpleNamespace(**jax.tree.unflatten(trees[1], results)["outs"])
    grads = out.grads
    return (
        out.new_latents[None],
        out.latent_grads[None],
        out.byte_grads[None],
        out.gain_grads[0],
        out.byte_gain_grad,
        grads[CQ],
        grads[CK],
        grads[CV],
        grads[CO],
        out.gain_grads[1],
        grads[FI1],
        grads[FO1].T,
        out.gain_grads[2],
        out.self_grads[0],
        out.self_grads[1],
        out.self_grads[2],
        grads[SO],
        out.gain_grads[3],
        grads[FI2],
        grads[FO2].T,
        out.counts,
    )


def solution(mesh):
    in_specs = (
        P("dp", None, None),
        P("dp", None, None),
        P("dp"),
        P("dp", None),
        P("dp"),
        P(),
        P(),
        P(None, "tensor"),
        P(None, "tensor"),
        P(None, "tensor"),
        P("tensor", None),
        P(),
        P(None, "tensor"),
        P("tensor", None),
        P(),
        P(None, "tensor"),
        P(None, "tensor"),
        P(None, "tensor"),
        P("tensor", None),
        P(),
        P(None, "tensor"),
        P("tensor", None),
        P("dp", None, None),
    )
    out_specs = (
        P("dp", None, None),
        P("dp", None, None),
        P("dp", "tensor", None),
        P("dp"),
        P(),
        P("dp", "tensor"),
        P("dp", "tensor"),
        P("dp", "tensor"),
        P("tensor", "dp"),
        P("dp"),
        P("dp", "tensor"),
        P("tensor", "dp"),
        P("dp"),
        P("dp", "tensor"),
        P("dp", "tensor"),
        P("dp", "tensor"),
        P("tensor", "dp"),
        P("dp"),
        P("dp", "tensor"),
        P("tensor", "dp"),
        P(),
    )
    return jax.shard_map(
        functools.partial(on_device, mesh.shape["dp"]),
        mesh=mesh,
        in_specs=in_specs,
        out_specs=out_specs,
        check_vma=False,
    )
```
